128 devices in a mesh: seq: 8 (over z, x_hi), shard: 16 (over y, x_lo, core).
Axes of the slice: x: 4 (x_hi: 2, x_lo: 2; x = x_hi * 2 + x_lo), y: 4, z: 4, core: 2. Of those that a mesh axis runs over, the one named last changes fastest.
Arguments:
- layer_input: bfloat16 [16384, 1024], P(('seq', 'shard')), may hold values from -6 to 6
- attn_gain: bfloat16 [1024], P(('seq', 'shard')), may hold values from 0.5 to 1.5
- moe_gain: bfloat16 [1024], P(('seq', 'shard')), may hold values from 0.5 to 1.5
- w_qkv: bfloat16 [1024, 2048], P(('seq', 'shard')), may hold values from -0.1875 to 0.1875
- w_out: bfloat16 [1024, 1024], P(('seq', 'shard')), may hold values from -4 to 4
- w_gate: bfloat16 [32, 1024, 512], P('shard', 'seq'), may hold values from -0.1875 to 0.1875
- w_up: bfloat16 [32, 1024, 512], P('shard', 'seq'), may hold values from -0.1875 to 0.1875
- w_down: bfloat16 [32, 512, 1024], P('shard', 'seq'), may hold values from -0.5 to 0.5
- routes: int32 [16384, 8], P(('seq', 'shard')), may hold values from 0 to 31, all different within a row; in each aligned block of 128 rows (0 to 127, 128 to 255, ...) at most 40 rows name the same one
- route_weights: float32 [16384, 8], P(('seq', 'shard')), may hold values from 0.05 to 0.4
- cotangent: bfloat16 [16384, 1024], P(('seq', 'shard')), may hold values from -6 to 6
Outputs:
- block_out: bfloat16 [16384, 1024], P(('seq', 'shard'))
- input_grad: bfloat16 [16384, 1024], P(('seq', 'shard'))
- attn_gain_grad: float32 [1024], P(('seq', 'shard'))
- moe_gain_grad: float32 [1024], P(('seq', 'shard'))
- w_qkv_grad: float32 [1024, 2048], P(('seq', 'shard'))
- w_out_grad: float32 [1024, 1024], P(('seq', 'shard'))
- w_gate_grad: float32 [32, 1024, 512], P('shard', 'seq')
- w_up_grad: float32 [32, 1024, 512], P('shard', 'seq')
- w_down_grad: float32 [32, 512, 1024], P('shard', 'seq')
The draws below stay inside these ranges and needn't reach their ends.
Inputs may be any that keep to these rules, and one draw needn't show every extreme that they name: `routes`: each row names 8 different experts. In the rows of one device no expert is named more than 40 times, and in every draw some expert is named exactly 40 times in some device's rows.
All inputs are finite; a program needn't handle non-finite values.
Results may differ from the reference program's by a relative error of at most 0.029.
Values may be sent and summed in bfloat16 or wider, within the bound.
A program may use at most 128 MiB of HBM per device.

```python
import math
import jax
import jax.numpy as jnp
import numpy as np
from jax import lax

D = 1024
HEADS = 16
KV = 8
HEAD = 64
EXPERTS = 32
FF = 512
TOPK = 8
TOK_DEV = 128
CAP = 40
TOKENS = 16384
N_SEQ = 8
N_SHARD = 16


def block_scale(stream_key, extent, shards, low, largest):
    def one(dim, blocks):
        steps = jax.random.uniform(jax.random.fold_in(jax.random.fold_in(stream_key, 6), dim), (blocks,), jnp.float32, low / len(shards), largest / len(shards))
        return jnp.repeat(jnp.exp(steps), extent[dim] // blocks).reshape((-1,) + (1,) * (len(extent) - dim - 1))

    gain = one(*shards[0])
    for cut in shards[1:]:
        gain = gain * one(*cut)
    return gain


def shared_out(own_key, own, number, rows, number_of, top, reach, lean):
    sequence = jax.random.permutation(own_key, number_of)
    heavy_load, ordinary = shares(number_of, rows * top, reach, lean, True), shares(number_of, rows * top, reach, lean, False)
    places = jnp.arange(number_of)

    def named(sizes, turn):
        used = int((sizes > 0).sum())
        fixed = max(1, used // 4)
        moved = fixed + (places - fixed + turn * (used - fixed)) % max(1, number_of - fixed)
        return jnp.zeros((number_of,), jnp.int32).at[sequence[jnp.where(places < fixed, places, moved)]].set(jnp.asarray(sizes, jnp.int32))

    sizes = jnp.where(number % 4 == 0, named(heavy_load, number // 4), named(ordinary, number - number // 4 - 1))
    mixed = jax.random.permutation(jax.random.fold_in(own, 3), number_of)
    source_of, taker = mixed[0:number_of // 2 * 2:2], mixed[1:number_of // 2 * 2:2]
    room = jnp.minimum(sizes[source_of] - 1, reach - sizes[taker]) // 2
    room = jnp.where((source_of == sequence[0]) | (taker == sequence[0]) | (sizes[taker] == 0), 0, jnp.maximum(room, 0))
    moved = jax.random.randint(jax.random.fold_in(own, 4), (number_of // 2,), 0, 1 << 20) % (room + 1)
    sizes = sizes.at[source_of].add(-moved).at[taker].add(moved)
    labels = jnp.searchsorted(jnp.cumsum(sizes), jnp.arange(rows * top), side="right").astype(jnp.int32)
    listing = labels.reshape(top, rows).T
    listing = listing[jax.random.permutation(jax.random.fold_in(own, 1), rows)]
    turn = jax.random.randint(jax.random.fold_in(own, 2), (rows, 1), 0, top)
    return jnp.take_along_axis(listing, (jnp.arange(top)[None, :] + turn) % top, axis=1)


def shares(number_of, total, limit, skew, full):
    loads = [(1 << 20) // math.isqrt(grade ** skew) + 1 for grade in range(1, number_of + 1)]
    largest = limit if full else min(limit, max(-(-total // number_of), total * loads[0] // sum(loads)))
    least = 1 if total - largest >= number_of - 1 else 0
    holding, rest = [largest] + [least] * (number_of - 1), total - largest - least * (number_of - 1)
    while rest > 0:
        movable = [i for i in range(1, number_of) if holding[i] < largest] or [i for i in range(1, number_of) if holding[i] < limit]
        mass, left = sum([loads[i] for i in movable]), rest
        for i in movable:
            addition = min(limit - holding[i], max(1, left * loads[i] // mass), rest)
            holding[i] = holding[i] + addition
            rest = rest - addition
    return np.array(holding)


def normal_values(own_key, shape, scale, most, split=(), kind=jnp.bfloat16):
    array = jax.random.normal(own_key, shape, jnp.float32) * scale
    if len(split) > 0:
        array = block_scale(own_key, shape, split, -0.22, 0.18) * array
    return jnp.clip(array, min=-most, max=most).astype(kind)


def setup_inputs(seed: int = 0) -> dict:
    splits = jax.random.split(jax.random.key(seed), 12)
    layer_input = normal_values(splits[0], (TOKENS, D), 1.0, 6.0, ((0, 128),))
    attn_gain = jnp.clip(1.0 + 0.1 * jax.random.normal(splits[1], (D,), jnp.float32), 0.5, 1.5).astype(jnp.bfloat16)
    moe_gain = jnp.clip(1.0 + 0.1 * jax.random.normal(splits[2], (D,), jnp.float32), 0.5, 1.5).astype(jnp.bfloat16)
    w_qkv = normal_values(splits[3], (D, (HEADS + 2 * KV) * HEAD), D ** -0.5, 0.1875, ((0, 128),))
    w_out = normal_values(splits[4], (HEADS * HEAD, D), 0.5, 4.0, ((0, 128),))
    w_gate = normal_values(splits[5], (EXPERTS, D, FF), D ** -0.5, 0.1875, ((0, 16), (1, 8)))
    w_up = normal_values(splits[6], (EXPERTS, D, FF), D ** -0.5, 0.1875, ((0, 16), (1, 8)))
    w_down = normal_values(splits[7], (EXPERTS, FF, D), (FF // 4) ** -0.5, 0.5, ((0, 16), (1, 8)))
    routes_keys = jax.random.split(jax.random.fold_in(splits[8], 1), TOKENS // TOK_DEV)
    routes_turns = jax.random.permutation(jax.random.fold_in(splits[8], 3), TOKENS // TOK_DEV)
    routes = jax.vmap(lambda own, number: shared_out(jax.random.fold_in(splits[8], 2), own, number, TOK_DEV, EXPERTS, TOPK, CAP, 1))(routes_keys, routes_turns).reshape((TOKENS, TOPK))
    route_weights = jnp.clip(jnp.exp(math.log(0.4) - 2.0794415 * jax.random.uniform(splits[9], (TOKENS, TOPK), jnp.float32) ** block_scale(splits[9], (TOKENS, TOPK), ((0, 128),), -0.2, 0.2)), 0.05, 0.4)
    cotangent = normal_values(splits[10], (TOKENS, D), 1.0, 6.0, ((0, 128),))
    return {"layer_input": layer_input, "attn_gain": attn_gain, "moe_gain": moe_gain, "w_qkv": w_qkv, "w_out": w_out, "w_gate": w_gate, "w_up": w_up, "w_down": w_down, "routes": routes, "route_weights": route_weights, "cotangent": cotangent}


@jax.custom_vjp
def low(v):
    return lax.optimization_barrier(v.astype(jnp.bfloat16)).astype(jnp.float32)

@jax.custom_vjp
def low_back(v):
    return v

def low_keep(v):
    return (low(v), None)

def low_pass(kept, grad):
    return (grad,)

def back_keep(v):
    return (v, None)

def back_low(kept, grad):
    return (low(grad),)
low.defvjp(low_keep, low_pass)
low_back.defvjp(back_keep, back_low)
epsilon = 1e-06
rope_base = 10000.0
highest = lax.Precision.HIGHEST

def rms_scale(values, gain_vector):
    inverse = lax.rsqrt(lax.optimization_barrier(jnp.mean(values * values, axis=-1, keepdims=True)) + epsilon)
    return values * inverse * gain_vector

def rope_tables(start_pos, position_count):
    half_width = HEAD // 2
    frequency = jnp.exp(jnp.arange(half_width, dtype=jnp.float32) * jnp.float32(-2.0 * math.log(rope_base) / HEAD))
    position = (start_pos + jnp.arange(position_count, dtype=jnp.int32)).astype(jnp.float32)
    angles = position[:, None] * frequency[None, :]
    return (jnp.cos(angles)[:, None, :], jnp.sin(angles)[:, None, :])

def rotate(values, cosine_table, sine_table):
    half_width = values.shape[-1] // 2
    first_half = values[..., :half_width]
    second_half = values[..., half_width:]
    return jnp.concatenate([first_half * cosine_table - second_half * sine_table, second_half * cosine_table + first_half * sine_table], axis=-1)

def attend(queries, key_heads, values):
    group_size = HEADS // KV
    block_rows = min(512, TOKENS)
    block_count = TOKENS // block_rows
    key_pos = jnp.arange(TOKENS, dtype=jnp.int32)
    score_scale = 1.0 / math.sqrt(HEAD)

    def one_block(item_index):
        head_index = item_index // block_count
        query_start = item_index % block_count * block_rows
        query_tile = lax.dynamic_slice_in_dim(lax.dynamic_index_in_dim(queries, head_index, 0, keepdims=False), query_start, block_rows, 1)
        key_head = lax.dynamic_index_in_dim(key_heads, head_index, 0, keepdims=False)
        value_head = lax.dynamic_index_in_dim(values, head_index, 0, keepdims=False)
        scores = low_back(jnp.einsum('gqd,kd->gqk', query_tile, key_head, precision=highest) * score_scale)
        query_pos = query_start + jnp.arange(block_rows, dtype=jnp.int32)
        scores = jnp.where(query_pos[:, None] >= key_pos[None, :], scores, -1e+30)
        row_peak = lax.optimization_barrier(jnp.max(scores, axis=-1, keepdims=True))
        exponent = jnp.exp(scores - row_peak)
        softmax_weights = exponent / lax.optimization_barrier(jnp.sum(exponent, axis=-1, keepdims=True))
        return jnp.einsum('gqk,kd->gqd', low(softmax_weights), value_head, precision=highest)
    blocks = lax.map(jax.checkpoint(one_block), jnp.arange(KV * block_count, dtype=jnp.int32))
    blocks = blocks.reshape(KV, block_count, group_size, block_rows, HEAD)
    return blocks.transpose(1, 3, 0, 2, 4).reshape(TOKENS, HEADS * HEAD)

def dispatch_tables(routes, route_weights):
    devices = N_SEQ * N_SHARD
    flat_routes = routes.reshape(devices, TOK_DEV * TOPK)
    onehot = (flat_routes[:, :, None] == jnp.arange(EXPERTS, dtype=jnp.int32)[None, None, :]).astype(jnp.int32)
    slot_index = lax.optimization_barrier(jnp.sum((jnp.cumsum(onehot, axis=1) - 1) * onehot, axis=2))
    owner_device = jnp.broadcast_to(jnp.arange(devices, dtype=jnp.int32)[:, None], flat_routes.shape)
    token_index = owner_device * TOK_DEV + jnp.arange(TOK_DEV * TOPK, dtype=jnp.int32)[None, :] // TOPK
    slot_rows = jnp.zeros((EXPERTS, devices, CAP), jnp.int32).at[flat_routes, owner_device, slot_index].set(token_index)
    slot_gate = jnp.zeros((EXPERTS, devices, CAP), jnp.float32).at[flat_routes, owner_device, slot_index].set(route_weights.reshape(devices, TOK_DEV * TOPK))
    return (slot_rows.reshape(EXPERTS, devices * CAP), slot_gate.reshape(EXPERTS, devices * CAP))

def mixture(normed_moe, slot_rows, slot_gate, w_gate, w_up, w_down):

    def one_expert(inputs):
        row_index, gate_scale, gate_matrix, up_matrix, down_matrix = inputs
        picked = low_back(normed_moe[row_index])
        gate_pre = low_back(jnp.dot(picked, gate_matrix, precision=highest))
        up_pre = low_back(jnp.dot(picked, up_matrix, precision=highest))
        hidden_units = low(jax.nn.silu(gate_pre) * up_pre)
        result = low(low_back(jnp.dot(hidden_units, down_matrix, precision=highest)))
        return result * gate_scale[:, None]
    results = lax.map(jax.checkpoint(one_expert), (slot_rows, slot_gate, w_gate, w_up, w_down))
    return jnp.zeros_like(normed_moe).at[slot_rows.reshape(-1)].add(results.reshape(-1, normed_moe.shape[1]))

def reference(layer_input, attn_gain, moe_gain, w_qkv, w_out, w_gate, w_up, w_down, routes, route_weights, cotangent):
    slot_rows, slot_gate = dispatch_tables(routes, route_weights.astype(jnp.float32))
    cosine_table, sine_table = rope_tables(0, TOKENS)
    group_size = HEADS // KV
    width_q = HEADS * HEAD
    width_kv = KV * HEAD

    def forward(input_wide, attn_gain, moe_gain, w_qkv, w_out, w_gate, w_up, w_down):
        normed = low(rms_scale(input_wide, attn_gain))
        projected = low_back(jnp.dot(normed, w_qkv, precision=highest))
        queries = rotate(projected[:, :width_q].reshape(TOKENS, HEADS, HEAD), cosine_table, sine_table)
        key_heads = rotate(projected[:, width_q:width_q + width_kv].reshape(TOKENS, KV, HEAD), cosine_table, sine_table)
        values = projected[:, width_q + width_kv:].reshape(TOKENS, KV, HEAD)
        queries = low(low_back(queries)).reshape(TOKENS, KV, group_size, HEAD).transpose(1, 2, 0, 3)
        key_heads = low(low_back(key_heads)).transpose(1, 0, 2)
        values = low(low_back(values)).transpose(1, 0, 2)
        attended = low(low_back(attend(queries, key_heads, values)))
        residual = input_wide + low_back(jnp.dot(attended, w_out, precision=highest))
        normed_moe = low(rms_scale(residual, moe_gain))
        return residual + mixture(normed_moe, slot_rows, slot_gate, w_gate, w_up, w_down)
    result, pullback = jax.vjp(forward, layer_input.astype(jnp.float32), attn_gain.astype(jnp.float32), moe_gain.astype(jnp.float32), w_qkv.astype(jnp.float32), w_out.astype(jnp.float32), w_gate.astype(jnp.float32), w_up.astype(jnp.float32), w_down.astype(jnp.float32))
    gradients = pullback(cotangent.astype(jnp.float32))
    return (result.astype(jnp.bfloat16), gradients[0].astype(jnp.bfloat16), gradients[1], gradients[2], gradients[3], gradients[4], gradients[5], gradients[6], gradients[7])
```

```python
import functools
import math

import jax
import jax.numpy as jnp
from jax import lax
from jax.experimental import pallas as pl
from jax.experimental.pallas import tpu as pltpu
from jax.sharding import PartitionSpec as P

HEADS = 16
KV = 8
HEAD = 64
EXPERTS = 32
TOPK = 8
TOK_DEV = 128
CAP = 40
WIDTH = 1024
FF = 512
N_SEQ = 8
N_SHARD = 16
HEAD_ROWS = TOK_DEV * N_SEQ
TOKENS = TOK_DEV * N_SEQ * N_SHARD
LOCAL_EXPERTS = EXPERTS // N_SHARD
EXPERT_ROWS = N_SHARD * CAP
COLS = 256
FWD_TILE = 2048
BWD_TILE = 1024

epsilon = 1e-06
rope_base = 10000.0

f32 = jnp.float32
bf16 = jnp.bfloat16
MESH = pl.DeviceIdType.MESH
ANY = pl.BlockSpec(memory_space=pl.ANY)
NT = (((1,), (1,)), ((), ()))
NN = (((1,), (0,)), ((), ()))
TN = (((0,), (0,)), ((), ()))


def dot(left, right, dims):
    return lax.dot_general(left, right, dims, preferred_element_type=f32)


def greet(peers):
    barrier = pltpu.get_barrier_semaphore()
    for axis, peer in peers:
        pl.semaphore_signal(barrier, inc=1, device_id={axis: peer}, device_id_type=MESH)
    pl.semaphore_wait(barrier, len(peers))


def remote(source, target, send, recv, axis, peer):
    copy = pltpu.make_async_remote_copy(
        src_ref=source,
        dst_ref=target,
        send_sem=send,
        recv_sem=recv,
        device_id={axis: peer},
        device_id_type=MESH,
    )
    copy.start()
    return copy


def exchange_kernel(axis, count, dim, x_ref, o_ref, send, recv, own):
    def block(ref, index):
        return ref.at[:, index] if dim == 1 else ref.at[index]

    me = lax.axis_index(axis)
    greet([(axis, lax.rem(me + k, count)) for k in range(1, count)])
    mine = pltpu.make_async_copy(block(x_ref, me), block(o_ref, me), own)
    mine.start()
    copies = []
    for k in range(1, count):
        peer = lax.rem(me + k, count)
        copies.append(
            remote(block(x_ref, peer), block(o_ref, me), send.at[k - 1], recv.at[k - 1], axis, peer)
        )
    mine.wait()
    for copy in copies:
        copy.wait()


def exchange(x, axis, count, ident, dim=0):
    return pl.pallas_call(
        functools.partial(exchange_kernel, axis, count, dim),
        out_shape=jax.ShapeDtypeStruct(x.shape, x.dtype),
        in_specs=[ANY],
        out_specs=ANY,
        scratch_shapes=[
            pltpu.SemaphoreType.DMA((count - 1,)),
            pltpu.SemaphoreType.DMA((count - 1,)),
            pltpu.SemaphoreType.DMA,
        ],
        compiler_params=pltpu.CompilerParams(collective_id=ident, has_side_effects=True),
        name="exchange_" + axis,
    )(x)


def staged(axis, share, x_ref, place, sem_send, sem_recv, own):
    me = lax.axis_index(axis)
    cores = 2 if axis == "shard" else 1
    core = lax.rem(me, cores)
    pair = lax.rem(me // cores, 2)
    ring = me // (2 * cores)

    def at(r, p, c):
        return (r * 2 + p) * cores + c

    ring_peer = [at(lax.rem(ring + k, 4), pair, core) for k in (1, 2, 3)]
    ring_from = [lax.rem(ring + 4 - k, 4) for k in (1, 2, 3)]
    pair_peer = at(ring, 1 - pair, core)
    core_peer = at(ring, pair, 1 - core)
    mine = pltpu.make_async_copy(x_ref, place(me, 0, 8), own)
    mine.start()
    sends = []

    def go(source, index, low, high, peer):
        n = len(sends)
        sends.append(
            remote(source, place(index, low, high), sem_send.at[n], sem_recv.at[n], axis, peer)
        )
        return sends[-1]

    to_pair = go(x_ref, me, 0, 8, pair_peer)
    to_ring = [go(x_ref, me, 0, 8, peer) for peer in ring_peer]
    landed = []
    if cores == 2:
        landed.append(go(x_ref, me, 0, 8, core_peer))

    def pass_core(index, low, high):
        if cores == 2:
            landed.append(go(place(index, low, high), index, low, high, core_peer))

    to_pair.wait_recv()
    fwd_ring = [
        go(place(pair_peer, 0, share), pair_peer, 0, share, peer) for peer in ring_peer
    ]
    pass_core(pair_peer, 0, 8)
    fwd_pair = []
    for k in (0, 2, 1):
        to_ring[k].wait_recv()
        source = at(ring_from[k], pair, core)
        fwd_pair.append((k, go(place(source, share, 8), source, share, 8, pair_peer)))
        pass_core(source, 0, 8)
    for k in (0, 2, 1):
        fwd_ring[k].wait_recv()
        pass_core(at(ring_from[k], 1 - pair, core), 0, share)
    for k, copy in fwd_pair:
        copy.wait_recv()
        pass_core(at(ring_from[k], 1 - pair, core), share, 8)
    for copy in landed:
        copy.wait_recv()
    mine.wait()
    for copy in sends:
        copy.wait_send()


def staged_peers(axis):
    me = lax.axis_index(axis)
    cores = 2 if axis == "shard" else 1
    core = lax.rem(me, cores)
    pair = lax.rem(me // cores, 2)
    ring = me // (2 * cores)
    peers = [(lax.rem(ring + k, 4) * 2 + pair) * cores + core for k in (1, 2, 3)]
    peers.append((ring * 2 + 1 - pair) * cores + core)
    if cores == 2:
        peers.append((ring * 2 + pair) * cores + 1 - core)
    return [(axis, peer) for peer in peers]


def gather_memory_kernel(x_ref, o_ref, send, recv, own):
    greet(staged_peers("shard"))
    staged("shard", 4, x_ref, lambda j, low, high: o_ref.at[low:high, j], send, recv, own)


def gather_memory(x, ident):
    return pl.pallas_call(
        gather_memory_kernel,
        out_shape=jax.ShapeDtypeStruct((N_SEQ, N_SHARD, TOK_DEV, 2 * HEAD), x.dtype),
        in_specs=[ANY],
        out_specs=ANY,
        scratch_shapes=[
            pltpu.SemaphoreType.DMA((24,)),
            pltpu.SemaphoreType.DMA((24,)),
            pltpu.SemaphoreType.DMA,
        ],
        compiler_params=pltpu.CompilerParams(collective_id=ident, has_side_effects=True),
        name="gather_memory",
    )(x)


def first_kernel(x_ref, w_ref, xo_ref, wo_ref, w_mid, send, recv, own, wsend, wrecv, wown):
    seq = lax.axis_index("seq")
    shard = lax.axis_index("shard")
    greet(
        [("seq", lax.rem(seq + k, N_SEQ)) for k in range(1, N_SEQ)]
        + [("shard", lax.rem(shard + k, N_SHARD)) for k in range(1, N_SHARD)]
    )
    mine = pltpu.make_async_copy(w_ref.at[seq], w_mid.at[seq], wown)
    mine.start()
    pieces = []
    for k in range(1, N_SEQ):
        peer = lax.rem(seq + k, N_SEQ)
        pieces.append(
            remote(w_ref.at[peer], w_mid.at[seq], wsend.at[k - 1], wrecv.at[k - 1], "seq", peer)
        )
    mine.wait()
    for piece in pieces:
        piece.wait()
    mine = pltpu.make_async_copy(w_mid, wo_ref.at[shard], wown)
    mine.start()
    pieces = []
    for k in range(1, N_SHARD):
        peer = lax.rem(shard + k, N_SHARD)
        n = N_SEQ - 2 + k
        pieces.append(
            remote(w_mid, wo_ref.at[shard], wsend.at[n], wrecv.at[n], "shard", peer)
        )
    staged("seq", 4, x_ref, lambda s, low, high: xo_ref.at[s, low:high], send, recv, own)
    mine.wait()
    for piece in pieces:
        piece.wait()


def first_gather(x, pieces, ident):
    return pl.pallas_call(
        first_kernel,
        out_shape=[
            jax.ShapeDtypeStruct((N_SEQ, 8, TOK_DEV // 8, WIDTH), bf16),
            jax.ShapeDtypeStruct((N_SHARD,) + pieces.shape, bf16),
        ],
        in_specs=[ANY, ANY],
        out_specs=[ANY, ANY],
        scratch_shapes=[
            pltpu.VMEM(pieces.shape, bf16),
            pltpu.SemaphoreType.DMA((12,)),
            pltpu.SemaphoreType.DMA((12,)),
            pltpu.SemaphoreType.DMA,
            pltpu.SemaphoreType.DMA((N_SEQ + N_SHARD,)),
            pltpu.SemaphoreType.DMA((N_SEQ + N_SHARD,)),
            pltpu.SemaphoreType.DMA,
        ],
        compiler_params=pltpu.CompilerParams(collective_id=ident, has_side_effects=True),
        name="gather_tokens",
    )(x, pieces)


def attention_kernel(j_ref, q_ref, kv_ref, o_ref, wide_ref, lse_ref, vt):
    i = pl.program_id(0)
    j = j_ref[0]

    @pl.when(i == 0)
    def _():
        def turn(t, carry):
            rows = pl.ds(pl.multiple_of(t * 512, 512), 512)
            vt[:, rows] = kv_ref[rows, :].T
            return carry

        lax.fori_loop(0, TOKENS // 512, turn, 0)

    queries = spread(q_ref[0], False)
    first = (i * N_SHARD + j) * TOK_DEV
    full = first // FWD_TILE

    def tile(t, carry, masked):
        peak, total, acc = carry
        rows = pl.ds(pl.multiple_of(t * FWD_TILE, FWD_TILE), FWD_TILE)
        scores = dot(kv_ref[rows, :], queries, NT)
        if masked:
            key_pos = t * FWD_TILE + lax.broadcasted_iota(jnp.int32, scores.shape, 0)
            query_pos = first + (lax.broadcasted_iota(jnp.int32, scores.shape, 1) & (TOK_DEV - 1))
            scores = jnp.where(query_pos >= key_pos, scores, -1e30)
        newest = jnp.maximum(peak, jnp.max(scores, axis=0, keepdims=True))
        weights = jnp.exp(scores - newest)
        shrink = jnp.exp(peak - newest)
        total = total * shrink + jnp.sum(weights, axis=0, keepdims=True)
        acc = acc * shrink + dot(vt[HEAD:, rows], weights.astype(bf16), NN)
        return newest, total, acc

    start = (
        jnp.full((1, 2 * TOK_DEV), -1e30, f32),
        jnp.zeros((1, 2 * TOK_DEV), f32),
        jnp.zeros((HEAD, 2 * TOK_DEV), f32),
    )
    carry = lax.fori_loop(0, full, lambda t, c: tile(t, c, False), start)
    peak, total, acc = tile(full, carry, True)
    acc = acc / total
    stacked = jnp.concatenate([acc[:, :TOK_DEV], acc[:, TOK_DEV:]], axis=0)
    wide_ref[0] = stacked
    o_ref[0] = stacked.T.astype(bf16)
    lse_ref[0] = peak + jnp.log(total)


def spread(rows, right):
    zeros = jnp.zeros((TOK_DEV, HEAD), rows.dtype)
    parts = [rows[:, :HEAD], rows[:, HEAD:]]
    if right:
        parts = [jnp.concatenate([zeros, part], axis=1) for part in parts]
    else:
        parts = [jnp.concatenate([part, zeros], axis=1) for part in parts]
    return jnp.concatenate(parts, axis=0)


def attention(shard, queries, memory):
    return pl.pallas_call(
        attention_kernel,
        grid_spec=pltpu.PrefetchScalarGridSpec(
            num_scalar_prefetch=1,
            grid=(N_SEQ,),
            in_specs=[
                pl.BlockSpec((1, TOK_DEV, 2 * HEAD), lambda i, j: (i, 0, 0)),
                pl.BlockSpec((TOKENS, 2 * HEAD), lambda i, j: (0, 0)),
            ],
            out_specs=[
                pl.BlockSpec((1, TOK_DEV, 2 * HEAD), lambda i, j: (i, 0, 0)),
                pl.BlockSpec((1, 2 * HEAD, TOK_DEV), lambda i, j: (i, 0, 0)),
                pl.BlockSpec((1, 1, 2 * TOK_DEV), lambda i, j: (i, 0, 0)),
            ],
            scratch_shapes=[pltpu.VMEM((2 * HEAD, TOKENS), bf16)],
        ),
        out_shape=[
            jax.ShapeDtypeStruct((N_SEQ, TOK_DEV, 2 * HEAD), bf16),
            jax.ShapeDtypeStruct((N_SEQ, 2 * HEAD, TOK_DEV), f32),
            jax.ShapeDtypeStruct((N_SEQ, 1, 2 * TOK_DEV), f32),
        ],
        compiler_params=pltpu.CompilerParams(vmem_limit_bytes=48 << 20),
        cost_estimate=pl.CostEstimate(
            flops=9_000_000_000, bytes_accessed=6 << 20, transcendentals=18_000_000
        ),
        name="attention_forward",
    )(shard, queries, memory)


def attention_back_kernel(
    j_ref, q_ref, g_ref, wide_ref, lse_ref, kv_ref, dq_ref, dkv_ref, kt, acc
):
    i = pl.program_id(0)
    j = j_ref[0]

    @pl.when(i == 0)
    def _():
        def turn(t, carry):
            rows = pl.ds(pl.multiple_of(t * 512, 512), 512)
            kt[:, rows] = kv_ref[rows, :].T[:HEAD]
            acc[rows, :] = jnp.zeros((512, 2 * HEAD), f32)
            return carry

        lax.fori_loop(0, TOKENS // 512, turn, 0)

    queries = spread(q_ref[0], False)
    upstream = spread(g_ref[0], True)
    lse = lse_ref[0]
    product = wide_ref[0] * g_ref[0].astype(f32).T
    delta = jnp.concatenate(
        [
            jnp.sum(product[:HEAD], axis=0, keepdims=True),
            jnp.sum(product[HEAD:], axis=0, keepdims=True),
        ],
        axis=1,
    )
    first = (i * N_SHARD + j) * TOK_DEV
    full = first // BWD_TILE

    def tile(t, query_grad, masked):
        rows = pl.ds(pl.multiple_of(t * BWD_TILE, BWD_TILE), BWD_TILE)
        memory = kv_ref[rows, :]
        scores = dot(memory, queries, NT)
        weights = jnp.exp(scores - lse)
        if masked:
            key_pos = t * BWD_TILE + lax.broadcasted_iota(jnp.int32, scores.shape, 0)
            query_pos = first + (lax.broadcasted_iota(jnp.int32, scores.shape, 1) & (TOK_DEV - 1))
            weights = jnp.where(query_pos >= key_pos, weights, 0.0)
        weight_grad = dot(memory, upstream, NT)
        score_grad = (weights * (weight_grad - delta)).astype(bf16)
        acc[rows, :] += dot(weights.astype(bf16), upstream, NN) + dot(score_grad, queries, NN)
        return query_grad + dot(kt[:, rows], score_grad, NN)

    start = jnp.zeros((HEAD, 2 * TOK_DEV), f32)
    query_grad = lax.fori_loop(0, full, lambda t, c: tile(t, c, False), start)
    query_grad = tile(full, query_grad, True) * (1.0 / math.sqrt(HEAD))
    stacked = jnp.concatenate([query_grad[:, :TOK_DEV], query_grad[:, TOK_DEV:]], axis=0)
    dq_ref[0] = stacked.T.astype(bf16)

    @pl.when(i == N_SEQ - 1)
    def _():
        def put(t, carry):
            rows = pl.ds(pl.multiple_of(t * 512, 512), 512)
            dkv_ref[rows, :] = acc[rows, :].astype(bf16)
            return carry

        lax.fori_loop(0, TOKENS // 512, put, 0)


def attention_back(shard, queries, upstream, wide, lse, memory):
    return pl.pallas_call(
        attention_back_kernel,
        grid_spec=pltpu.PrefetchScalarGridSpec(
            num_scalar_prefetch=1,
            grid=(N_SEQ,),
            in_specs=[
                pl.BlockSpec((1, TOK_DEV, 2 * HEAD), lambda i, j: (i, 0, 0)),
                pl.BlockSpec((1, TOK_DEV, 2 * HEAD), lambda i, j: (i, 0, 0)),
                pl.BlockSpec((1, 2 * HEAD, TOK_DEV), lambda i, j: (i, 0, 0)),
                pl.BlockSpec((1, 1, 2 * TOK_DEV), lambda i, j: (i, 0, 0)),
                pl.BlockSpec((TOKENS, 2 * HEAD), lambda i, j: (0, 0)),
            ],
            out_specs=[
                pl.BlockSpec((1, TOK_DEV, 2 * HEAD), lambda i, j: (i, 0, 0)),
                pl.BlockSpec((TOKENS, 2 * HEAD), lambda i, j: (0, 0)),
            ],
            scratch_shapes=[
                pltpu.VMEM((HEAD, TOKENS), bf16),
                pltpu.VMEM((TOKENS, 2 * HEAD), f32),
            ],
        ),
        out_shape=[
            jax.ShapeDtypeStruct((N_SEQ, TOK_DEV, 2 * HEAD), bf16),
            jax.ShapeDtypeStruct((TOKENS, 2 * HEAD), bf16),
        ],
        compiler_params=pltpu.CompilerParams(vmem_limit_bytes=56 << 20),
        cost_estimate=pl.CostEstimate(
            flops=23_000_000_000, bytes_accessed=12 << 20, transcendentals=18_000_000
        ),
        name="attention_backward",
    )(shard, queries, upstream, wide, lse, memory)


def expert_kernel(x_ref, g_ref, w_ref, out_ref, back_ref, wg_ref, gu, down, xt, ht, both):
    gu[...] = w_ref[0, :, :128, :].reshape(WIDTH, 2 * FF)
    down[...] = w_ref[0, :, 128:, :].reshape(FF, WIDTH)

    def rows_step(t, carry):
        rows = pl.ds(pl.multiple_of(t * 128, 128), 128)
        x = x_ref[0, rows, :]
        pre = dot(x, gu[...], NN)
        gate, up = pre[:, :FF], pre[:, FF:]
        sigmoid = jax.nn.sigmoid(gate)
        act = gate * sigmoid
        hidden = (act * up).astype(bf16)
        out_ref[0, rows, :] = dot(hidden, down[...], NN).astype(bf16)
        units = dot(g_ref[0, rows, :], down[...], NT)
        gate_grad = (units * up * sigmoid * (1.0 + gate * (1.0 - sigmoid))).astype(bf16)
        up_grad = (units * act).astype(bf16)
        pair = jnp.concatenate([gate_grad, up_grad], axis=1)
        back_ref[0, rows, :] = dot(pair, gu[...], NT).astype(bf16)
        both[rows, :] = pair
        xt[:, rows] = x.T
        ht[:, rows] = hidden.T
        return carry

    lax.fori_loop(0, EXPERT_ROWS // 128, rows_step, 0)

    def grad_step(s, carry):
        features = pl.ds(pl.multiple_of(s * 128, 128), 128)
        units = pl.ds(pl.multiple_of(s * 64, 64), 64)
        wg_ref[s, 0, :128, :] = dot(xt[features, :], both[...], NN).astype(bf16)
        wg_ref[s, 0, 128:, :] = dot(ht[units, :], g_ref[0], NN).astype(bf16)
        return carry

    lax.fori_loop(0, N_SEQ, grad_step, 0)


def experts(x, g, w):
    rows = pl.BlockSpec((1, EXPERT_ROWS, WIDTH), lambda e: (e, 0, 0))
    shape = jax.ShapeDtypeStruct((LOCAL_EXPERTS, EXPERT_ROWS, WIDTH), bf16)
    return pl.pallas_call(
        expert_kernel,
        grid=(LOCAL_EXPERTS,),
        in_specs=[rows, rows, pl.BlockSpec((1, N_SEQ, 192, WIDTH), lambda e: (e, 0, 0, 0))],
        out_specs=[rows, rows, pl.BlockSpec((N_SEQ, 1, 192, WIDTH), lambda e: (0, e, 0, 0))],
        out_shape=[
            shape,
            shape,
            jax.ShapeDtypeStruct((N_SEQ, LOCAL_EXPERTS, 192, WIDTH), bf16),
        ],
        scratch_shapes=[
            pltpu.VMEM((WIDTH, 2 * FF), bf16),
            pltpu.VMEM((FF, WIDTH), bf16),
            pltpu.VMEM((WIDTH, EXPERT_ROWS), bf16),
            pltpu.VMEM((FF, EXPERT_ROWS), bf16),
            pltpu.VMEM((EXPERT_ROWS, 2 * FF), bf16),
        ],
        compiler_params=pltpu.CompilerParams(vmem_limit_bytes=56 << 20),
        cost_estimate=pl.CostEstimate(
            flops=12_000_000_000, bytes_accessed=24 << 20, transcendentals=1_000_000
        ),
        name="experts",
    )(x, g, w)


def group_columns(rows):
    lead = rows.shape[:-1]
    queries = rows[..., : HEADS * HEAD].reshape(lead + (N_SEQ, 2 * HEAD))
    keys = rows[..., HEADS * HEAD : (HEADS + KV) * HEAD].reshape(lead + (N_SEQ, HEAD))
    values = rows[..., (HEADS + KV) * HEAD :].reshape(lead + (N_SEQ, HEAD))
    return jnp.concatenate([queries, keys, values], axis=-1)


def ungroup_columns(groups):
    rows = groups.shape[0]
    return jnp.concatenate(
        [
            groups[:, :, : 2 * HEAD].reshape(rows, HEADS * HEAD),
            groups[:, :, 2 * HEAD : 3 * HEAD].reshape(rows, KV * HEAD),
            groups[:, :, 3 * HEAD :].reshape(rows, KV * HEAD),
        ],
        axis=1,
    )


def rope_pair(shard):
    half = HEAD // 2
    frequency = jnp.exp(
        jnp.arange(half, dtype=f32) * jnp.float32(-2.0 * math.log(rope_base) / HEAD)
    )
    chunk = jnp.arange(N_SEQ, dtype=jnp.int32)[:, None] * N_SHARD + shard
    position = chunk * TOK_DEV + jnp.arange(TOK_DEV, dtype=jnp.int32)[None, :]
    angles = position.reshape(HEAD_ROWS, 1).astype(f32) * frequency[None, :]
    return jnp.tile(jnp.cos(angles), (1, 6)), jnp.tile(jnp.sin(angles), (1, 6))


def turn_matrix():
    row = jnp.arange(3 * HEAD, dtype=jnp.int32)[:, None]
    col = jnp.arange(3 * HEAD, dtype=jnp.int32)[None, :]
    half = HEAD // 2
    low = col % HEAD < half
    minus = low & (row == col + half)
    plus = (~low) & (row == col - half)
    return (plus.astype(f32) - minus.astype(f32)).astype(bf16)


def on_device(
    layer_input,
    attn_gain,
    moe_gain,
    w_qkv,
    w_out,
    w_gate,
    w_up,
    w_down,
    routes,
    route_weights,
    cotangent,
):
    shard = lax.axis_index("shard")
    shard_array = shard.astype(jnp.int32).reshape(1)

    expert_pack = jnp.concatenate(
        [jnp.concatenate([w_gate, w_up], axis=2), w_down], axis=1
    )
    grouped = group_columns(w_qkv)
    projections = jnp.concatenate([w_out, grouped.reshape(8, 2 * WIDTH)], axis=1)
    projections = lax.all_gather(projections, "shard", axis=0, tiled=True)
    expert_weights = lax.all_gather(expert_pack, "seq", axis=1)
    pieces = grouped.transpose(1, 0, 2).reshape(N_SEQ, 8, 2, 128).transpose(0, 2, 1, 3)
    gains = jnp.concatenate([attn_gain, moe_gain, jnp.zeros((112,), bf16)])
    gains = jnp.broadcast_to(gains[None, None, :], (N_SEQ, 16, 128))
    pieces = jnp.concatenate([pieces.reshape(N_SEQ, 16, 128), gains], axis=1)
    tokens, columns = first_gather(
        layer_input.reshape(8, TOK_DEV // 8, WIDTH), pieces, 1
    )
    gain_rows = columns[:, :, 16, :16].transpose(1, 0, 2)
    gain_attn = gain_rows[:, :, :8].reshape(WIDTH).astype(f32)
    gain_moe = gain_rows[:, :, 8:].reshape(WIDTH).astype(f32)
    columns = columns[:, :, :16].reshape(N_SHARD, N_SEQ, 2, 8, 128)
    columns = columns.transpose(1, 0, 3, 2, 4).reshape(WIDTH, COLS)

    wide = tokens.reshape(HEAD_ROWS, WIDTH).astype(f32)
    inverse = lax.rsqrt(jnp.mean(wide * wide, axis=1, keepdims=True) + epsilon)
    normed = (wide * inverse * gain_attn).astype(bf16)
    cosine, sine = rope_pair(shard)
    turn = turn_matrix()
    turned = dot(columns[:, : 3 * HEAD], turn, NN).astype(bf16)
    projected = dot(normed, jnp.concatenate([columns, turned], axis=1), NN)
    rotated = projected[:, : 3 * HEAD] * cosine + projected[:, COLS:] * sine
    queries = rotated[:, : 2 * HEAD].astype(bf16) * jnp.bfloat16(1.0 / math.sqrt(HEAD))
    queries = queries.reshape(N_SEQ, TOK_DEV, 2 * HEAD)
    memory = jnp.concatenate(
        [rotated[:, 2 * HEAD :], projected[:, 3 * HEAD : COLS]], axis=1
    ).astype(bf16)
    memory = gather_memory(memory.reshape(N_SEQ, TOK_DEV, 2 * HEAD), 2)
    memory = memory.reshape(TOKENS, 2 * HEAD)

    flat_routes = routes.reshape(TOK_DEV * TOPK)
    onehot = (flat_routes[:, None] == jnp.arange(EXPERTS, dtype=jnp.int32)[None, :]).astype(
        jnp.int32
    )
    slot_index = jnp.sum((jnp.cumsum(onehot, axis=0) - 1) * onehot, axis=1)
    slot_row = flat_routes % LOCAL_EXPERTS * N_SHARD + flat_routes // LOCAL_EXPERTS
    slot_place = (slot_row * CAP + slot_index).reshape(TOK_DEV, TOPK)
    here = slot_place[:, :, None] == jnp.arange(EXPERTS * CAP, dtype=jnp.int32)[None, None, :]
    pick = jnp.sum(here.astype(f32), axis=1)
    scale = jnp.sum(jnp.where(here, route_weights[:, :, None], 0.0), axis=1)
    pick = pick.astype(bf16)
    scale_high = scale.astype(bf16)
    scale_low = (scale - scale_high.astype(f32)).astype(bf16)
    slot_scale = jnp.sum(scale, axis=0)[:, None]
    out_grad = cotangent.astype(f32)
    slots = (LOCAL_EXPERTS, N_SHARD, CAP, WIDTH)
    grad_send = (slot_scale * dot(pick, cotangent, TN)).astype(bf16).reshape(slots)
    grad_rows = [
        lax.all_to_all(grad_send[e], "shard", 0, 0).reshape(EXPERT_ROWS, WIDTH)
        for e in range(LOCAL_EXPERTS)
    ]
    grad_rows = jnp.stack(grad_rows)

    attended, attended_wide, lse = attention(shard_array, queries, memory)
    out_weight = lax.all_to_all(
        jnp.broadcast_to(projections[None, :, :WIDTH], (N_SEQ, 128, WIDTH)), "seq", 0, 0
    ).reshape(WIDTH, WIDTH)

    attended_full = exchange(attended, "seq", N_SEQ, 3)
    attended_full = attended_full.transpose(1, 0, 2).reshape(TOK_DEV, WIDTH)
    x_wide = layer_input.astype(f32)
    residual = x_wide + dot(attended_full, out_weight, NN)
    inverse_two = lax.rsqrt(jnp.mean(residual * residual, axis=1, keepdims=True) + epsilon)
    normed_moe = (residual * inverse_two * gain_moe).astype(bf16)

    send_rows = dot(pick, normed_moe, TN).astype(bf16).reshape(slots)
    expert_rows = exchange(send_rows, "shard", N_SHARD, 4, dim=1)
    expert_rows = expert_rows.reshape(LOCAL_EXPERTS, EXPERT_ROWS, WIDTH)
    expert_out, rows_grad, expert_grads = experts(expert_rows, grad_rows, expert_weights)
    returned = exchange(rows_grad.reshape(slots), "shard", N_SHARD, 5, dim=1)
    expert_out = expert_out.reshape(slots)
    came_back = [
        lax.all_to_all(expert_out[e], "shard", 0, 0).reshape(EXPERT_ROWS, WIDTH)
        for e in range(LOCAL_EXPERTS)
    ]
    came_back = jnp.concatenate(came_back, axis=0)
    moe_sum = dot(scale_high, came_back, NN) + dot(scale_low, came_back, NN)
    block_out = (residual + moe_sum).astype(bf16)
    expert_grads = lax.all_to_all(expert_grads, "seq", 0, 0)
    expert_sums = jnp.sum(expert_grads.astype(f32), axis=0)

    moe_in_grad = dot(pick, returned.reshape(EXPERTS * CAP, WIDTH), NN)
    scaled = moe_in_grad * gain_moe
    moe_part = inverse_two * scaled - residual * inverse_two**3 * jnp.mean(
        residual * scaled, axis=1, keepdims=True
    )
    residual_grad = out_grad + moe_part
    branch_grad = residual_grad.astype(bf16)
    attended_grad = dot(branch_grad, out_weight, NT).astype(bf16)
    attended_grad = attended_grad.reshape(TOK_DEV, N_SEQ, 2 * HEAD).transpose(1, 0, 2)
    attended_grad = exchange(attended_grad, "seq", N_SEQ, 6)
    branch_all = lax.all_to_all(
        jnp.broadcast_to(branch_grad[None], (N_SEQ, TOK_DEV, WIDTH)), "seq", 0, 0
    ).reshape(HEAD_ROWS, WIDTH)

    query_grad, memory_grad = attention_back(
        shard_array, queries, attended_grad, attended_wide, lse, memory
    )
    memory_grad = memory_grad.reshape(N_SEQ, N_SHARD, TOK_DEV, 2 * HEAD)
    memory_grad = exchange(memory_grad, "shard", N_SHARD, 7, dim=1)
    memory_grad = jnp.sum(memory_grad.astype(f32), axis=1).astype(bf16)
    memory_grad = memory_grad.reshape(HEAD_ROWS, 2 * HEAD)
    rotary = jnp.concatenate(
        [query_grad.reshape(HEAD_ROWS, 2 * HEAD), memory_grad[:, :HEAD]], axis=1
    )
    rotary = rotary.astype(f32) * cosine + dot(rotary, turn, NT) * sine
    projected_grad = jnp.concatenate([rotary.astype(bf16), memory_grad[:, HEAD:]], axis=1)
    token_grad = exchange(projected_grad.reshape(N_SEQ, TOK_DEV, COLS), "seq", N_SEQ, 8)

    qkv_part = dot(normed, projected_grad, TN)
    qkv_part = qkv_part.reshape(N_SEQ, N_SHARD, 8, COLS).transpose(1, 0, 2, 3)
    out_part = dot(attended.reshape(HEAD_ROWS, 2 * HEAD), branch_all, TN)
    out_part = out_part.reshape(N_SHARD, 8, WIDTH)
    pack = expert_pack.astype(f32)
    moe_gain_part = jnp.sum(
        pack[:, :128] * expert_sums[:, :128], axis=(0, 2)
    ) / lax.dynamic_slice_in_dim(gain_moe, lax.axis_index("seq") * 128, 128)
    moe_gain_part = moe_gain_part.reshape(N_SHARD, 1, 8)
    moe_gain_high = moe_gain_part.astype(bf16)
    moe_gain_low = (moe_gain_part - moe_gain_high.astype(f32)).astype(bf16)
    gain_part = jnp.concatenate([moe_gain_high, moe_gain_low], axis=1)
    gain_part = jnp.pad(gain_part, ((0, 0), (0, 14), (0, COLS - 8)))
    sums = jnp.concatenate(
        [
            qkv_part.reshape(N_SHARD, 64, COLS).astype(bf16),
            out_part.reshape(N_SHARD, 32, COLS).astype(bf16),
            gain_part,
        ],
        axis=1,
    )
    sums = jnp.sum(exchange(sums, "shard", N_SHARD, 9).astype(f32), axis=0)
    out_weight_grad = sums[64:96].reshape(8, WIDTH)
    moe_gain_grad = sums[96, :8] + sums[97, :8]
    qkv_groups = exchange(sums[:64].reshape(N_SEQ, 8, COLS), "seq", N_SEQ, 10).transpose(1, 0, 2)
    attn_gain_grad = jnp.sum(grouped.astype(f32) * qkv_groups, axis=(1, 2)) / attn_gain.astype(f32)
    qkv_weight_grad = ungroup_columns(qkv_groups)

    qkv_all = lax.all_gather(projections[:, WIDTH:], "seq", axis=0, tiled=True)
    token_grad = token_grad.transpose(1, 0, 2).reshape(TOK_DEV, N_SEQ * COLS)
    normed_grad = dot(token_grad, qkv_all, NT)
    inverse_one = lax.rsqrt(jnp.mean(x_wide * x_wide, axis=1, keepdims=True) + epsilon)
    scaled = normed_grad * gain_attn
    attn_part = inverse_one * scaled - x_wide * inverse_one**3 * jnp.mean(
        x_wide * scaled, axis=1, keepdims=True
    )
    input_grad = (residual_grad + attn_part).astype(bf16)
    return (
        block_out,
        input_grad,
        attn_gain_grad,
        moe_gain_grad,
        qkv_weight_grad,
        out_weight_grad,
        expert_sums[:, :128, :FF],
        expert_sums[:, :128, FF:],
        expert_sums[:, 128:],
    )


def solution(mesh):
    token = P(("seq", "shard"), None)
    vector = P(("seq", "shard"))
    expert = P("shard", "seq", None)
    return jax.shard_map(
        on_device,
        mesh=mesh,
        in_specs=(
            token,
            vector,
            vector,
            token,
            token,
            expert,
            expert,
            expert,
            token,
            token,
            token,
        ),
        out_specs=(token, token, vector, vector, token, token, expert, expert, expert),
        check_vma=False,
    )
```

```python
import functools
import math

import jax
import jax.numpy as jnp
from jax import lax
from jax.experimental import pallas as pl
from jax.experimental.pallas import tpu as pltpu
from jax.sharding import PartitionSpec as P

HEADS = 16
KV = 8
HEAD = 64
EXPERTS = 32
TOPK = 8
TOK_DEV = 128
CAP = 40
WIDTH = 1024
FF = 512
N_SEQ = 8
N_SHARD = 16
HEAD_ROWS = TOK_DEV * N_SEQ
TOKENS = TOK_DEV * N_SEQ * N_SHARD
LOCAL_EXPERTS = EXPERTS // N_SHARD
EXPERT_ROWS = N_SHARD * CAP
COLS = 256
SUPER = TOK_DEV * N_SHARD
BWD_TILE = 1024

epsilon = 1e-06
rope_base = 10000.0

f32 = jnp.float32
bf16 = jnp.bfloat16
MESH = pl.DeviceIdType.MESH
ANY = pl.BlockSpec(memory_space=pl.ANY)
NT = (((1,), (1,)), ((), ()))
NN = (((1,), (0,)), ((), ()))
TN = (((0,), (0,)), ((), ()))


def dot(left, right, dims):
    return lax.dot_general(left, right, dims, preferred_element_type=f32)


def greet(peers):
    barrier = pltpu.get_barrier_semaphore()
    for axis, peer in peers:
        pl.semaphore_signal(barrier, inc=1, device_id={axis: peer}, device_id_type=MESH)
    pl.semaphore_wait(barrier, len(peers))


def remote(source, target, send, recv, axis, peer):
    copy = pltpu.make_async_remote_copy(
        src_ref=source,
        dst_ref=target,
        send_sem=send,
        recv_sem=recv,
        device_id={axis: peer},
        device_id_type=MESH,
    )
    copy.start()
    return copy


def exchange_kernel(axis, count, dim, x_ref, o_ref, send, recv, own):
    def block(ref, index):
        return ref.at[:, index] if dim == 1 else ref.at[index]

    me = lax.axis_index(axis)
    greet([(axis, lax.rem(me + k, count)) for k in range(1, count)])
    mine = pltpu.make_async_copy(block(x_ref, me), block(o_ref, me), own)
    mine.start()
    copies = []
    for k in range(1, count):
        peer = lax.rem(me + k, count)
        copies.append(
            remote(block(x_ref, peer), block(o_ref, me), send.at[k - 1], recv.at[k - 1], axis, peer)
        )
    mine.wait()
    for copy in copies:
        copy.wait()


def exchange(x, axis, count, ident, dim=0):
    return pl.pallas_call(
        functools.partial(exchange_kernel, axis, count, dim),
        out_shape=jax.ShapeDtypeStruct(x.shape, x.dtype),
        in_specs=[ANY],
        out_specs=ANY,
        scratch_shapes=[
            pltpu.SemaphoreType.DMA((count - 1,)),
            pltpu.SemaphoreType.DMA((count - 1,)),
            pltpu.SemaphoreType.DMA,
        ],
        compiler_params=pltpu.CompilerParams(collective_id=ident, has_side_effects=True),
        name="exchange_" + axis,
    )(x)


def staged(axis, units, share, x_ref, place, sem_send, sem_recv, own):
    me = lax.axis_index(axis)
    cores = 2 if axis == "shard" else 1
    core = lax.rem(me, cores)
    pair = lax.rem(me // cores, 2)
    ring = me // (2 * cores)

    def at(r, p, c):
        return (r * 2 + p) * cores + c

    ring_peer = [at(lax.rem(ring + k, 4), pair, core) for k in (1, 2, 3)]
    ring_from = [lax.rem(ring + 4 - k, 4) for k in (1, 2, 3)]
    pair_peer = at(ring, 1 - pair, core)
    core_peer = at(ring, pair, 1 - core)
    mine = pltpu.make_async_copy(x_ref, place(me, 0, units), own)
    mine.start()
    sends = []

    def go(source, index, low, high, peer):
        n = len(sends)
        sends.append(
            remote(source, place(index, low, high), sem_send.at[n], sem_recv.at[n], axis, peer)
        )
        return sends[-1]

    to_pair = go(x_ref, me, 0, units, pair_peer)
    to_ring = [go(x_ref, me, 0, units, peer) for peer in ring_peer]
    landed = []
    if cores == 2:
        landed.append(go(x_ref, me, 0, units, core_peer))

    def pass_core(index, low, high):
        if cores == 2:
            landed.append(go(place(index, low, high), index, low, high, core_peer))

    to_pair.wait_recv()
    fwd_ring = [
        go(place(pair_peer, 0, share), pair_peer, 0, share, peer) for peer in ring_peer
    ]
    pass_core(pair_peer, 0, units)
    fwd_pair = []
    for k in (0, 2, 1):
        to_ring[k].wait_recv()
        source = at(ring_from[k], pair, core)
        if share < units:
            fwd_pair.append((k, go(place(source, share, units), source, share, units, pair_peer)))
        pass_core(source, 0, units)
    for k in (0, 2, 1):
        fwd_ring[k].wait_recv()
        pass_core(at(ring_from[k], 1 - pair, core), 0, share)
    for k, copy in fwd_pair:
        copy.wait_recv()
        pass_core(at(ring_from[k], 1 - pair, core), share, units)
    for copy in landed:
        copy.wait_recv()
    mine.wait()
    for copy in sends:
        copy.wait_send()


def first_kernel(
    x_ref, w_ref, v_ref, xo_ref, wo_ref, vo_ref, w_mid, w_pack, send, recv, own, wsend, wrecv, wown, vown
):
    seq = lax.axis_index("seq")
    shard = lax.axis_index("shard")
    far = lax.rem(seq, 2)
    partner = seq + 1 - 2 * far
    greet(
        [("seq", lax.rem(seq + k, N_SEQ)) for k in range(1, N_SEQ)]
        + [("shard", lax.rem(shard + k, N_SHARD)) for k in range(1, N_SHARD)]
    )
    mine = pltpu.make_async_copy(w_ref.at[seq], w_mid.at[seq], wown)
    mine.start()
    slab = pltpu.make_async_copy(v_ref, vo_ref.at[far, shard], vown)
    slab.start()
    pieces = []
    for k in range(1, N_SEQ):
        peer = lax.rem(seq + k, N_SEQ)
        pieces.append(
            remote(w_ref.at[peer], w_mid.at[seq], wsend.at[k - 1], wrecv.at[k - 1], "seq", peer)
        )
    rows = []
    for k in range(1, N_SHARD):
        peer = lax.rem(shard + k, N_SHARD)
        n = 21 + k
        rows.append(
            remote(v_ref, vo_ref.at[far, shard], wsend.at[n], wrecv.at[n], "shard", peer)
        )
    mine.wait()
    for piece in pieces:
        piece.wait()
    packed = jnp.zeros((16, 128), f32)
    row = lax.broadcasted_iota(jnp.int32, (16, 128), 0)
    for s in range(N_SEQ):
        packed = jnp.where(row == s, w_mid[s, 16:].astype(f32), packed)
        w_pack[s] = w_mid[s, :16]
    w_pack[N_SEQ] = packed.astype(bf16)
    mine = pltpu.make_async_copy(w_pack, wo_ref.at[shard], wown)
    mine.start()
    pieces = []
    for k in range(1, N_SHARD):
        peer = lax.rem(shard + k, N_SHARD)
        n = 6 + k
        pieces.append(
            remote(w_pack, wo_ref.at[shard], wsend.at[n], wrecv.at[n], "shard", peer)
        )
    staged("seq", 8, 8, x_ref, lambda s, low, high: xo_ref.at[s, low:high], send, recv, own)
    slab.wait()
    for row in rows:
        row.wait()
    pair = remote(vo_ref.at[far], vo_ref.at[far], wsend.at[37], wrecv.at[37], "seq", partner)
    mine.wait()
    for piece in pieces:
        piece.wait()
    pair.wait()


def first_gather(x, pieces, rows, ident):
    return pl.pallas_call(
        first_kernel,
        out_shape=[
            jax.ShapeDtypeStruct((N_SEQ, 8, TOK_DEV // 8, WIDTH), bf16),
            jax.ShapeDtypeStruct((N_SHARD, N_SEQ + 1, 16, 128), bf16),
            jax.ShapeDtypeStruct((2, N_SHARD) + rows.shape, bf16),
        ],
        in_specs=[ANY, ANY, ANY],
        out_specs=[ANY, ANY, ANY],
        scratch_shapes=[
            pltpu.VMEM(pieces.shape, bf16),
            pltpu.VMEM((N_SEQ + 1, 16, 128), bf16),
            pltpu.SemaphoreType.DMA((12,)),
            pltpu.SemaphoreType.DMA((12,)),
            pltpu.SemaphoreType.DMA,
            pltpu.SemaphoreType.DMA((38,)),
            pltpu.SemaphoreType.DMA((38,)),
            pltpu.SemaphoreType.DMA,
            pltpu.SemaphoreType.DMA,
        ],
        compiler_params=pltpu.CompilerParams(collective_id=ident, has_side_effects=True),
        name="gather_tokens",
    )(x, pieces, rows)


def spread(rows, right):
    zeros = jnp.zeros((TOK_DEV, HEAD), rows.dtype)
    parts = [rows[:, :HEAD], rows[:, HEAD:]]
    if right:
        parts = [jnp.concatenate([zeros, part], axis=1) for part in parts]
    else:
        parts = [jnp.concatenate([part, zeros], axis=1) for part in parts]
    return jnp.concatenate(parts, axis=0)


def admitted(shape, j, first_key):
    key_pos = first_key + lax.broadcasted_iota(jnp.int32, shape, 0)
    query_pos = j * TOK_DEV + (lax.broadcasted_iota(jnp.int32, shape, 1) & (TOK_DEV - 1))
    return query_pos >= key_pos


def transfer(source, target, send, recv, axis, peer):
    return pltpu.make_async_remote_copy(
        src_ref=source,
        dst_ref=target,
        send_sem=send,
        recv_sem=recv,
        device_id={axis: peer},
        device_id_type=MESH,
    )


def everyone(seq, shard):
    return [("seq", lax.rem(seq + k, N_SEQ)) for k in range(1, N_SEQ)] + [
        ("shard", lax.rem(shard + k, N_SHARD)) for k in range(1, N_SHARD)
    ]


def attention_kernel(
    q_ref,
    kv_ref,
    cot_ref,
    slab_ref,
    wide_ref,
    lse_ref,
    att_ref,
    mem_ref,
    cot_out,
    slab_out,
    land,
    vt,
    heads,
    peak_ref,
    total_ref,
    acc_ref,
    ksend,
    krecv,
    gsend,
    grecv,
    esend,
    erecv,
    fsend,
    frecv,
    own,
    msem,
):
    seq = lax.axis_index("seq")
    me = lax.axis_index("shard")
    core = lax.rem(me, 2)
    pair = lax.rem(me // 2, 2)
    ring = me // 4

    def at(k, other_pair, other_core):
        p = 1 - pair if other_pair else pair
        c = 1 - core if other_core else core
        return (lax.rem(ring + 4 + k, 4) * 2 + p) * 2 + c

    def message(t, m, block, peer):
        return transfer(
            land.at[t, block], land.at[t, block], ksend.at[t, m], krecv.at[t, m], "shard", peer
        )

    def first(t):
        for k in (1, 2, 3):
            message(t, k - 1, me, at(k, 0, 0)).start()
        message(t, 3, me, at(0, 1, 0)).start()
        message(t, 4, me, at(0, 0, 1)).start()

    def second(t):
        block = at(0, 1, 0)
        message(t, 3, block, block).wait_recv()
        for k in (1, 2, 3):
            message(t, 4 + k, block, at(k, 0, 0)).start()
        message(t, 8, block, at(0, 0, 1)).start()
        for k in (1, 2, 3):
            block = at(-k, 0, 0)
            message(t, k - 1, block, block).wait_recv()
            message(t, 8 + k, block, at(0, 0, 1)).start()

    def third(t):
        for k in (1, 2, 3):
            block = at(-k, 1, 0)
            message(t, 4 + k, block, at(-k, 0, 0)).wait_recv()
            message(t, 11 + k, block, at(0, 0, 1)).start()

    def fourth(t):
        peer = at(0, 0, 1)
        message(t, 4, peer, peer).wait_recv()
        message(t, 8, at(0, 1, 1), peer).wait_recv()
        for k in (1, 2, 3):
            message(t, 8 + k, at(-k, 0, 1), peer).wait_recv()
            message(t, 11 + k, at(-k, 1, 1), peer).wait_recv()

    def to_expert(k):
        peer = lax.rem(me + k, N_SHARD)
        return transfer(
            cot_ref.at[peer], cot_out.at[me], esend.at[k - 1], erecv.at[k - 1], "shard", peer
        )

    def to_ring(k):
        peer = lax.rem(seq + 2 * k, N_SEQ)
        return transfer(slab_ref, slab_out.at[k], fsend.at[k - 1], frecv.at[k - 1], "seq", peer)

    def to_token(t, source):
        return transfer(
            heads.at[t], att_ref.at[source], gsend.at[t], grecv.at[source], "seq", t
        )

    greet(everyone(seq, me))

    def begin(t, carry):
        land[t, me] = kv_ref[t]
        first(t)
        peak_ref[t] = jnp.full((1, 2 * TOK_DEV), -1e30, f32)
        total_ref[t] = jnp.zeros((1, 2 * TOK_DEV), f32)
        acc_ref[t] = jnp.zeros((HEAD, 2 * TOK_DEV), f32)
        return carry

    lax.fori_loop(0, N_SEQ, begin, 0)
    second(0)
    third(0)
    second(1)
    fourth(0)
    for k in range(1, N_SHARD):
        to_expert(k).start()
    for k in (1, 2, 3):
        to_ring(k).start()
    cot_own = pltpu.make_async_copy(cot_ref.at[me], cot_out.at[me], own.at[0])
    cot_own.start()
    slab_own = pltpu.make_async_copy(slab_ref, slab_out.at[0], own.at[1])
    slab_own.start()

    def tile(t, i, masked):
        queries = spread(q_ref[i], False)
        scores = dot(land[t].reshape(SUPER, 2 * HEAD), queries, NT)
        if masked:
            scores = jnp.where(admitted(scores.shape, me, 0), scores, -1e30)
        peak = peak_ref[i]
        newest = jnp.maximum(peak, jnp.max(scores, axis=0, keepdims=True))
        weights = jnp.exp(scores - newest)
        shrink = jnp.exp(peak - newest)
        total = total_ref[i] * shrink + jnp.sum(weights, axis=0, keepdims=True)
        acc = acc_ref[i] * shrink + dot(vt[...], weights.astype(bf16), NN)
        return newest, total, acc

    def step(t, carry):
        pltpu.make_async_copy(land.at[t], mem_ref.at[t], msem.at[t]).start()

        @pl.when(t + 1 < N_SEQ)
        def _():
            third(t + 1)

        @pl.when(t + 2 < N_SEQ)
        def _():
            second(t + 2)

        for n in range(4):
            rows = land[t, 4 * n : 4 * n + 4].reshape(512, 2 * HEAD)
            vt[:, 512 * n : 512 * n + 512] = rows.T[HEAD:]
        newest, total, acc = tile(t, t, True)
        acc = acc / total
        stacked = jnp.concatenate([acc[:, :TOK_DEV], acc[:, TOK_DEV:]], axis=0)
        wide_ref[t] = stacked
        heads[t] = stacked.T.astype(bf16)
        lse_ref[t] = newest + jnp.log(total)

        @pl.when(t != seq)
        def _():
            to_token(t, seq).start()

        def rest(i, inner):
            peak_ref[i], total_ref[i], acc_ref[i] = tile(t, i, False)
            return inner

        lax.fori_loop(t + 1, N_SEQ, rest, 0)

        @pl.when(t + 1 < N_SEQ)
        def _():
            fourth(t + 1)

        return carry

    lax.fori_loop(0, N_SEQ, step, 0)
    mine = pltpu.make_async_copy(heads.at[seq], att_ref.at[seq], own.at[2])
    mine.start()
    for k in range(1, N_SEQ):
        to_token(lax.rem(seq + k, N_SEQ), seq).wait_send()
        source = lax.rem(seq + k, N_SEQ)
        to_token(source, source).wait_recv()
    mine.wait()
    cot_own.wait()
    slab_own.wait()
    for k in range(1, N_SHARD):
        to_expert(k).wait()
    for k in (1, 2, 3):
        to_ring(k).wait()

    def end(t, carry):
        for m in range(15):
            message(t, m, me, me).wait_send()
        pltpu.make_async_copy(land.at[t], mem_ref.at[t], msem.at[t]).wait()
        return carry

    lax.fori_loop(0, N_SEQ, end, 0)


def attention(queries, memory, cot_rows, slab, ident):
    dma = pltpu.SemaphoreType.DMA
    vmem = pl.BlockSpec(memory_space=pltpu.VMEM)
    return pl.pallas_call(
        attention_kernel,
        in_specs=[vmem, vmem, ANY, ANY],
        out_specs=[vmem, vmem, ANY, ANY, ANY, ANY],
        out_shape=[
            jax.ShapeDtypeStruct((N_SEQ, 2 * HEAD, TOK_DEV), f32),
            jax.ShapeDtypeStruct((N_SEQ, 1, 2 * TOK_DEV), f32),
            jax.ShapeDtypeStruct((N_SEQ, TOK_DEV, 2 * HEAD), bf16),
            jax.ShapeDtypeStruct((N_SEQ, N_SHARD, TOK_DEV, 2 * HEAD), bf16),
            jax.ShapeDtypeStruct(cot_rows.shape, bf16),
            jax.ShapeDtypeStruct((4,) + slab.shape, bf16),
        ],
        scratch_shapes=[
            pltpu.VMEM((N_SEQ, N_SHARD, TOK_DEV, 2 * HEAD), bf16),
            pltpu.VMEM((HEAD, SUPER), bf16),
            pltpu.VMEM((N_SEQ, TOK_DEV, 2 * HEAD), bf16),
            pltpu.VMEM((N_SEQ, 1, 2 * TOK_DEV), f32),
            pltpu.VMEM((N_SEQ, 1, 2 * TOK_DEV), f32),
            pltpu.VMEM((N_SEQ, HEAD, 2 * TOK_DEV), f32),
            dma((N_SEQ, 15)),
            dma((N_SEQ, 15)),
            dma((N_SEQ,)),
            dma((N_SEQ,)),
            dma((N_SHARD - 1,)),
            dma((N_SHARD - 1,)),
            dma((3,)),
            dma((3,)),
            dma((3,)),
            dma((N_SEQ,)),
        ],
        compiler_params=pltpu.CompilerParams(
            collective_id=ident, has_side_effects=True, vmem_limit_bytes=48 << 20
        ),
        name="attention_forward",
    )(queries, memory, cot_rows, slab)


def attention_back_kernel(*refs):
    (q_ref, g_ref, wide_ref, lse_ref, mem_ref, cos_ref, sin_ref, turn_ref, eo_ref) = refs[:9]
    parts = refs[9:15]
    pgq_ref, pgm_ref, tokq_ref, tokm_ref, came_ref = refs[15:20]
    parts_out = refs[20:26]
    gl, qs, gs, delta_ref, kt, acc, dq, stage, dl = refs[26:35]
    dsend, drecv, osend, orecv, jsend, jrecv, psend, precv, nsend, nrecv, own = refs[35:]
    seq = lax.axis_index("seq")
    me = lax.axis_index("shard")

    def to_head(k, source, peer):
        return transfer(
            g_ref.at[peer], gl.at[source], osend.at[k - 1], orecv.at[k - 1], "seq", peer
        )

    def to_token_expert(k):
        peer = lax.rem(me + k, N_SHARD)
        return transfer(
            eo_ref.at[:, peer], came_ref.at[:, me], jsend.at[k - 1], jrecv.at[k - 1], "shard", peer
        )

    def to_ring(n):
        peer = lax.rem(seq + 2 * (n % 3 + 1), N_SEQ)
        return transfer(parts[n], parts_out[n], psend.at[n], precv.at[n], "seq", peer)

    def to_owner(t, k, block, source, peer):
        return transfer(
            stage.at[t, block], dl.at[t, source], dsend.at[t, k - 1], drecv.at[t, k - 1], "shard", peer
        )

    def to_token(n, t, source):
        ref, out = ((pgq_ref, tokq_ref), (pgm_ref, tokm_ref))[n]
        return transfer(
            ref.at[t], out.at[source], nsend.at[n, t], nrecv.at[n, source], "seq", t
        )

    greet(everyone(seq, me))
    for k in range(1, N_SEQ):
        to_head(k, seq, lax.rem(seq + k, N_SEQ)).start()
    mine = pltpu.make_async_copy(g_ref.at[seq], gl.at[seq], own.at[0])
    mine.start()
    came_own = pltpu.make_async_copy(eo_ref.at[:, me], came_ref.at[:, me], own.at[1])
    came_own.start()
    mine.wait()
    for k in range(1, N_SEQ):
        source = lax.rem(seq + N_SEQ - k, N_SEQ)
        to_head(k, source, source).wait_recv()
    for n in range(6):
        to_ring(n).start()
    for k in range(1, N_SHARD):
        to_token_expert(k).start()

    def begin(i, carry):
        qs[i] = spread(q_ref[i], False)
        gs[i] = spread(gl[i], True)
        product = wide_ref[i] * gl[i].astype(f32).T
        delta_ref[i] = jnp.concatenate(
            [
                jnp.sum(product[:HEAD], axis=0, keepdims=True),
                jnp.sum(product[HEAD:], axis=0, keepdims=True),
            ],
            axis=1,
        )
        dq[i] = jnp.zeros((HEAD, 2 * TOK_DEV), f32)
        return carry

    lax.fori_loop(0, N_SEQ, begin, 0)

    def tile(t, i, n, masked):
        here = slice(n * BWD_TILE, (n + 1) * BWD_TILE)
        memory = mem_ref[t, 8 * n : 8 * n + 8].reshape(BWD_TILE, 2 * HEAD)
        scores = dot(memory, qs[i], NT)
        weights = jnp.exp(scores - lse_ref[i])
        if masked:
            weights = jnp.where(admitted(scores.shape, me, n * BWD_TILE), weights, 0.0)
        weight_grad = dot(memory, gs[i], NT)
        score_grad = (weights * (weight_grad - delta_ref[i])).astype(bf16)
        here_grad = dot(weights.astype(bf16), gs[i], NN) + dot(score_grad, qs[i], NN)
        if masked:
            acc[here, :] = here_grad
        else:
            acc[here, :] += here_grad
        dq[i] += dot(kt[:, here], score_grad, NN)

    def step(t, carry):
        for n in range(4):
            rows = mem_ref[t, 4 * n : 4 * n + 4].reshape(512, 2 * HEAD)
            kt[:, 512 * n : 512 * n + 512] = rows.T[:HEAD]
        tile(t, t, 0, True)
        tile(t, t, 1, True)
        grad = dq[t] * (1.0 / math.sqrt(HEAD))
        grad = jnp.concatenate([grad[:, :TOK_DEV], grad[:, TOK_DEV:]], axis=0).T.astype(bf16)
        turned = dot(grad, turn_ref[0], NT)
        grad = grad.astype(f32) * cos_ref[0, t] + turned * sin_ref[0, t]
        pgq_ref[t] = grad.astype(bf16)

        @pl.when(t != seq)
        def _():
            to_token(0, t, seq).start()

        def rest(i, inner):
            tile(t, i, 0, False)
            tile(t, i, 1, False)
            return inner

        lax.fori_loop(t + 1, N_SEQ, rest, 0)
        for n in range(4):
            rows = acc[512 * n : 512 * n + 512, :].astype(bf16)
            stage[t, 4 * n : 4 * n + 4] = rows.reshape(4, TOK_DEV, 2 * HEAD)
        dl[t, me] = stage[t, me]
        for k in range(1, N_SHARD):
            peer = lax.rem(me + k, N_SHARD)
            to_owner(t, k, peer, me, peer).start()
        return carry

    lax.fori_loop(0, N_SEQ, step, 0)

    def gathered(t, carry):
        for k in range(1, N_SHARD):
            source = lax.rem(me + N_SHARD - k, N_SHARD)
            to_owner(t, k, source, source, source).wait_recv()
        grad = jnp.sum(dl[t].astype(f32), axis=0).astype(bf16)
        turned = dot(grad, turn_ref[1], NT)
        grad = grad.astype(f32) * cos_ref[1, t] + turned * sin_ref[1, t]
        pgm_ref[t] = grad.astype(bf16)

        @pl.when(t != seq)
        def _():
            to_token(1, t, seq).start()

        return carry

    lax.fori_loop(0, N_SEQ, gathered, 0)
    mine = pltpu.make_async_copy(pgq_ref.at[seq], tokq_ref.at[seq], own.at[2])
    mine.start()
    other = pltpu.make_async_copy(pgm_ref.at[seq], tokm_ref.at[seq], own.at[3])
    other.start()
    for k in range(1, N_SEQ):
        to_head(k, seq, lax.rem(seq + k, N_SEQ)).wait_send()
    for k in range(1, N_SHARD):
        to_token_expert(k).wait()
    came_own.wait()
    for n in range(6):
        to_ring(n).wait()

    def end(t, carry):
        for k in range(1, N_SHARD):
            peer = lax.rem(me + k, N_SHARD)
            to_owner(t, k, peer, me, peer).wait_send()
        return carry

    lax.fori_loop(0, N_SEQ, end, 0)
    for n in range(2):
        for k in range(1, N_SEQ):
            peer = lax.rem(seq + k, N_SEQ)
            to_token(n, peer, seq).wait_send()
            to_token(n, peer, peer).wait_recv()
    mine.wait()
    other.wait()


def attention_back(
    queries, upstream, wide, lse, memory, cosine, sine, turn, expert_out, parts, ident
):
    dma = pltpu.SemaphoreType.DMA
    vmem = pl.BlockSpec(memory_space=pltpu.VMEM)
    chunk = jax.ShapeDtypeStruct((N_SEQ, TOK_DEV, 2 * HEAD), bf16)
    return pl.pallas_call(
        attention_back_kernel,
        in_specs=[vmem, ANY, vmem, vmem, vmem, vmem, vmem, vmem, ANY] + [ANY] * 6,
        out_specs=[vmem, vmem, ANY, ANY, ANY] + [ANY] * 6,
        out_shape=[chunk] * 4
        + [jax.ShapeDtypeStruct(expert_out.shape, bf16)]
        + [jax.ShapeDtypeStruct(part.shape, bf16) for part in parts],
        scratch_shapes=[
            pltpu.VMEM((N_SEQ, TOK_DEV, 2 * HEAD), bf16),
            pltpu.VMEM((N_SEQ, 2 * TOK_DEV, 2 * HEAD), bf16),
            pltpu.VMEM((N_SEQ, 2 * TOK_DEV, 2 * HEAD), bf16),
            pltpu.VMEM((N_SEQ, 1, 2 * TOK_DEV), f32),
            pltpu.VMEM((HEAD, SUPER), bf16),
            pltpu.VMEM((SUPER, 2 * HEAD), f32),
            pltpu.VMEM((N_SEQ, HEAD, 2 * TOK_DEV), f32),
            pltpu.VMEM((N_SEQ, N_SHARD, TOK_DEV, 2 * HEAD), bf16),
            pltpu.VMEM((N_SEQ, N_SHARD, TOK_DEV, 2 * HEAD), bf16),
            dma((N_SEQ, 15)),
            dma((N_SEQ, 15)),
            dma((N_SEQ - 1,)),
            dma((N_SEQ - 1,)),
            dma((N_SHARD - 1,)),
            dma((N_SHARD - 1,)),
            dma((6,)),
            dma((6,)),
            dma((2, N_SEQ)),
            dma((2, N_SEQ)),
            dma((4,)),
        ],
        compiler_params=pltpu.CompilerParams(
            collective_id=ident, has_side_effects=True, vmem_limit_bytes=56 << 20
        ),
        name="attention_backward",
    )(queries, upstream, wide, lse, memory, cosine, sine, turn, expert_out, *parts)


def expert_kernel(s_ref, x_ref, g_ref, w_ref, out_ref, back_ref, *refs):
    grad_refs, (gu, down, xt, ht, both) = refs[:4], refs[4:]
    gu[...] = w_ref[0, :, :128, :].reshape(WIDTH, 2 * FF)
    down[...] = w_ref[0, :, 128:, :].reshape(FF, WIDTH)

    def rows_step(t, carry):
        rows = pl.ds(pl.multiple_of(t * 128, 128), 128)
        x = x_ref[0, rows, :]
        pre = dot(x, gu[...], NN)
        gate, up = pre[:, :FF], pre[:, FF:]
        sigmoid = jax.nn.sigmoid(gate)
        act = gate * sigmoid
        hidden = (act * up).astype(bf16)
        out_ref[0, rows, :] = dot(hidden, down[...], NN).astype(bf16)
        units = dot(g_ref[0, rows, :], down[...], NT)
        gate_grad = (units * up * sigmoid * (1.0 + gate * (1.0 - sigmoid))).astype(bf16)
        up_grad = (units * act).astype(bf16)
        pair = jnp.concatenate([gate_grad, up_grad], axis=1)
        back_ref[0, rows, :] = dot(pair, gu[...], NT).astype(bf16)
        both[rows, :] = pair
        xt[:, rows] = x.T
        ht[:, rows] = hidden.T
        return carry

    lax.fori_loop(0, EXPERT_ROWS // 128, rows_step, 0)
    far = s_ref[0] % 2
    ring = s_ref[0] // 2
    for k in range(4):

        def grad_step(n, carry, k=k):
            s = (ring + k) % 4 * 2 + (far + n) % 2
            features = pl.ds(pl.multiple_of(s * 128, 128), 128)
            units = pl.ds(pl.multiple_of(s * 64, 64), 64)
            grad_refs[k][n, 0, :128, :] = dot(xt[features, :], both[...], NN).astype(bf16)
            grad_refs[k][n, 0, 128:, :] = dot(ht[units, :], g_ref[0], NN).astype(bf16)
            return carry

        lax.fori_loop(0, 2, grad_step, 0)


def experts(seq, x, g, w):
    rows = pl.BlockSpec((1, EXPERT_ROWS, WIDTH), lambda e, s: (e, 0, 0))
    shape = jax.ShapeDtypeStruct((LOCAL_EXPERTS, EXPERT_ROWS, WIDTH), bf16)
    return pl.pallas_call(
        expert_kernel,
        grid_spec=pltpu.PrefetchScalarGridSpec(
            num_scalar_prefetch=1,
            grid=(LOCAL_EXPERTS,),
            in_specs=[
                rows,
                rows,
                pl.BlockSpec((1, N_SEQ, 192, WIDTH), lambda e, s: (e, 0, 0, 0)),
            ],
            out_specs=[rows, rows]
            + [pl.BlockSpec((2, 1, 192, WIDTH), lambda e, s: (0, e, 0, 0))] * 4,
            scratch_shapes=[
                pltpu.VMEM((WIDTH, 2 * FF), bf16),
                pltpu.VMEM((FF, WIDTH), bf16),
                pltpu.VMEM((WIDTH, EXPERT_ROWS), bf16),
                pltpu.VMEM((FF, EXPERT_ROWS), bf16),
                pltpu.VMEM((EXPERT_ROWS, 2 * FF), bf16),
            ],
        ),
        out_shape=[shape, shape]
        + [jax.ShapeDtypeStruct((2, LOCAL_EXPERTS, 192, WIDTH), bf16)] * 4,
        compiler_params=pltpu.CompilerParams(vmem_limit_bytes=56 << 20),
        cost_estimate=pl.CostEstimate(
            flops=10**8, bytes_accessed=1 << 20, transcendentals=10**5
        ),
        name="experts",
    )(seq, x, g, w)


def group_columns(rows):
    lead = rows.shape[:-1]
    queries = rows[..., : HEADS * HEAD].reshape(lead + (N_SEQ, 2 * HEAD))
    keys = rows[..., HEADS * HEAD : (HEADS + KV) * HEAD].reshape(lead + (N_SEQ, HEAD))
    values = rows[..., (HEADS + KV) * HEAD :].reshape(lead + (N_SEQ, HEAD))
    return jnp.concatenate([queries, keys, values], axis=-1)


def ungroup_columns(groups):
    rows = groups.shape[0]
    return jnp.concatenate(
        [
            groups[:, :, : 2 * HEAD].reshape(rows, HEADS * HEAD),
            groups[:, :, 2 * HEAD : 3 * HEAD].reshape(rows, KV * HEAD),
            groups[:, :, 3 * HEAD :].reshape(rows, KV * HEAD),
        ],
        axis=1,
    )


def rope_pair(shard):
    half = HEAD // 2
    frequency = jnp.exp(
        jnp.arange(half, dtype=f32) * jnp.float32(-2.0 * math.log(rope_base) / HEAD)
    )
    chunk = jnp.arange(N_SEQ, dtype=jnp.int32)[:, None] * N_SHARD + shard
    position = chunk * TOK_DEV + jnp.arange(TOK_DEV, dtype=jnp.int32)[None, :]
    angles = position.reshape(HEAD_ROWS, 1).astype(f32) * frequency[None, :]
    return jnp.tile(jnp.cos(angles), (1, 6)), jnp.tile(jnp.sin(angles), (1, 6))


def turn_matrix():
    row = jnp.arange(3 * HEAD, dtype=jnp.int32)[:, None]
    col = jnp.arange(3 * HEAD, dtype=jnp.int32)[None, :]
    half = HEAD // 2
    low = col % HEAD < half
    minus = low & (row == col + half)
    plus = (~low) & (row == col - half)
    return (plus.astype(f32) - minus.astype(f32)).astype(bf16)


def after(value, *others):
    return lax.optimization_barrier((value,) + others)[0]


def routing(routes, route_weights):
    ids = jnp.arange(EXPERTS, dtype=jnp.int32)
    hit = routes[:, :, None] == ids[None, None, :]
    mask = jnp.sum(hit.astype(f32), axis=1)
    weight = jnp.sum(jnp.where(hit, route_weights[:, :, None], 0.0), axis=1)
    token = jnp.arange(TOK_DEV, dtype=jnp.int32)
    earlier = (token[:, None] > token[None, :]).astype(bf16)
    before = dot(earlier, mask.astype(bf16), NN)
    code = jnp.where(mask > 0.0, before, -1.0).astype(bf16)
    slot = jnp.arange(EXPERTS * CAP, dtype=jnp.int32)
    owner = slot // CAP % N_SHARD * LOCAL_EXPERTS + slot // (CAP * N_SHARD)
    widen = (owner[None, :] == ids[:, None]).astype(bf16)
    pick = dot(code, widen, NN) == (slot % CAP).astype(f32)[None, :]
    high = weight.astype(bf16)
    low = (weight - high.astype(f32)).astype(bf16)
    high = jnp.where(pick, dot(high, widen, NN), 0.0)
    low = jnp.where(pick, dot(low, widen, NN), 0.0)
    return pick.astype(bf16), high.astype(bf16), low.astype(bf16), jnp.sum(high + low, axis=0)


def on_device(
    layer_input,
    attn_gain,
    moe_gain,
    w_qkv,
    w_out,
    w_gate,
    w_up,
    w_down,
    routes,
    route_weights,
    cotangent,
):
    seq = lax.axis_index("seq")
    shard = lax.axis_index("shard")
    seq_array = seq.astype(jnp.int32).reshape(1)
    along_x = [(s, s + 1 - 2 * (s % 2)) for s in range(N_SEQ)]

    grouped = group_columns(w_qkv)
    pieces = grouped.reshape(8, N_SEQ, 2, 128).transpose(1, 2, 0, 3)
    gains = jnp.concatenate([attn_gain, moe_gain, jnp.zeros((112,), bf16)])
    gains = jnp.broadcast_to(gains[None, None, :], (N_SEQ, 16, 128))
    pieces = jnp.concatenate([pieces.reshape(N_SEQ, 16, 128), gains], axis=1)
    out_rows = w_out.reshape(8, 8, 128).transpose(1, 0, 2).reshape(2, 32, 128)
    tokens, columns, out_slabs = first_gather(
        layer_input.reshape(8, TOK_DEV // 8, WIDTH), pieces, out_rows, 1
    )
    out_slabs = out_slabs.reshape(2, N_SHARD, 8, 8, 128).transpose(0, 1, 3, 2, 4)
    out_slabs = out_slabs.reshape(2 * N_SHARD * 8, WIDTH)
    expert_pack = jnp.concatenate(
        [jnp.concatenate([w_gate, w_up], axis=2), w_down], axis=1
    )
    expert_weights = lax.all_gather(after(expert_pack, tokens), "seq", axis=1)
    gain_rows = columns[:, N_SEQ, :8, :16].transpose(1, 0, 2)
    gain_attn = gain_rows[:, :, :8].reshape(WIDTH).astype(f32)
    gain_moe = gain_rows[:, :, 8:].reshape(WIDTH).astype(f32)
    columns = columns[:, :N_SEQ].reshape(N_SHARD, N_SEQ, 2, 8, 128)
    columns = columns.transpose(1, 0, 3, 2, 4).reshape(WIDTH, COLS)

    wide = tokens.reshape(HEAD_ROWS, WIDTH).astype(f32)
    inverse = lax.rsqrt(jnp.mean(wide * wide, axis=1, keepdims=True) + epsilon)
    normed = (wide * inverse * gain_attn).astype(bf16)
    cosine, sine = rope_pair(shard)
    turn = turn_matrix()
    turned = dot(columns[:, : 3 * HEAD], turn, NN).astype(bf16)
    projected = dot(normed, jnp.concatenate([columns, turned], axis=1), NN)
    rotated = projected[:, : 3 * HEAD] * cosine + projected[:, COLS:] * sine
    queries = rotated[:, : 2 * HEAD].astype(bf16) * jnp.bfloat16(1.0 / math.sqrt(HEAD))
    queries = queries.reshape(N_SEQ, TOK_DEV, 2 * HEAD)
    memory = jnp.concatenate(
        [rotated[:, 2 * HEAD :], projected[:, 3 * HEAD : COLS]], axis=1
    ).astype(bf16)
    memory = memory.reshape(N_SEQ, TOK_DEV, 2 * HEAD)

    pick, scale_high, scale_low, slot_scale = routing(routes, route_weights)
    out_grad = cotangent.astype(f32)
    slots = (LOCAL_EXPERTS, N_SHARD, CAP, WIDTH)
    grad_send = (slot_scale[:, None] * dot(pick, cotangent, TN)).astype(bf16).reshape(slots)
    qkv_rows = jnp.broadcast_to(grouped.reshape(1, 16, WIDTH), (N_SHARD, 16, WIDTH))
    grad_send = jnp.concatenate([grad_send[0], grad_send[1], qkv_rows], axis=1)
    attended_wide, lse, attended_full, memory, grad_rows, out_slabs = attention(
        queries, memory, grad_send, out_slabs, 2
    )
    qkv_rows = grad_rows[:, 2 * CAP :].reshape(N_SHARD * 8, 2 * WIDTH)
    grad_rows = jnp.stack([grad_rows[:, :CAP], grad_rows[:, CAP : 2 * CAP]])
    grad_rows = grad_rows.reshape(LOCAL_EXPERTS, EXPERT_ROWS, WIDTH)

    order = jnp.stack(
        [(seq // 2 + 4 - k) % 4 * 2 + half for k in range(4) for half in range(2)]
    )
    attended_full = attended_full[order].transpose(1, 0, 2).reshape(TOK_DEV, WIDTH)
    x_wide = layer_input.astype(f32)
    out_weight = out_slabs.reshape(WIDTH, WIDTH)
    residual = x_wide + dot(attended_full, out_weight, NN)
    inverse_two = lax.rsqrt(jnp.mean(residual * residual, axis=1, keepdims=True) + epsilon)
    normed_moe = (residual * inverse_two * gain_moe).astype(bf16)

    send_rows = dot(pick, normed_moe, TN).astype(bf16).reshape(slots)
    expert_rows = exchange(send_rows, "shard", N_SHARD, 4, dim=1)
    expert_rows = expert_rows.reshape(LOCAL_EXPERTS, EXPERT_ROWS, WIDTH)
    expert_out, rows_grad, *expert_grads = experts(
        seq_array, expert_rows, grad_rows, expert_weights
    )
    returned = exchange(rows_grad.reshape(slots), "shard", N_SHARD, 5, dim=1)
    qkv_all = lax.all_gather(qkv_rows, "seq", axis=0, tiled=True)

    moe_in_grad = dot(pick, returned.reshape(EXPERTS * CAP, WIDTH), NN)
    scaled = moe_in_grad * gain_moe
    moe_part = inverse_two * scaled - residual * inverse_two**3 * jnp.mean(
        residual * scaled, axis=1, keepdims=True
    )
    residual_grad = out_grad + moe_part
    branch_grad = residual_grad.astype(bf16)
    attended_grad = dot(branch_grad, out_weight, NT).astype(bf16)
    attended_grad = attended_grad.reshape(TOK_DEV, N_SEQ, 2 * HEAD).transpose(1, 0, 2)
    back_order = jnp.stack(
        [(seq // 2 + 4 - z) % 4 * 2 + half for z in range(4) for half in range(2)]
    )
    attended_grad = attended_grad[back_order]

    out_parts = []
    for k in range(4):
        back = (4 - k) % 4 * COLS
        block = dot(attended_full[:, back : back + COLS], branch_grad, TN)
        out_parts.append(block.astype(bf16))
    tables = [
        (cosine[:, : 2 * HEAD], sine[:, : 2 * HEAD]),
        (
            jnp.concatenate([cosine[:, :HEAD], jnp.ones((HEAD_ROWS, HEAD), f32)], axis=1),
            jnp.concatenate([sine[:, :HEAD], jnp.zeros((HEAD_ROWS, HEAD), f32)], axis=1),
        ),
    ]
    tables = [
        jnp.stack(table).reshape(2, N_SEQ, TOK_DEV, 2 * HEAD) for table in zip(*tables)
    ]
    left = jnp.arange(2 * HEAD, dtype=jnp.int32) < HEAD
    turns = turn[: 2 * HEAD, : 2 * HEAD]
    turns = jnp.stack([turns, jnp.where(left[:, None] & left[None, :], turns, 0)])
    query_grad, memory_grad, token_query, token_memory, came_back, *sent = attention_back(
        queries,
        attended_grad,
        attended_wide,
        lse,
        memory,
        *tables,
        turns,
        expert_out.reshape(slots),
        expert_grads[1:] + out_parts[1:],
        6,
    )
    came_back = came_back.reshape(EXPERTS * CAP, WIDTH)
    expert_sums = sum(grad.astype(f32) for grad in [expert_grads[0]] + sent[:3])
    out_sums = sum(grad.astype(f32) for grad in [out_parts[0]] + sent[3:])
    out_sums = out_sums.reshape(2, 2 * HEAD, WIDTH)
    far = seq % 2
    out_mine = lax.dynamic_index_in_dim(out_sums, far, 0, keepdims=False)
    out_other = lax.dynamic_index_in_dim(out_sums, 1 - far, 0, keepdims=False)
    other = jnp.concatenate(
        [expert_sums[1].reshape(LOCAL_EXPERTS * 192, WIDTH), out_other], axis=0
    ).astype(bf16)
    other = lax.ppermute(other, "seq", along_x).astype(f32)
    expert_sums = expert_sums[0] + other[: LOCAL_EXPERTS * 192].reshape(
        LOCAL_EXPERTS, 192, WIDTH
    )
    out_part = out_mine + other[LOCAL_EXPERTS * 192 :]
    moe_sum = dot(scale_high, came_back, NN) + dot(scale_low, came_back, NN)
    block_out = (residual + moe_sum).astype(bf16)

    projected_grad = jnp.concatenate(
        [query_grad.reshape(HEAD_ROWS, 2 * HEAD), memory_grad.reshape(HEAD_ROWS, 2 * HEAD)], axis=1
    )

    qkv_part = dot(normed, projected_grad, TN)
    qkv_part = qkv_part.reshape(N_SEQ, N_SHARD, 8, COLS).transpose(1, 0, 2, 3)
    out_part = out_part.reshape(N_SHARD, 8, WIDTH)
    pack = expert_pack.astype(f32)
    moe_gain_part = jnp.sum(
        pack[:, :128] * expert_sums[:, :128], axis=(0, 2)
    ) / lax.dynamic_slice_in_dim(gain_moe, seq * 128, 128)
    moe_gain_part = moe_gain_part.reshape(N_SHARD, 1, 8)
    moe_gain_high = moe_gain_part.astype(bf16)
    moe_gain_low = (moe_gain_part - moe_gain_high.astype(f32)).astype(bf16)
    gain_part = jnp.concatenate([moe_gain_high, moe_gain_low], axis=1)
    gain_part = jnp.pad(gain_part, ((0, 0), (0, 14), (0, COLS - 8)))
    sums = jnp.concatenate(
        [
            qkv_part.reshape(N_SHARD, 64, COLS).astype(bf16),
            out_part.reshape(N_SHARD, 32, COLS).astype(bf16),
            gain_part,
        ],
        axis=1,
    )
    sums = jnp.sum(exchange(sums, "shard", N_SHARD, 7).astype(f32), axis=0)
    out_weight_grad = sums[64:96].reshape(8, WIDTH)
    moe_gain_grad = sums[96, :8] + sums[97, :8]
    qkv_groups = lax.all_to_all(sums[:64].reshape(N_SEQ, 8, COLS), "seq", 0, 0)
    qkv_groups = qkv_groups.transpose(1, 0, 2)
    attn_gain_grad = jnp.sum(grouped.astype(f32) * qkv_groups, axis=(1, 2)) / attn_gain.astype(f32)
    qkv_weight_grad = ungroup_columns(qkv_groups)

    token_grad = jnp.concatenate([token_query, token_memory], axis=2)
    token_grad = token_grad.transpose(1, 0, 2).reshape(TOK_DEV, N_SEQ * COLS)
    normed_grad = dot(token_grad, qkv_all, NT)
    inverse_one = lax.rsqrt(jnp.mean(x_wide * x_wide, axis=1, keepdims=True) + epsilon)
    scaled = normed_grad * gain_attn
    attn_part = inverse_one * scaled - x_wide * inverse_one**3 * jnp.mean(
        x_wide * scaled, axis=1, keepdims=True
    )
    input_grad = (residual_grad + attn_part).astype(bf16)
    return (
        block_out,
        input_grad,
        attn_gain_grad,
        moe_gain_grad,
        qkv_weight_grad,
        out_weight_grad,
        expert_sums[:, :128, :FF],
        expert_sums[:, :128, FF:],
        expert_sums[:, 128:],
    )


def solution(mesh):
    token = P(("seq", "shard"), None)
    vector = P(("seq", "shard"))
    expert = P("shard", "seq", None)
    return jax.shard_map(
        on_device,
        mesh=mesh,
        in_specs=(
            token,
            vector,
            vector,
            token,
            token,
            expert,
            expert,
            expert,
            token,
            token,
            token,
        ),
        out_specs=(token, token, vector, vector, token, token, expert, expert, expert),
        check_vma=False,
    )
```

```python
import functools
import math

import jax
import jax.numpy as jnp
from jax import lax
from jax.experimental import pallas as pl
from jax.experimental.pallas import tpu as pltpu
from jax.sharding import PartitionSpec as P

HEADS = 16
KV = 8
HEAD = 64
EXPERTS = 32
TOPK = 8
TOK_DEV = 128
CAP = 40
WIDTH = 1024
FF = 512
N_SEQ = 8
N_SHARD = 16
HEAD_ROWS = TOK_DEV * N_SEQ
TOKENS = TOK_DEV * N_SEQ * N_SHARD
LOCAL_EXPERTS = EXPERTS // N_SHARD
EXPERT_ROWS = N_SHARD * CAP
COLS = 256
SUPER = TOK_DEV * N_SHARD
BWD_TILE = 1024

epsilon = 1e-06
rope_base = 10000.0

f32 = jnp.float32
bf16 = jnp.bfloat16
MESH = pl.DeviceIdType.MESH
ANY = pl.BlockSpec(memory_space=pl.ANY)
NT = (((1,), (1,)), ((), ()))
NN = (((1,), (0,)), ((), ()))
TN = (((0,), (0,)), ((), ()))


def dot(left, right, dims):
    return lax.dot_general(left, right, dims, preferred_element_type=f32)


def greet(peers):
    barrier = pltpu.get_barrier_semaphore()
    for axis, peer in peers:
        pl.semaphore_signal(barrier, inc=1, device_id={axis: peer}, device_id_type=MESH)
    pl.semaphore_wait(barrier, len(peers))


def remote(source, target, send, recv, axis, peer):
    copy = pltpu.make_async_remote_copy(
        src_ref=source,
        dst_ref=target,
        send_sem=send,
        recv_sem=recv,
        device_id={axis: peer},
        device_id_type=MESH,
    )
    copy.start()
    return copy


def exchange_kernel(axis, count, dim, x_ref, o_ref, send, recv, own):
    def block(ref, index):
        return ref.at[:, index] if dim == 1 else ref.at[index]

    me = lax.axis_index(axis)
    greet([(axis, lax.rem(me + k, count)) for k in range(1, count)])
    mine = pltpu.make_async_copy(block(x_ref, me), block(o_ref, me), own)
    mine.start()
    copies = []
    for k in range(1, count):
        peer = lax.rem(me + k, count)
        copies.append(
            remote(block(x_ref, peer), block(o_ref, me), send.at[k - 1], recv.at[k - 1], axis, peer)
        )
    mine.wait()
    for copy in copies:
        copy.wait()


def exchange(x, axis, count, ident, dim=0):
    return pl.pallas_call(
        functools.partial(exchange_kernel, axis, count, dim),
        out_shape=jax.ShapeDtypeStruct(x.shape, x.dtype),
        in_specs=[ANY],
        out_specs=ANY,
        scratch_shapes=[
            pltpu.SemaphoreType.DMA((count - 1,)),
            pltpu.SemaphoreType.DMA((count - 1,)),
            pltpu.SemaphoreType.DMA,
        ],
        compiler_params=pltpu.CompilerParams(collective_id=ident, has_side_effects=True),
        name="exchange_" + axis,
    )(x)


def staged(axis, units, share, x_ref, place, sem_send, sem_recv, own):
    me = lax.axis_index(axis)
    cores = 2 if axis == "shard" else 1
    core = lax.rem(me, cores)
    pair = lax.rem(me // cores, 2)
    ring = me // (2 * cores)

    def at(r, p, c):
        return (r * 2 + p) * cores + c

    ring_peer = [at(lax.rem(ring + k, 4), pair, core) for k in (1, 2, 3)]
    ring_from = [lax.rem(ring + 4 - k, 4) for k in (1, 2, 3)]
    pair_peer = at(ring, 1 - pair, core)
    core_peer = at(ring, pair, 1 - core)
    mine = pltpu.make_async_copy(x_ref, place(me, 0, units), own)
    mine.start()
    sends = []

    def go(source, index, low, high, peer):
        n = len(sends)
        sends.append(
            remote(source, place(index, low, high), sem_send.at[n], sem_recv.at[n], axis, peer)
        )
        return sends[-1]

    to_pair = go(x_ref, me, 0, units, pair_peer)
    to_ring = [go(x_ref, me, 0, units, peer) for peer in ring_peer]
    landed = []
    if cores == 2:
        landed.append(go(x_ref, me, 0, units, core_peer))

    def pass_core(index, low, high):
        if cores == 2:
            landed.append(go(place(index, low, high), index, low, high, core_peer))

    to_pair.wait_recv()
    fwd_ring = [
        go(place(pair_peer, 0, share), pair_peer, 0, share, peer) for peer in ring_peer
    ]
    pass_core(pair_peer, 0, units)
    fwd_pair = []
    for k in (0, 2, 1):
        to_ring[k].wait_recv()
        source = at(ring_from[k], pair, core)
        if share < units:
            fwd_pair.append((k, go(place(source, share, units), source, share, units, pair_peer)))
        pass_core(source, 0, units)
    for k in (0, 2, 1):
        fwd_ring[k].wait_recv()
        pass_core(at(ring_from[k], 1 - pair, core), 0, share)
    for k, copy in fwd_pair:
        copy.wait_recv()
        pass_core(at(ring_from[k], 1 - pair, core), share, units)
    for copy in landed:
        copy.wait_recv()
    mine.wait()
    for copy in sends:
        copy.wait_send()


def first_kernel(
    x_ref, w_ref, v_ref, xo_ref, wo_ref, vo_ref, w_mid, w_pack, send, recv, own, wsend, wrecv, wown, vown
):
    seq = lax.axis_index("seq")
    shard = lax.axis_index("shard")
    far = lax.rem(seq, 2)
    partner = seq + 1 - 2 * far
    greet(
        [("seq", lax.rem(seq + k, N_SEQ)) for k in range(1, N_SEQ)]
        + [("shard", lax.rem(shard + k, N_SHARD)) for k in range(1, N_SHARD)]
    )
    mine = pltpu.make_async_copy(w_ref.at[seq], w_mid.at[seq], wown)
    mine.start()
    slab = pltpu.make_async_copy(v_ref, vo_ref.at[far, shard], vown)
    slab.start()
    pieces = []
    for k in range(1, N_SEQ):
        peer = lax.rem(seq + k, N_SEQ)
        pieces.append(
            remote(w_ref.at[peer], w_mid.at[seq], wsend.at[k - 1], wrecv.at[k - 1], "seq", peer)
        )
    rows = []
    for k in range(1, N_SHARD):
        peer = lax.rem(shard + k, N_SHARD)
        n = 21 + k
        rows.append(
            remote(v_ref, vo_ref.at[far, shard], wsend.at[n], wrecv.at[n], "shard", peer)
        )
    mine.wait()
    for piece in pieces:
        piece.wait()
    packed = jnp.zeros((16, 128), f32)
    row = lax.broadcasted_iota(jnp.int32, (16, 128), 0)
    for s in range(N_SEQ):
        packed = jnp.where(row == s, w_mid[s, 16:].astype(f32), packed)
        w_pack[s] = w_mid[s, :16]
    w_pack[N_SEQ] = packed.astype(bf16)
    mine = pltpu.make_async_copy(w_pack, wo_ref.at[shard], wown)
    mine.start()
    pieces = []
    for k in range(1, N_SHARD):
        peer = lax.rem(shard + k, N_SHARD)
        n = 6 + k
        pieces.append(
            remote(w_pack, wo_ref.at[shard], wsend.at[n], wrecv.at[n], "shard", peer)
        )
    staged("seq", 8, 8, x_ref, lambda s, low, high: xo_ref.at[s, low:high], send, recv, own)
    slab.wait()
    for row in rows:
        row.wait()
    pair = remote(vo_ref.at[far], vo_ref.at[far], wsend.at[37], wrecv.at[37], "seq", partner)
    mine.wait()
    for piece in pieces:
        piece.wait()
    pair.wait()


def first_gather(x, pieces, rows, ident):
    return pl.pallas_call(
        first_kernel,
        out_shape=[
            jax.ShapeDtypeStruct((N_SEQ, 8, TOK_DEV // 8, WIDTH), bf16),
            jax.ShapeDtypeStruct((N_SHARD, N_SEQ + 1, 16, 128), bf16),
            jax.ShapeDtypeStruct((2, N_SHARD) + rows.shape, bf16),
        ],
        in_specs=[ANY, ANY, ANY],
        out_specs=[ANY, ANY, ANY],
        scratch_shapes=[
            pltpu.VMEM(pieces.shape, bf16),
            pltpu.VMEM((N_SEQ + 1, 16, 128), bf16),
            pltpu.SemaphoreType.DMA((12,)),
            pltpu.SemaphoreType.DMA((12,)),
            pltpu.SemaphoreType.DMA,
            pltpu.SemaphoreType.DMA((38,)),
            pltpu.SemaphoreType.DMA((38,)),
            pltpu.SemaphoreType.DMA,
            pltpu.SemaphoreType.DMA,
        ],
        compiler_params=pltpu.CompilerParams(collective_id=ident, has_side_effects=True),
        name="gather_tokens",
    )(x, pieces, rows)


def spread(rows, right):
    zeros = jnp.zeros((TOK_DEV, HEAD), rows.dtype)
    parts = [rows[:, :HEAD], rows[:, HEAD:]]
    if right:
        parts = [jnp.concatenate([zeros, part], axis=1) for part in parts]
    else:
        parts = [jnp.concatenate([part, zeros], axis=1) for part in parts]
    return jnp.concatenate(parts, axis=0)


def admitted(shape, j, first_key):
    key_pos = first_key + lax.broadcasted_iota(jnp.int32, shape, 0)
    query_pos = j * TOK_DEV + (lax.broadcasted_iota(jnp.int32, shape, 1) & (TOK_DEV - 1))
    return query_pos >= key_pos


def transfer(source, target, send, recv, axis, peer):
    return pltpu.make_async_remote_copy(
        src_ref=source,
        dst_ref=target,
        send_sem=send,
        recv_sem=recv,
        device_id={axis: peer},
        device_id_type=MESH,
    )


def everyone(seq, shard):
    return [("seq", lax.rem(seq + k, N_SEQ)) for k in range(1, N_SEQ)] + [
        ("shard", lax.rem(shard + k, N_SHARD)) for k in range(1, N_SHARD)
    ]


def attention_kernel(
    q_ref,
    kv_ref,
    cot_ref,
    qkv_ref,
    slab_ref,
    wide_ref,
    lse_ref,
    att_ref,
    mem_ref,
    cot_out,
    qkv_out,
    slab_out,
    land,
    vt,
    heads,
    peak_ref,
    total_ref,
    acc_ref,
    ksend,
    krecv,
    gsend,
    grecv,
    esend,
    erecv,
    vsend,
    vrecv,
    fsend,
    frecv,
    own,
    msem,
):
    seq = lax.axis_index("seq")
    me = lax.axis_index("shard")
    core = lax.rem(me, 2)
    pair = lax.rem(me // 2, 2)
    ring = me // 4

    def at(k, other_pair, other_core):
        p = 1 - pair if other_pair else pair
        c = 1 - core if other_core else core
        return (lax.rem(ring + 4 + k, 4) * 2 + p) * 2 + c

    def message(t, m, block, peer):
        return transfer(
            land.at[t, block], land.at[t, block], ksend.at[t, m], krecv.at[t, m], "shard", peer
        )

    def first(t):
        for k in (1, 2, 3):
            message(t, k - 1, me, at(k, 0, 0)).start()
        message(t, 3, me, at(0, 1, 0)).start()
        message(t, 4, me, at(0, 0, 1)).start()

    def second(t):
        block = at(0, 1, 0)
        message(t, 3, block, block).wait_recv()
        for k in (1, 2, 3):
            message(t, 4 + k, block, at(k, 0, 0)).start()
        message(t, 8, block, at(0, 0, 1)).start()
        for k in (1, 2, 3):
            block = at(-k, 0, 0)
            message(t, k - 1, block, block).wait_recv()
            message(t, 8 + k, block, at(0, 0, 1)).start()

    def third(t):
        for k in (1, 2, 3):
            block = at(-k, 1, 0)
            message(t, 4 + k, block, at(-k, 0, 0)).wait_recv()
            message(t, 11 + k, block, at(0, 0, 1)).start()

    def fourth(t):
        peer = at(0, 0, 1)
        message(t, 4, peer, peer).wait_recv()
        message(t, 8, at(0, 1, 1), peer).wait_recv()
        for k in (1, 2, 3):
            message(t, 8 + k, at(-k, 0, 1), peer).wait_recv()
            message(t, 11 + k, at(-k, 1, 1), peer).wait_recv()

    def to_expert(k):
        peer = lax.rem(me + k, N_SHARD)
        return transfer(
            cot_ref.at[peer], cot_out.at[me], esend.at[k - 1], erecv.at[k - 1], "shard", peer
        )

    def to_shard(k):
        peer = lax.rem(me + k, N_SHARD)
        return transfer(
            qkv_ref, qkv_out.at[me], vsend.at[k - 1], vrecv.at[k - 1], "shard", peer
        )

    def to_ring(k):
        peer = lax.rem(seq + 2 * k, N_SEQ)
        return transfer(slab_ref, slab_out.at[k], fsend.at[k - 1], frecv.at[k - 1], "seq", peer)

    def to_token(t, source):
        return transfer(
            heads.at[t], att_ref.at[source], gsend.at[t], grecv.at[source], "seq", t
        )

    greet(everyone(seq, me))

    def begin(t, carry):
        land[t, me] = kv_ref[t]
        first(t)
        peak_ref[t] = jnp.full((1, 2 * TOK_DEV), -1e30, f32)
        total_ref[t] = jnp.zeros((1, 2 * TOK_DEV), f32)
        acc_ref[t] = jnp.zeros((HEAD, 2 * TOK_DEV), f32)
        return carry

    lax.fori_loop(0, N_SEQ, begin, 0)
    second(0)
    third(0)
    second(1)
    fourth(0)
    for k in range(1, N_SHARD):
        to_expert(k).start()
        to_shard(k).start()
    for k in (1, 2, 3):
        to_ring(k).start()
    qkv_own = pltpu.make_async_copy(qkv_ref, qkv_out.at[me], own.at[3])
    qkv_own.start()
    cot_own = pltpu.make_async_copy(cot_ref.at[me], cot_out.at[me], own.at[0])
    cot_own.start()
    slab_own = pltpu.make_async_copy(slab_ref, slab_out.at[0], own.at[1])
    slab_own.start()

    def tile(t, i, masked):
        queries = spread(q_ref[i], False)
        scores = dot(land[t].reshape(SUPER, 2 * HEAD), queries, NT)
        if masked:
            scores = jnp.where(admitted(scores.shape, me, 0), scores, -1e30)
        peak = peak_ref[i]
        newest = jnp.maximum(peak, jnp.max(scores, axis=0, keepdims=True))
        weights = jnp.exp(scores - newest)
        shrink = jnp.exp(peak - newest)
        total = total_ref[i] * shrink + jnp.sum(weights, axis=0, keepdims=True)
        acc = acc_ref[i] * shrink + dot(vt[...], weights.astype(bf16), NN)
        return newest, total, acc

    def step(t, carry):
        pltpu.make_async_copy(land.at[t], mem_ref.at[t], msem.at[t]).start()

        @pl.when(t + 1 < N_SEQ)
        def _():
            third(t + 1)

        @pl.when(t + 2 < N_SEQ)
        def _():
            second(t + 2)

        for n in range(4):
            rows = land[t, 4 * n : 4 * n + 4].reshape(512, 2 * HEAD)
            vt[:, 512 * n : 512 * n + 512] = rows.T[HEAD:]
        newest, total, acc = tile(t, t, True)
        acc = acc / total
        stacked = jnp.concatenate([acc[:, :TOK_DEV], acc[:, TOK_DEV:]], axis=0)
        wide_ref[t] = stacked
        heads[t] = stacked.T.astype(bf16)
        lse_ref[t] = newest + jnp.log(total)

        @pl.when(t != seq)
        def _():
            to_token(t, seq).start()

        def rest(i, inner):
            peak_ref[i], total_ref[i], acc_ref[i] = tile(t, i, False)
            return inner

        lax.fori_loop(t + 1, N_SEQ, rest, 0)

        @pl.when(t + 1 < N_SEQ)
        def _():
            fourth(t + 1)

        return carry

    lax.fori_loop(0, N_SEQ, step, 0)
    mine = pltpu.make_async_copy(heads.at[seq], att_ref.at[seq], own.at[2])
    mine.start()
    for k in range(1, N_SEQ):
        to_token(lax.rem(seq + k, N_SEQ), seq).wait_send()
        source = lax.rem(seq + k, N_SEQ)
        to_token(source, source).wait_recv()
    mine.wait()
    cot_own.wait()
    qkv_own.wait()
    slab_own.wait()
    for k in range(1, N_SHARD):
        to_expert(k).wait()
        to_shard(k).wait()
    for k in (1, 2, 3):
        to_ring(k).wait()

    def end(t, carry):
        for m in range(15):
            message(t, m, me, me).wait_send()
        pltpu.make_async_copy(land.at[t], mem_ref.at[t], msem.at[t]).wait()
        return carry

    lax.fori_loop(0, N_SEQ, end, 0)


def attention(queries, memory, cot_rows, qkv_rows, slab, ident):
    dma = pltpu.SemaphoreType.DMA
    vmem = pl.BlockSpec(memory_space=pltpu.VMEM)
    return pl.pallas_call(
        attention_kernel,
        in_specs=[vmem, vmem, ANY, ANY, ANY],
        out_specs=[vmem, vmem, ANY, ANY, ANY, ANY, ANY],
        out_shape=[
            jax.ShapeDtypeStruct((N_SEQ, 2 * HEAD, TOK_DEV), f32),
            jax.ShapeDtypeStruct((N_SEQ, 1, 2 * TOK_DEV), f32),
            jax.ShapeDtypeStruct((N_SEQ, TOK_DEV, 2 * HEAD), bf16),
            jax.ShapeDtypeStruct((N_SEQ, N_SHARD, TOK_DEV, 2 * HEAD), bf16),
            jax.ShapeDtypeStruct(cot_rows.shape, bf16),
            jax.ShapeDtypeStruct((N_SHARD,) + qkv_rows.shape, bf16),
            jax.ShapeDtypeStruct((4,) + slab.shape, bf16),
        ],
        scratch_shapes=[
            pltpu.VMEM((N_SEQ, N_SHARD, TOK_DEV, 2 * HEAD), bf16),
            pltpu.VMEM((HEAD, SUPER), bf16),
            pltpu.VMEM((N_SEQ, TOK_DEV, 2 * HEAD), bf16),
            pltpu.VMEM((N_SEQ, 1, 2 * TOK_DEV), f32),
            pltpu.VMEM((N_SEQ, 1, 2 * TOK_DEV), f32),
            pltpu.VMEM((N_SEQ, HEAD, 2 * TOK_DEV), f32),
            dma((N_SEQ, 15)),
            dma((N_SEQ, 15)),
            dma((N_SEQ,)),
            dma((N_SEQ,)),
            dma((N_SHARD - 1,)),
            dma((N_SHARD - 1,)),
            dma((N_SHARD - 1,)),
            dma((N_SHARD - 1,)),
            dma((3,)),
            dma((3,)),
            dma((4,)),
            dma((N_SEQ,)),
        ],
        compiler_params=pltpu.CompilerParams(
            collective_id=ident, has_side_effects=True, vmem_limit_bytes=48 << 20
        ),
        name="attention_forward",
    )(queries, memory, cot_rows, qkv_rows, slab)


def late_kernel(*refs):
    (att_ref, ow_ref, x_ref, cot_ref, gain_ref, pick_ref, pickt_ref, gr_ref, w_ref) = refs[:9]
    (q_ref, wide_ref, lse_ref, mem_ref, cos_ref, sin_ref, turn_ref) = refs[9:16]
    (res_ref, resg_ref, pgq_ref, pgm_ref, tokq_ref, tokm_ref, came_ref) = refs[16:23]
    (dw_ref, kz_ref, po_ref, oz_ref) = refs[23:27]
    (gu, dn, land, rows, returned, xt, ht, hg, gm, mixed, dw, attp, ags, po) = refs[27:41]
    (gl, qs, gs, delta_ref, kt, acc, dq, stage, dl) = refs[41:50]
    (wsem, hsend, hrecv, isend, irecv, ksend, krecv, psend, precv) = refs[50:59]
    (dsend, drecv, osend, orecv, jsend, jrecv, nsend, nrecv, own) = refs[59:]
    seq = lax.axis_index("seq")
    me = lax.axis_index("shard")
    ring = seq // 2
    far = lax.rem(seq, 2)

    def weights(e, s):
        return (
            pltpu.make_async_copy(
                w_ref.at[e, s, :128], gu.at[e, 128 * s : 128 * s + 128], wsem.at[e, s, 0]
            ),
            pltpu.make_async_copy(
                w_ref.at[e, s, 128:], dn.at[e, 64 * s : 64 * s + 64], wsem.at[e, s, 1]
            ),
        )

    pieces = ((0, 48), (48, 80))

    def to_expert(part, k, block, source, peer):
        low, high = pieces[part]
        return transfer(
            rows.at[block, low:high],
            land.at[source, low:high],
            hsend.at[part, k - 1],
            hrecv.at[part, k - 1],
            "shard",
            peer,
        )

    back_pieces = ((0, 32), (32, 80))

    def to_source(part, k, block, source, peer):
        low, high = back_pieces[part]
        return transfer(
            rows.at[block, low:high],
            returned.at[source, low:high],
            isend.at[part, k - 1],
            irecv.at[part, k - 1],
            "shard",
            peer,
        )

    def to_token_expert(k):
        peer = lax.rem(me + k, N_SHARD)
        return transfer(
            land.at[peer], came_ref.at[me], jsend.at[k - 1], jrecv.at[k - 1], "shard", peer
        )

    def to_ring(e, k):
        peer = lax.rem(seq + 2 * k, N_SEQ)
        return transfer(
            dw.at[e, k], kz_ref.at[k - 1, e], ksend.at[e, k - 1], krecv.at[e, k - 1], "seq", peer
        )

    def out_to_ring(k):
        peer = lax.rem(seq + 2 * k, N_SEQ)
        return transfer(
            po.at[k], oz_ref.at[k - 1], psend.at[k - 1], precv.at[k - 1], "seq", peer
        )

    def head_of(p):
        return lax.rem(ring + 4 - p // 2, 4) * 2 + p % 2

    def to_head(p):
        return transfer(
            ags.at[p], gl.at[seq], osend.at[p], orecv.at[seq], "seq", head_of(p)
        )

    def from_head(source):
        return transfer(gl.at[source], gl.at[source], osend.at[0], orecv.at[source], "seq", source)

    def to_owner(t, k, block, source, peer):
        return transfer(
            stage.at[t, block],
            dl.at[t, source],
            dsend.at[t, k - 1],
            drecv.at[t, k - 1],
            "shard",
            peer,
        )

    def to_token(n, t, source):
        ref, out = ((pgq_ref, tokq_ref), (pgm_ref, tokm_ref))[n]
        return transfer(
            ref.at[t], out.at[source], nsend.at[n, t], nrecv.at[n, source], "seq", t
        )

    greet(everyone(seq, me))
    for e in range(LOCAL_EXPERTS):
        for s in range(N_SEQ):
            for copy in weights(e, s):
                copy.start()

    for p in range(N_SEQ):
        attp[:, 128 * p : 128 * p + 128] = att_ref[head_of(p)]
    residual = x_ref[...].astype(f32) + dot(attp[...], ow_ref[...], NN)
    res_ref[...] = residual
    inverse = lax.rsqrt(jnp.mean(residual * residual, axis=1, keepdims=True) + epsilon)
    normed = (residual * inverse * gain_ref[...]).astype(bf16)

    for k in range(N_SHARD):
        peer = lax.rem(me + k, N_SHARD)
        here = pl.ds(pl.multiple_of(peer * 80, 16), 80)
        block = dot(pickt_ref[here, :], normed, NN).astype(bf16)
        rows[peer] = block
        if k:
            to_expert(0, k, peer, me, peer).start()
        else:
            land[me] = block
    for k in range(1, N_SHARD):
        peer = lax.rem(me + k, N_SHARD)
        to_expert(1, k, peer, me, peer).start()

    def split(block, e):
        return (
            block.astype(f32)
            .reshape(N_SHARD, LOCAL_EXPERTS, 8, WIDTH)[:, e]
            .reshape(128, WIDTH)
            .astype(bf16)
        )

    def join(first, second):
        halves = [half.astype(f32).reshape(N_SHARD, 1, 8, WIDTH) for half in (first, second)]
        return jnp.concatenate(halves, axis=1).reshape(N_SHARD, 16, WIDTH).astype(bf16)

    def expert(e, x, g, here):
        pre = dot(x, gu[e], NN)
        gate, up = pre[:, :FF], pre[:, FF:]
        sigmoid = jax.nn.sigmoid(gate)
        act = gate * sigmoid
        hidden = (act * up).astype(bf16)
        units = dot(g, dn[e], NT)
        gate_grad = (units * up * sigmoid * (1.0 + gate * (1.0 - sigmoid))).astype(bf16)
        up_grad = (units * act).astype(bf16)
        both = jnp.concatenate([gate_grad, up_grad], axis=1)
        hg[e, here, :] = both
        xt[e, :, here] = x.T
        ht[e, :, here] = hidden.T
        return dot(hidden, dn[e], NN).astype(bf16), dot(both, gu[e], NT).astype(bf16)

    def run_expert(e, low):
        def aligned(n, carry):
            group = pl.ds(n * 8, 8)
            here = pl.ds(pl.multiple_of(n * 256, 256), 256)
            x = land[group, low : low + 32].reshape(256, WIDTH)
            g = gr_ref[group, low : low + 32].reshape(256, WIDTH)
            out, back = expert(e, x, g, here)
            land[group, low : low + 32] = out.reshape(8, 32, WIDTH)
            rows[group, low : low + 32] = back.reshape(8, 32, WIDTH)
            return carry

        lax.fori_loop(0, 2, aligned, 0)
        g = split(gr_ref[:, 32:48], e)
        gm[e] = g
        out, back = expert(e, split(land[:, 32:48], e), g, slice(512, 640))
        mixed[0, e] = out
        mixed[1, e] = back

    def expert_grads(e):
        for k in (1, 3, 2, 0):

            def block(n, carry, k=k):
                s = lax.rem(ring + k, 4) * 2 + lax.rem(far + n, 2)
                features = pl.ds(pl.multiple_of(s * 128, 128), 128)
                units = pl.ds(pl.multiple_of(s * 64, 64), 64)
                dw[e, k, n, :128, :] = dot(xt[e, features, :], hg[e], NN).astype(bf16)
                low = 48 * e
                part = dot(
                    ht[e, units, :512], gr_ref[:, low : low + 32].reshape(512, WIDTH), NN
                )
                part += dot(ht[e, units, 512:], gm[e], NN)
                dw[e, k, n, 128:, :] = part.astype(bf16)
                return carry

            lax.fori_loop(0, 2, block, 0)

    def arrived(part):
        for k in range(1, N_SHARD):
            source = lax.rem(me + N_SHARD - k, N_SHARD)
            to_expert(part, k, source, source, source).wait_recv()

    for e in range(LOCAL_EXPERTS):
        for s in range(N_SEQ):
            for copy in weights(e, s):
                copy.wait()
    arrived(0)
    for part in range(2):
        for k in range(1, N_SHARD):
            peer = lax.rem(me + k, N_SHARD)
            to_expert(part, k, peer, me, peer).wait_send()
    run_expert(0, 0)
    for k in range(1, N_SHARD):
        peer = lax.rem(me + k, N_SHARD)
        to_source(0, k, peer, me, peer).start()
    arrived(1)
    run_expert(1, 48)
    land[:, 32:48] = join(mixed[0, 0], mixed[0, 1])
    rows[:, 32:48] = join(mixed[1, 0], mixed[1, 1])
    for k in range(1, N_SHARD):
        peer = lax.rem(me + k, N_SHARD)
        to_source(1, k, peer, me, peer).start()
    returned[me] = rows[me]
    expert_grads(0)
    for k in (1, 3):
        to_ring(0, k).start()
    expert_grads(1)

    for part in range(2):
        for k in range(1, N_SHARD):
            source = lax.rem(me + N_SHARD - k, N_SHARD)
            to_source(part, k, source, source, source).wait_recv()
    moe_in_grad = dot(pick_ref[...], returned[...].reshape(N_SHARD * 80, WIDTH), NN)
    residual = res_ref[...]
    inverse = lax.rsqrt(jnp.mean(residual * residual, axis=1, keepdims=True) + epsilon)
    scaled = moe_in_grad * gain_ref[...]
    moe_part = inverse * scaled - residual * (inverse * inverse * inverse) * jnp.mean(
        residual * scaled, axis=1, keepdims=True
    )
    residual_grad = cot_ref[...].astype(f32) + moe_part
    resg_ref[...] = residual_grad
    branch = residual_grad.astype(bf16)
    attended_grad = dot(branch, ow_ref[...], NT).astype(bf16)
    for p in range(N_SEQ):
        ags[p] = attended_grad[:, 128 * p : 128 * p + 128]
        if p > 1:
            to_head(p).start()
        else:

            @pl.when(far != p)
            def _(p=p):
                to_head(p).start()

    gl[seq] = ags[far]
    for p in range(N_SEQ):
        po[(4 - p // 2) % 4, p % 2] = dot(attp[:, 128 * p : 128 * p + 128].T, branch, NN).astype(
            bf16
        )
    for k in range(1, N_SEQ):
        from_head(lax.rem(seq + k, N_SEQ)).wait_recv()
    for k in (1, 3, 2):
        to_ring(1, k).start()
    to_ring(0, 2).start()
    for k in (1, 2, 3):
        out_to_ring(k).start()
    for k in range(1, N_SHARD):
        to_token_expert(k).start()
    came_own = pltpu.make_async_copy(land.at[me], came_ref.at[me], own.at[0])
    came_own.start()
    dw_own = [pltpu.make_async_copy(dw.at[e, 0], dw_ref.at[e], own.at[1 + e]) for e in range(2)]
    for copy in dw_own:
        copy.start()
    po_own = pltpu.make_async_copy(po.at[0], po_ref, own.at[3])
    po_own.start()

    def begin(i, carry):
        qs[i] = spread(q_ref[i], False)
        gs[i] = spread(gl[i], True)
        product = wide_ref[i] * gl[i].astype(f32).T
        delta_ref[i] = jnp.concatenate(
            [
                jnp.sum(product[:HEAD], axis=0, keepdims=True),
                jnp.sum(product[HEAD:], axis=0, keepdims=True),
            ],
            axis=1,
        )
        dq[i] = jnp.zeros((HEAD, 2 * TOK_DEV), f32)
        return carry

    lax.fori_loop(0, N_SEQ, begin, 0)

    def tile(t, i, n, masked):
        here = slice(n * BWD_TILE, (n + 1) * BWD_TILE)
        memory = mem_ref[t, 8 * n : 8 * n + 8].reshape(BWD_TILE, 2 * HEAD)
        scores = dot(memory, qs[i], NT)
        weight = jnp.exp(scores - lse_ref[i])
        if masked:
            weight = jnp.where(admitted(scores.shape, me, n * BWD_TILE), weight, 0.0)
        weight_grad = dot(memory, gs[i], NT)
        score_grad = (weight * (weight_grad - delta_ref[i])).astype(bf16)
        here_grad = dot(weight.astype(bf16), gs[i], NN) + dot(score_grad, qs[i], NN)
        if masked:
            acc[here, :] = here_grad
        else:
            acc[here, :] += here_grad
        dq[i] += dot(kt[:, here], score_grad, NN)

    def turned(grad, n, t):
        cosine, sine = cos_ref[t], sin_ref[t]
        if n:
            key = lax.broadcasted_iota(jnp.int32, cosine.shape, 1) < HEAD
            cosine = jnp.where(key, cosine, 1.0)
            sine = jnp.where(key, sine, 0.0)
        other = dot(grad, turn_ref[n], NT)
        return (grad.astype(f32) * cosine + other * sine).astype(bf16)

    def step(t, carry):
        for n in range(4):
            block = mem_ref[t, 4 * n : 4 * n + 4].reshape(512, 2 * HEAD)
            kt[:, 512 * n : 512 * n + 512] = block.T[:HEAD]
        tile(t, t, 0, True)
        tile(t, t, 1, True)
        grad = dq[t] * (1.0 / math.sqrt(HEAD))
        grad = jnp.concatenate([grad[:, :TOK_DEV], grad[:, TOK_DEV:]], axis=0).T.astype(bf16)
        pgq_ref[t] = turned(grad, 0, t)

        @pl.when(t != seq)
        def _():
            to_token(0, t, seq).start()

        def rest(i, inner):
            tile(t, i, 0, False)
            tile(t, i, 1, False)
            return inner

        lax.fori_loop(t + 1, N_SEQ, rest, 0)
        for n in range(4):
            block = acc[512 * n : 512 * n + 512, :].astype(bf16)
            stage[t, 4 * n : 4 * n + 4] = block.reshape(4, TOK_DEV, 2 * HEAD)
        dl[t, me] = stage[t, me]
        for k in range(1, N_SHARD):
            peer = lax.rem(me + k, N_SHARD)
            to_owner(t, k, peer, me, peer).start()
        return carry

    lax.fori_loop(0, N_SEQ, step, 0)

    def gathered(t, carry):
        for k in range(1, N_SHARD):
            source = lax.rem(me + N_SHARD - k, N_SHARD)
            to_owner(t, k, source, source, source).wait_recv()
        grad = jnp.sum(dl[t].astype(f32), axis=0).astype(bf16)
        pgm_ref[t] = turned(grad, 1, t)

        @pl.when(t != seq)
        def _():
            to_token(1, t, seq).start()

        return carry

    lax.fori_loop(0, N_SEQ, gathered, 0)
    mine = [
        pltpu.make_async_copy(pgq_ref.at[seq], tokq_ref.at[seq], own.at[4]),
        pltpu.make_async_copy(pgm_ref.at[seq], tokm_ref.at[seq], own.at[5]),
    ]
    for copy in mine:
        copy.start()

    for part in range(2):
        for k in range(1, N_SHARD):
            peer = lax.rem(me + k, N_SHARD)
            to_source(part, k, peer, me, peer).wait_send()
    for p in range(N_SEQ):
        if p > 1:
            to_head(p).wait_send()
        else:

            @pl.when(far != p)
            def _(p=p):
                to_head(p).wait_send()

    for k in range(1, N_SHARD):
        to_token_expert(k).wait()
    for e in range(LOCAL_EXPERTS):
        for k in (1, 2, 3):
            to_ring(e, k).wait()
    for k in (1, 2, 3):
        out_to_ring(k).wait()

    def end(t, carry):
        for k in range(1, N_SHARD):
            peer = lax.rem(me + k, N_SHARD)
            to_owner(t, k, peer, me, peer).wait_send()
        return carry

    lax.fori_loop(0, N_SEQ, end, 0)
    for n in range(2):
        for k in range(1, N_SEQ):
            peer = lax.rem(seq + k, N_SEQ)
            to_token(n, peer, seq).wait_send()
            to_token(n, peer, peer).wait_recv()
    for copy in mine + dw_own + [came_own, po_own]:
        copy.wait()


def late(operands, ident):
    dma = pltpu.SemaphoreType.DMA
    vmem = pl.BlockSpec(memory_space=pltpu.VMEM)
    chunk = jax.ShapeDtypeStruct((N_SEQ, TOK_DEV, 2 * HEAD), bf16)
    wide = jax.ShapeDtypeStruct((TOK_DEV, WIDTH), f32)
    routed = (N_SHARD, 80, WIDTH)
    grads = (LOCAL_EXPERTS, 2, 192, WIDTH)
    return pl.pallas_call(
        late_kernel,
        in_specs=[vmem] * 8 + [ANY] + [vmem] * 7,
        out_specs=[vmem] * 4 + [ANY] * 7,
        out_shape=[
            wide,
            wide,
            chunk,
            chunk,
            chunk,
            chunk,
            jax.ShapeDtypeStruct(routed, bf16),
            jax.ShapeDtypeStruct(grads, bf16),
            jax.ShapeDtypeStruct((3,) + grads, bf16),
            jax.ShapeDtypeStruct((2, 128, WIDTH), bf16),
            jax.ShapeDtypeStruct((3, 2, 128, WIDTH), bf16),
        ],
        scratch_shapes=[
            pltpu.VMEM((LOCAL_EXPERTS, WIDTH, 2 * FF), bf16),
            pltpu.VMEM((LOCAL_EXPERTS, FF, WIDTH), bf16),
            pltpu.VMEM(routed, bf16),
            pltpu.VMEM(routed, bf16),
            pltpu.VMEM(routed, bf16),
            pltpu.VMEM((LOCAL_EXPERTS, WIDTH, EXPERT_ROWS), bf16),
            pltpu.VMEM((LOCAL_EXPERTS, FF, EXPERT_ROWS), bf16),
            pltpu.VMEM((LOCAL_EXPERTS, EXPERT_ROWS, 2 * FF), bf16),
            pltpu.VMEM((LOCAL_EXPERTS, 128, WIDTH), bf16),
            pltpu.VMEM((2, LOCAL_EXPERTS, 128, WIDTH), bf16),
            pltpu.VMEM((LOCAL_EXPERTS, 4, 2, 192, WIDTH), bf16),
            pltpu.VMEM((TOK_DEV, WIDTH), bf16),
            pltpu.VMEM((N_SEQ, TOK_DEV, 128), bf16),
            pltpu.VMEM((4, 2, 128, WIDTH), bf16),
            pltpu.VMEM((N_SEQ, TOK_DEV, 2 * HEAD), bf16),
            pltpu.VMEM((N_SEQ, 2 * TOK_DEV, 2 * HEAD), bf16),
            pltpu.VMEM((N_SEQ, 2 * TOK_DEV, 2 * HEAD), bf16),
            pltpu.VMEM((N_SEQ, 1, 2 * TOK_DEV), f32),
            pltpu.VMEM((HEAD, SUPER), bf16),
            pltpu.VMEM((SUPER, 2 * HEAD), f32),
            pltpu.VMEM((N_SEQ, HEAD, 2 * TOK_DEV), f32),
            pltpu.VMEM((N_SEQ, N_SHARD, TOK_DEV, 2 * HEAD), bf16),
            pltpu.VMEM((N_SEQ, N_SHARD, TOK_DEV, 2 * HEAD), bf16),
            dma((LOCAL_EXPERTS, N_SEQ, 2)),
            dma((2, N_SHARD - 1)),
            dma((2, N_SHARD - 1)),
            dma((2, N_SHARD - 1)),
            dma((2, N_SHARD - 1)),
            dma((LOCAL_EXPERTS, 3)),
            dma((LOCAL_EXPERTS, 3)),
            dma((3,)),
            dma((3,)),
            dma((N_SEQ, N_SHARD - 1)),
            dma((N_SEQ, N_SHARD - 1)),
            dma((N_SEQ,)),
            dma((N_SEQ,)),
            dma((N_SHARD - 1,)),
            dma((N_SHARD - 1,)),
            dma((2, N_SEQ)),
            dma((2, N_SEQ)),
            dma((6,)),
        ],
        compiler_params=pltpu.CompilerParams(
            collective_id=ident, has_side_effects=True, vmem_limit_bytes=63 << 20
        ),
        name="experts_attention_backward",
    )(*operands)


def group_columns(rows):
    lead = rows.shape[:-1]
    queries = rows[..., : HEADS * HEAD].reshape(lead + (N_SEQ, 2 * HEAD))
    keys = rows[..., HEADS * HEAD : (HEADS + KV) * HEAD].reshape(lead + (N_SEQ, HEAD))
    values = rows[..., (HEADS + KV) * HEAD :].reshape(lead + (N_SEQ, HEAD))
    return jnp.concatenate([queries, keys, values], axis=-1)


def ungroup_columns(groups):
    rows = groups.shape[0]
    return jnp.concatenate(
        [
            groups[:, :, : 2 * HEAD].reshape(rows, HEADS * HEAD),
            groups[:, :, 2 * HEAD : 3 * HEAD].reshape(rows, KV * HEAD),
            groups[:, :, 3 * HEAD :].reshape(rows, KV * HEAD),
        ],
        axis=1,
    )


def rope_pair(shard):
    half = HEAD // 2
    frequency = jnp.exp(
        jnp.arange(half, dtype=f32) * jnp.float32(-2.0 * math.log(rope_base) / HEAD)
    )
    chunk = jnp.arange(N_SEQ, dtype=jnp.int32)[:, None] * N_SHARD + shard
    position = chunk * TOK_DEV + jnp.arange(TOK_DEV, dtype=jnp.int32)[None, :]
    angles = position.reshape(HEAD_ROWS, 1).astype(f32) * frequency[None, :]
    return jnp.tile(jnp.cos(angles), (1, 6)), jnp.tile(jnp.sin(angles), (1, 6))


def turn_matrix():
    row = jnp.arange(3 * HEAD, dtype=jnp.int32)[:, None]
    col = jnp.arange(3 * HEAD, dtype=jnp.int32)[None, :]
    half = HEAD // 2
    low = col % HEAD < half
    minus = low & (row == col + half)
    plus = (~low) & (row == col - half)
    return (plus.astype(f32) - minus.astype(f32)).astype(bf16)


def after(value, *others):
    return lax.optimization_barrier((value,) + others)[0]


def routing(routes, route_weights):
    ids = jnp.arange(EXPERTS, dtype=jnp.int32)
    hit = routes[:, :, None] == ids[None, None, :]
    mask = jnp.sum(hit.astype(f32), axis=1)
    weight = jnp.sum(jnp.where(hit, route_weights[:, :, None], 0.0), axis=1)
    token = jnp.arange(TOK_DEV, dtype=jnp.int32)
    earlier = (token[:, None] > token[None, :]).astype(bf16)
    before = dot(earlier, mask.astype(bf16), NN)
    code = jnp.where(mask > 0.0, before, -1.0).astype(bf16)
    place = jnp.arange(N_SHARD * 80, dtype=jnp.int32)
    row = place % 80
    slot = jnp.where(row < 40, row, jnp.where(row < 48, row - 8, row - 48))
    owner = place // 80 * LOCAL_EXPERTS + (row >= 40).astype(jnp.int32)
    widen = (owner[None, :] == ids[:, None]).astype(bf16)
    pick = dot(code, widen, NN) == slot.astype(f32)[None, :]
    high = weight.astype(bf16)
    low = (weight - high.astype(f32)).astype(bf16)
    high = jnp.where(pick, dot(high, widen, NN), 0.0)
    low = jnp.where(pick, dot(low, widen, NN), 0.0)
    return pick.astype(bf16), high.astype(bf16), low.astype(bf16), jnp.sum(high + low, axis=0)


def on_device(
    layer_input,
    attn_gain,
    moe_gain,
    w_qkv,
    w_out,
    w_gate,
    w_up,
    w_down,
    routes,
    route_weights,
    cotangent,
):
    seq = lax.axis_index("seq")
    shard = lax.axis_index("shard")
    along_x = [(s, s + 1 - 2 * (s % 2)) for s in range(N_SEQ)]

    grouped = group_columns(w_qkv)
    pieces = grouped.reshape(8, N_SEQ, 2, 128).transpose(1, 2, 0, 3)
    gains = jnp.concatenate([attn_gain, moe_gain, jnp.zeros((112,), bf16)])
    gains = jnp.broadcast_to(gains[None, None, :], (N_SEQ, 16, 128))
    pieces = jnp.concatenate([pieces.reshape(N_SEQ, 16, 128), gains], axis=1)
    out_rows = w_out.reshape(8, 8, 128).transpose(1, 0, 2).reshape(2, 32, 128)
    tokens, columns, out_slabs = first_gather(
        layer_input.reshape(8, TOK_DEV // 8, WIDTH), pieces, out_rows, 1
    )
    out_slabs = out_slabs.reshape(2, N_SHARD, 8, 8, 128).transpose(0, 1, 3, 2, 4)
    out_slabs = out_slabs.reshape(2 * N_SHARD * 8, WIDTH)
    expert_pack = jnp.concatenate(
        [jnp.concatenate([w_gate, w_up], axis=2), w_down], axis=1
    )
    expert_weights = lax.all_gather(after(expert_pack, tokens), "seq", axis=1)
    gain_rows = columns[:, N_SEQ, :8, :16].transpose(1, 0, 2)
    gain_attn = gain_rows[:, :, :8].reshape(WIDTH).astype(f32)
    gain_moe = gain_rows[:, :, 8:].reshape(WIDTH).astype(f32)
    columns = columns[:, :N_SEQ].reshape(N_SHARD, N_SEQ, 2, 8, 128)
    columns = columns.transpose(1, 0, 3, 2, 4).reshape(WIDTH, COLS)

    wide = tokens.reshape(HEAD_ROWS, WIDTH).astype(f32)
    inverse = lax.rsqrt(jnp.mean(wide * wide, axis=1, keepdims=True) + epsilon)
    normed = (wide * inverse * gain_attn).astype(bf16)
    cosine, sine = rope_pair(shard)
    turn = turn_matrix()
    turned = dot(columns[:, : 3 * HEAD], turn, NN).astype(bf16)
    projected = dot(normed, jnp.concatenate([columns, turned], axis=1), NN)
    rotated = projected[:, : 3 * HEAD] * cosine + projected[:, COLS:] * sine
    queries = rotated[:, : 2 * HEAD].astype(bf16) * jnp.bfloat16(1.0 / math.sqrt(HEAD))
    queries = queries.reshape(N_SEQ, TOK_DEV, 2 * HEAD)
    memory = jnp.concatenate(
        [rotated[:, 2 * HEAD :], projected[:, 3 * HEAD : COLS]], axis=1
    ).astype(bf16)
    memory = memory.reshape(N_SEQ, TOK_DEV, 2 * HEAD)

    pick, scale_high, scale_low, slot_scale = routing(routes, route_weights)
    pick_turned = pick.T
    grad_send = (slot_scale[:, None] * dot(pick_turned, cotangent, NN)).astype(bf16)
    attended_wide, lse, attended, memory, grad_rows, qkv_rows, out_slabs = attention(
        queries,
        memory,
        grad_send.reshape(N_SHARD, 80, WIDTH),
        grouped.reshape(16, WIDTH),
        out_slabs,
        2,
    )
    qkv_rows = qkv_rows.reshape(N_SHARD * 8, 2 * WIDTH)
    qkv_all = lax.all_gather(qkv_rows, "seq", axis=0, tiled=True)
    left = jnp.arange(2 * HEAD, dtype=jnp.int32) < HEAD
    turns = turn[: 2 * HEAD, : 2 * HEAD]
    turns = jnp.stack([turns, jnp.where(left[:, None] & left[None, :], turns, 0)])
    (
        residual,
        residual_grad,
        query_grad,
        memory_grad,
        token_query,
        token_memory,
        came_back,
        expert_mine,
        expert_sent,
        out_own,
        out_sent,
    ) = late(
        (
            attended,
            out_slabs.reshape(WIDTH, WIDTH),
            layer_input,
            cotangent,
            gain_moe[None, :],
            pick,
            pick_turned,
            grad_rows,
            expert_weights,
            queries,
            attended_wide,
            lse,
            memory,
            cosine[:, : 2 * HEAD].reshape(N_SEQ, TOK_DEV, 2 * HEAD),
            sine[:, : 2 * HEAD].reshape(N_SEQ, TOK_DEV, 2 * HEAD),
            turns,
        ),
        3,
    )
    came_back = came_back.reshape(N_SHARD * 80, WIDTH)
    expert_sums = expert_mine.astype(f32) + jnp.sum(expert_sent.astype(f32), axis=0)
    out_sums = out_own.astype(f32) + jnp.sum(out_sent.astype(f32), axis=0)
    far = seq % 2
    out_mine = lax.dynamic_index_in_dim(out_sums, far, 0, keepdims=False)
    out_other = lax.dynamic_index_in_dim(out_sums, 1 - far, 0, keepdims=False)
    other = jnp.concatenate(
        [expert_sums[:, 1].reshape(LOCAL_EXPERTS * 192, WIDTH), out_other], axis=0
    ).astype(bf16)
    other = lax.ppermute(other, "seq", along_x).astype(f32)
    expert_sums = expert_sums[:, 0] + other[: LOCAL_EXPERTS * 192].reshape(
        LOCAL_EXPERTS, 192, WIDTH
    )
    out_part = out_mine + other[LOCAL_EXPERTS * 192 :]
    x_wide = layer_input.astype(f32)
    moe_sum = dot(scale_high, came_back, NN) + dot(scale_low, came_back, NN)
    block_out = (residual + moe_sum).astype(bf16)

    projected_grad = jnp.concatenate(
        [query_grad.reshape(HEAD_ROWS, 2 * HEAD), memory_grad.reshape(HEAD_ROWS, 2 * HEAD)], axis=1
    )

    qkv_part = dot(normed, projected_grad, TN)
    qkv_part = qkv_part.reshape(N_SEQ, N_SHARD, 8, COLS).transpose(1, 0, 2, 3)
    out_part = out_part.reshape(N_SHARD, 8, WIDTH)
    pack = expert_pack.astype(f32)
    moe_gain_part = jnp.sum(
        pack[:, :128] * expert_sums[:, :128], axis=(0, 2)
    ) / lax.dynamic_slice_in_dim(gain_moe, seq * 128, 128)
    moe_gain_part = moe_gain_part.reshape(N_SHARD, 1, 8)
    moe_gain_high = moe_gain_part.astype(bf16)
    moe_gain_low = (moe_gain_part - moe_gain_high.astype(f32)).astype(bf16)
    gain_part = jnp.concatenate([moe_gain_high, moe_gain_low], axis=1)
    gain_part = jnp.pad(gain_part, ((0, 0), (0, 14), (0, COLS - 8)))
    sums = jnp.concatenate(
        [
            qkv_part.reshape(N_SHARD, 64, COLS).astype(bf16),
            out_part.reshape(N_SHARD, 32, COLS).astype(bf16),
            gain_part,
        ],
        axis=1,
    )
    sums = jnp.sum(exchange(sums, "shard", N_SHARD, 4).astype(f32), axis=0)
    out_weight_grad = sums[64:96].reshape(8, WIDTH)
    moe_gain_grad = sums[96, :8] + sums[97, :8]
    qkv_groups = lax.all_to_all(sums[:64].reshape(N_SEQ, 8, COLS), "seq", 0, 0)
    qkv_groups = qkv_groups.transpose(1, 0, 2)
    attn_gain_grad = jnp.sum(grouped.astype(f32) * qkv_groups, axis=(1, 2)) / attn_gain.astype(f32)
    qkv_weight_grad = ungroup_columns(qkv_groups)

    token_grad = jnp.concatenate([token_query, token_memory], axis=2)
    token_grad = token_grad.transpose(1, 0, 2).reshape(TOK_DEV, N_SEQ * COLS)
    normed_grad = dot(token_grad, qkv_all, NT)
    inverse_one = lax.rsqrt(jnp.mean(x_wide * x_wide, axis=1, keepdims=True) + epsilon)
    scaled = normed_grad * gain_attn
    attn_part = inverse_one * scaled - x_wide * inverse_one**3 * jnp.mean(
        x_wide * scaled, axis=1, keepdims=True
    )
    input_grad = (residual_grad + attn_part).astype(bf16)
    return (
        block_out,
        input_grad,
        attn_gain_grad,
        moe_gain_grad,
        qkv_weight_grad,
        out_weight_grad,
        expert_sums[:, :128, :FF],
        expert_sums[:, :128, FF:],
        expert_sums[:, 128:],
    )


def solution(mesh):
    token = P(("seq", "shard"), None)
    vector = P(("seq", "shard"))
    expert = P("shard", "seq", None)
    return jax.shard_map(
        on_device,
        mesh=mesh,
        in_specs=(
            token,
            vector,
            vector,
            token,
            token,
            expert,
            expert,
            expert,
            token,
            token,
            token,
        ),
        out_specs=(token, token, vector, vector, token, token, expert, expert, expert),
        check_vma=False,
    )
```

```python
import functools
import math

import jax
import jax.numpy as jnp
from jax import lax
from jax.experimental import pallas as pl
from jax.experimental.pallas import tpu as pltpu
from jax.sharding import PartitionSpec as P

HEADS = 16
KV = 8
HEAD = 64
EXPERTS = 32
TOPK = 8
TOK_DEV = 128
CAP = 40
WIDTH = 1024
FF = 512
N_SEQ = 8
N_SHARD = 16
HEAD_ROWS = TOK_DEV * N_SEQ
TOKENS = TOK_DEV * N_SEQ * N_SHARD
LOCAL_EXPERTS = EXPERTS // N_SHARD
EXPERT_ROWS = N_SHARD * CAP
COLS = 256
SUPER = TOK_DEV * N_SHARD
BWD_TILE = 1024
LIMIT = 63

epsilon = 1e-06
rope_base = 10000.0

f32 = jnp.float32
bf16 = jnp.bfloat16
MESH = pl.DeviceIdType.MESH
ANY = pl.BlockSpec(memory_space=pl.ANY)
NT = (((1,), (1,)), ((), ()))
NN = (((1,), (0,)), ((), ()))
TN = (((0,), (0,)), ((), ()))


def dot(left, right, dims):
    return lax.dot_general(left, right, dims, preferred_element_type=f32)


def greet(peers):
    barrier = pltpu.get_barrier_semaphore()
    for axis, peer in peers:
        pl.semaphore_signal(barrier, inc=1, device_id={axis: peer}, device_id_type=MESH)
    pl.semaphore_wait(barrier, len(peers))


def remote(source, target, send, recv, axis, peer):
    copy = pltpu.make_async_remote_copy(
        src_ref=source,
        dst_ref=target,
        send_sem=send,
        recv_sem=recv,
        device_id={axis: peer},
        device_id_type=MESH,
    )
    copy.start()
    return copy


def staged(axis, units, share, x_ref, place, sem_send, sem_recv, own):
    me = lax.axis_index(axis)
    cores = 2 if axis == "shard" else 1
    core = lax.rem(me, cores)
    pair = lax.rem(me // cores, 2)
    ring = me // (2 * cores)

    def at(r, p, c):
        return (r * 2 + p) * cores + c

    ring_peer = [at(lax.rem(ring + k, 4), pair, core) for k in (1, 2, 3)]
    ring_from = [lax.rem(ring + 4 - k, 4) for k in (1, 2, 3)]
    pair_peer = at(ring, 1 - pair, core)
    core_peer = at(ring, pair, 1 - core)
    mine = pltpu.make_async_copy(x_ref, place(me, 0, units), own)
    mine.start()
    sends = []

    def go(source, index, low, high, peer):
        n = len(sends)
        sends.append(
            remote(source, place(index, low, high), sem_send.at[n], sem_recv.at[n], axis, peer)
        )
        return sends[-1]

    to_pair = go(x_ref, me, 0, units, pair_peer)
    to_ring = [go(x_ref, me, 0, units, peer) for peer in ring_peer]
    landed = []
    if cores == 2:
        landed.append(go(x_ref, me, 0, units, core_peer))

    def pass_core(index, low, high):
        if cores == 2:
            landed.append(go(place(index, low, high), index, low, high, core_peer))

    to_pair.wait_recv()
    fwd_ring = [
        go(place(pair_peer, 0, share), pair_peer, 0, share, peer) for peer in ring_peer
    ]
    pass_core(pair_peer, 0, units)
    fwd_pair = []
    for k in (0, 2, 1):
        to_ring[k].wait_recv()
        source = at(ring_from[k], pair, core)
        if share < units:
            fwd_pair.append((k, go(place(source, share, units), source, share, units, pair_peer)))
        pass_core(source, 0, units)
    for k in (0, 2, 1):
        fwd_ring[k].wait_recv()
        pass_core(at(ring_from[k], 1 - pair, core), 0, share)
    for k, copy in fwd_pair:
        copy.wait_recv()
        pass_core(at(ring_from[k], 1 - pair, core), share, units)
    for copy in landed:
        copy.wait_recv()
    mine.wait()
    for copy in sends:
        copy.wait_send()


def first_kernel(
    x_ref, w_ref, v_ref, xo_ref, wo_ref, vo_ref, w_mid, w_pack, send, recv, own, wsend, wrecv, wown, vown
):
    seq = lax.axis_index("seq")
    shard = lax.axis_index("shard")
    greet(
        [("seq", lax.rem(seq + k, N_SEQ)) for k in range(1, N_SEQ)]
        + [("shard", lax.rem(shard + k, N_SHARD)) for k in range(1, N_SHARD)]
    )
    mine = pltpu.make_async_copy(w_ref.at[seq], w_mid.at[seq], wown)
    mine.start()
    slab = pltpu.make_async_copy(v_ref, vo_ref.at[shard], vown)
    slab.start()
    pieces = []
    for k in range(1, N_SEQ):
        peer = lax.rem(seq + k, N_SEQ)
        pieces.append(
            remote(w_ref.at[peer], w_mid.at[seq], wsend.at[k - 1], wrecv.at[k - 1], "seq", peer)
        )
    rows = []
    for k in range(1, N_SHARD):
        peer = lax.rem(shard + k, N_SHARD)
        n = 21 + k
        rows.append(
            remote(v_ref, vo_ref.at[shard], wsend.at[n], wrecv.at[n], "shard", peer)
        )
    mine.wait()
    for piece in pieces:
        piece.wait()
    packed = jnp.zeros((16, 128), f32)
    row = lax.broadcasted_iota(jnp.int32, (16, 128), 0)
    for s in range(N_SEQ):
        packed = jnp.where(row == s, w_mid[s, 16:].astype(f32), packed)
        w_pack[s] = w_mid[s, :16]
    w_pack[N_SEQ] = packed.astype(bf16)
    mine = pltpu.make_async_copy(w_pack, wo_ref.at[shard], wown)
    mine.start()
    pieces = []
    for k in range(1, N_SHARD):
        peer = lax.rem(shard + k, N_SHARD)
        n = 6 + k
        pieces.append(
            remote(w_pack, wo_ref.at[shard], wsend.at[n], wrecv.at[n], "shard", peer)
        )
    staged("seq", 8, 4, x_ref, lambda s, low, high: xo_ref.at[s, low:high], send, recv, own)
    slab.wait()
    for row in rows:
        row.wait()
    mine.wait()
    for piece in pieces:
        piece.wait()


def first_gather(x, pieces, rows, ident):
    return pl.pallas_call(
        first_kernel,
        out_shape=[
            jax.ShapeDtypeStruct((N_SEQ, 8, TOK_DEV // 8, WIDTH), bf16),
            jax.ShapeDtypeStruct((N_SHARD, N_SEQ + 1, 16, 128), bf16),
            jax.ShapeDtypeStruct((N_SHARD,) + rows.shape, bf16),
        ],
        in_specs=[ANY, ANY, ANY],
        out_specs=[ANY, ANY, ANY],
        scratch_shapes=[
            pltpu.VMEM(pieces.shape, bf16),
            pltpu.VMEM((N_SEQ + 1, 16, 128), bf16),
            pltpu.SemaphoreType.DMA((12,)),
            pltpu.SemaphoreType.DMA((12,)),
            pltpu.SemaphoreType.DMA,
            pltpu.SemaphoreType.DMA((38,)),
            pltpu.SemaphoreType.DMA((38,)),
            pltpu.SemaphoreType.DMA,
            pltpu.SemaphoreType.DMA,
        ],
        compiler_params=pltpu.CompilerParams(collective_id=ident, has_side_effects=True),
        name="gather_tokens",
    )(x, pieces, rows)


def spread(rows, right):
    zeros = jnp.zeros((TOK_DEV, HEAD), rows.dtype)
    parts = [rows[:, :HEAD], rows[:, HEAD:]]
    if right:
        parts = [jnp.concatenate([zeros, part], axis=1) for part in parts]
    else:
        parts = [jnp.concatenate([part, zeros], axis=1) for part in parts]
    return jnp.concatenate(parts, axis=0)


def admitted(shape, j, first_key):
    key_pos = first_key + lax.broadcasted_iota(jnp.int32, shape, 0)
    query_pos = j * TOK_DEV + (lax.broadcasted_iota(jnp.int32, shape, 1) & (TOK_DEV - 1))
    return query_pos >= key_pos


def transfer(source, target, send, recv, axis, peer):
    return pltpu.make_async_remote_copy(
        src_ref=source,
        dst_ref=target,
        send_sem=send,
        recv_sem=recv,
        device_id={axis: peer},
        device_id_type=MESH,
    )


def everyone(seq, shard):
    return [("seq", lax.rem(seq + k, N_SEQ)) for k in range(1, N_SEQ)] + [
        ("shard", lax.rem(shard + k, N_SHARD)) for k in range(1, N_SHARD)
    ]


def attention_kernel(*refs):
    (x_ref, cols_ref, gain_ref, cos_ref, sin_ref, turn_ref, slab_ref, rows_ref) = refs[:8]
    (own_ref, gain2_ref, pickt_ref, cot_ref) = refs[8:12]
    (q_ref, wide_ref, lse_ref, attp_ref, res_ref) = refs[12:17]
    (norm_ref, mem_ref, rows_out, ow_ref, land_ref, cot_out) = refs[17:23]
    (land, vt, heads, peak_ref, total_ref, acc_ref, att, ow, weights_ref, norm, rows) = refs[23:34]
    (ksend, krecv, gsend, grecv, esend, erecv, fsend, frecv, hsend, hrecv, own, msem) = refs[34:46]
    dsend, drecv = refs[46:]
    seq = lax.axis_index("seq")
    me = lax.axis_index("shard")
    core = lax.rem(me, 2)
    pair = lax.rem(me // 2, 2)
    ring = me // 4
    far = lax.rem(seq, 2)
    partner = seq + 1 - 2 * far

    def at(k, other_pair, other_core):
        p = 1 - pair if other_pair else pair
        c = 1 - core if other_core else core
        return (lax.rem(ring + 4 + k, 4) * 2 + p) * 2 + c

    def message(t, m, block, peer):
        return transfer(
            land.at[t, block], land.at[t, block], ksend.at[t, m], krecv.at[t, m], "shard", peer
        )

    def first(t):
        for k in (1, 2, 3):
            message(t, k - 1, me, at(k, 0, 0)).start()
        message(t, 3, me, at(0, 1, 0)).start()
        message(t, 4, me, at(0, 0, 1)).start()

    def second(t):
        block = at(0, 1, 0)
        message(t, 3, block, block).wait_recv()
        for k in (1, 2, 3):
            message(t, 4 + k, block, at(k, 0, 0)).start()
        message(t, 8, block, at(0, 0, 1)).start()
        for k in (1, 2, 3):
            block = at(-k, 0, 0)
            message(t, k - 1, block, block).wait_recv()
            message(t, 8 + k, block, at(0, 0, 1)).start()

    def third(t):
        for k in (1, 2, 3):
            block = at(-k, 1, 0)
            message(t, 4 + k, block, at(-k, 0, 0)).wait_recv()
            message(t, 11 + k, block, at(0, 0, 1)).start()

    def fourth(t):
        peer = at(0, 0, 1)
        message(t, 4, peer, peer).wait_recv()
        message(t, 8, at(0, 1, 1), peer).wait_recv()
        for k in (1, 2, 3):
            message(t, 8 + k, at(-k, 0, 1), peer).wait_recv()
            message(t, 11 + k, at(-k, 1, 1), peer).wait_recv()

    def to_shard(k):
        peer = lax.rem(me + k, N_SHARD)
        return transfer(
            rows_ref, rows_out.at[me], esend.at[k - 1], erecv.at[k - 1], "shard", peer
        )

    def slab_to_ring(n, k, block, peer):
        source = slab_ref if n == 0 else ow.at[block]
        return transfer(source, ow.at[block], fsend.at[n, k], frecv.at[n, k], "seq", peer)

    def grads_to_expert(k):
        peer = lax.rem(me + k, N_SHARD)
        return transfer(
            cot_ref.at[peer], cot_out.at[me], dsend.at[k - 1], drecv.at[k - 1], "shard", peer
        )

    def to_expert(k):
        peer = lax.rem(me + k, N_SHARD)
        here = pl.ds(pl.multiple_of(peer * 80, 16), 80)
        return transfer(
            rows.at[here], land_ref.at[me], hsend.at[k - 1], hrecv.at[k - 1], "shard", peer
        )

    def to_token(t, source):
        return transfer(
            heads.at[t], att.at[source], gsend.at[t], grecv.at[source], "seq", t
        )

    greet(everyone(seq, me))

    for half in range(2):
        block = cols_ref[...].astype(f32).reshape(N_SHARD, N_SEQ, 2, 8, 128)[:, :, half]
        block = jnp.swapaxes(block, 0, 1).reshape(WIDTH, 128).astype(bf16)
        weights_ref[:, 128 * half : 128 * half + 128] = block
    weights_ref[:, COLS:] = dot(weights_ref[:, :COLS], turn_ref[...], NN).astype(bf16)
    key = lax.broadcasted_iota(jnp.int32, (TOK_DEV, 2 * HEAD), 1) < HEAD

    def project(n, carry):
        here = pl.ds(pl.multiple_of(n * 512, 512), 512)
        x = x_ref[here, :].astype(f32)
        inverse = lax.rsqrt(jnp.mean(x * x, axis=1, keepdims=True) + epsilon)
        normed = (x * inverse * gain_ref[...]).astype(bf16)
        norm[here, :] = normed
        wide = dot(normed, weights_ref[...], NN).reshape(4, TOK_DEV, 2 * COLS)
        for m in range(4):
            t = 4 * n + m
            cosine, sine = cos_ref[t], sin_ref[t]
            query = wide[m, :, :128] * cosine + wide[m, :, 256:384] * sine
            q_ref[t] = query.astype(bf16) * jnp.bfloat16(1.0 / math.sqrt(HEAD))
            cosine, sine = jnp.where(key, cosine, 1.0), jnp.where(key, sine, 0.0)
            memory = wide[m, :, 128:256] * cosine + wide[m, :, 384:] * sine
            land[t, me] = memory.astype(bf16)
        return carry

    lax.fori_loop(0, 2, project, 0)
    norm_own = pltpu.make_async_copy(norm, norm_ref, own.at[3])
    norm_own.start()
    cot_own = pltpu.make_async_copy(cot_ref.at[me], cot_out.at[me], own.at[4])
    cot_own.start()

    def begin(t, carry):
        first(t)
        peak_ref[t] = jnp.full((1, 2 * TOK_DEV), -1e30, f32)
        total_ref[t] = jnp.zeros((1, 2 * TOK_DEV), f32)
        acc_ref[t] = jnp.zeros((HEAD, 2 * TOK_DEV), f32)
        return carry

    lax.fori_loop(0, N_SEQ, begin, 0)
    second(0)
    third(0)
    second(1)
    fourth(0)
    for k in range(1, N_SHARD):
        to_shard(k).start()
    slab_to_ring(0, 0, seq, partner).start()
    for k in (1, 2, 3):
        slab_to_ring(0, k, seq, lax.rem(seq + 2 * k, N_SEQ)).start()
    rows_own = pltpu.make_async_copy(rows_ref, rows_out.at[me], own.at[0])
    rows_own.start()
    slab_own = pltpu.make_async_copy(slab_ref, ow.at[seq], own.at[1])
    slab_own.start()

    def tile(t, i, masked):
        queries = spread(q_ref[i], False)
        scores = dot(land[t].reshape(SUPER, 2 * HEAD), queries, NT)
        if masked:
            scores = jnp.where(admitted(scores.shape, me, 0), scores, -1e30)
        peak = peak_ref[i]
        newest = jnp.maximum(peak, jnp.max(scores, axis=0, keepdims=True))
        weights = jnp.exp(scores - newest)
        shrink = jnp.exp(peak - newest)
        total = total_ref[i] * shrink + jnp.sum(weights, axis=0, keepdims=True)
        acc = acc_ref[i] * shrink + dot(vt[...], weights.astype(bf16), NN)
        return newest, total, acc

    def step(t, carry):
        pltpu.make_async_copy(land.at[t], mem_ref.at[t], msem.at[t]).start()

        for n in range(5):

            @pl.when(t == n)
            def _(n=n):
                for k in range(1, 4):
                    grads_to_expert(3 * n + k).start()

        @pl.when(t == 2)
        def _():
            slab_to_ring(0, 0, partner, partner).wait_recv()
            for k in (1, 2, 3):
                slab_to_ring(1, k, partner, lax.rem(seq + 2 * k, N_SEQ)).start()

        @pl.when(t + 1 < N_SEQ)
        def _():
            third(t + 1)

        @pl.when(t + 2 < N_SEQ)
        def _():
            second(t + 2)

        for n in range(4):
            rows = land[t, 4 * n : 4 * n + 4].reshape(512, 2 * HEAD)
            vt[:, 512 * n : 512 * n + 512] = rows.T[HEAD:]
        newest, total, acc = tile(t, t, True)
        acc = acc / total
        stacked = jnp.concatenate([acc[:, :TOK_DEV], acc[:, TOK_DEV:]], axis=0)
        wide_ref[t] = stacked
        heads[t] = stacked.T.astype(bf16)
        lse_ref[t] = newest + jnp.log(total)

        @pl.when(t != seq)
        def _():
            to_token(t, seq).start()

        def rest(i, inner):
            peak_ref[i], total_ref[i], acc_ref[i] = tile(t, i, False)
            return inner

        lax.fori_loop(t + 1, N_SEQ, rest, 0)

        @pl.when(t + 1 < N_SEQ)
        def _():
            fourth(t + 1)

        return carry

    lax.fori_loop(0, N_SEQ, step, 0)
    slab_own.wait()
    for k in (1, 2, 3):
        for n, block in enumerate((seq, partner)):
            slab_to_ring(n, k, block, lax.rem(seq + 2 * k, N_SEQ)).wait_send()
            source = lax.rem(block + N_SEQ - 2 * k, N_SEQ)
            slab_to_ring(n, k, source, lax.rem(seq + N_SEQ - 2 * k, N_SEQ)).wait_recv()
    slab_to_ring(0, 0, seq, partner).wait_send()
    ow_own = pltpu.make_async_copy(ow, ow_ref, own.at[1])
    ow_own.start()
    att[seq] = heads[seq]
    for k in range(1, N_SEQ):
        source = lax.rem(seq + k, N_SEQ)
        to_token(source, source).wait_recv()

    for s in range(N_SEQ):
        attp_ref[:, 128 * s : 128 * s + 128] = att[s]
    residual = own_ref[...].astype(f32) + dot(
        attp_ref[...], ow[...].reshape(WIDTH, WIDTH), NN
    )
    res_ref[...] = residual
    inverse = lax.rsqrt(jnp.mean(residual * residual, axis=1, keepdims=True) + epsilon)
    normed = (residual * inverse * gain2_ref[...]).astype(bf16)
    for k in range(N_SHARD):
        peer = lax.rem(me + k, N_SHARD)
        here = pl.ds(pl.multiple_of(peer * 80, 16), 80)
        rows[here, :] = dot(pickt_ref[here, :], normed, NN).astype(bf16)
        if k:
            to_expert(k).start()
    here = pl.ds(pl.multiple_of(me * 80, 16), 80)
    mine = pltpu.make_async_copy(rows.at[here], land_ref.at[me], own.at[2])
    mine.start()
    for k in range(1, N_SEQ):
        to_token(lax.rem(seq + k, N_SEQ), seq).wait_send()
    rows_own.wait()
    norm_own.wait()
    ow_own.wait()
    for k in range(1, N_SHARD):
        to_shard(k).wait()
    for k in range(1, N_SHARD):
        grads_to_expert(k).wait()
        to_expert(k).wait()
    mine.wait()
    cot_own.wait()

    def end(t, carry):
        for m in range(15):
            message(t, m, me, me).wait_send()
        pltpu.make_async_copy(land.at[t], mem_ref.at[t], msem.at[t]).wait()
        return carry

    lax.fori_loop(0, N_SEQ, end, 0)


def attention(operands, ident):
    dma = pltpu.SemaphoreType.DMA
    vmem = pl.BlockSpec(memory_space=pltpu.VMEM)
    shards = (N_SHARD - 1,)
    return pl.pallas_call(
        attention_kernel,
        in_specs=[vmem] * 6 + [ANY] * 2 + [vmem] * 3 + [ANY],
        out_specs=[vmem] * 5 + [ANY] * 6,
        out_shape=[
            jax.ShapeDtypeStruct((N_SEQ, TOK_DEV, 2 * HEAD), bf16),
            jax.ShapeDtypeStruct((N_SEQ, 2 * HEAD, TOK_DEV), f32),
            jax.ShapeDtypeStruct((N_SEQ, 1, 2 * TOK_DEV), f32),
            jax.ShapeDtypeStruct((TOK_DEV, WIDTH), bf16),
            jax.ShapeDtypeStruct((TOK_DEV, WIDTH), f32),
            jax.ShapeDtypeStruct((HEAD_ROWS, WIDTH), bf16),
            jax.ShapeDtypeStruct((N_SEQ, N_SHARD, TOK_DEV, 2 * HEAD), bf16),
            jax.ShapeDtypeStruct((N_SHARD, 8, 2 * WIDTH), bf16),
            jax.ShapeDtypeStruct((N_SEQ, 128, WIDTH), bf16),
            jax.ShapeDtypeStruct((N_SHARD, 80, WIDTH), bf16),
            jax.ShapeDtypeStruct((N_SHARD, 80, WIDTH), bf16),
        ],
        scratch_shapes=[
            pltpu.VMEM((N_SEQ, N_SHARD, TOK_DEV, 2 * HEAD), bf16),
            pltpu.VMEM((HEAD, SUPER), bf16),
            pltpu.VMEM((N_SEQ, TOK_DEV, 2 * HEAD), bf16),
            pltpu.VMEM((N_SEQ, 1, 2 * TOK_DEV), f32),
            pltpu.VMEM((N_SEQ, 1, 2 * TOK_DEV), f32),
            pltpu.VMEM((N_SEQ, HEAD, 2 * TOK_DEV), f32),
            pltpu.VMEM((N_SEQ, TOK_DEV, 128), bf16),
            pltpu.VMEM((N_SEQ, 128, WIDTH), bf16),
            pltpu.VMEM((WIDTH, 2 * COLS), bf16),
            pltpu.VMEM((HEAD_ROWS, WIDTH), bf16),
            pltpu.VMEM((N_SHARD * 80, WIDTH), bf16),
            dma((N_SEQ, 15)),
            dma((N_SEQ, 15)),
            dma((N_SEQ,)),
            dma((N_SEQ,)),
            dma(shards),
            dma(shards),
            dma((2, 4)),
            dma((2, 4)),
            dma(shards),
            dma(shards),
            dma((5,)),
            dma((N_SEQ,)),
            dma(shards),
            dma(shards),
        ],
        compiler_params=pltpu.CompilerParams(
            collective_id=ident, has_side_effects=True, vmem_limit_bytes=56 << 20
        ),
        name="attention_forward",
    )(*operands)


def late_kernel(*refs):
    (attp, ow_ref, res_ref, cot_ref, gain_ref, pick_ref, land_ref, gr_ref, w_ref) = refs[:9]
    (q_ref, wide_ref, lse_ref, mem_ref, cos_ref, sin_ref, turn_ref) = refs[9:16]
    (normed_ref, slab_ref, pack_ref, gcol_ref) = refs[16:20]
    (resg_ref, tok_ref, came_ref, sums_ref, qkv_ref, wout_ref, mgain_ref, kz_ref) = refs[20:28]
    qall_ref = refs[28]
    (gu, dn, land, rows, returned, xt, ht, hg, gm, mixed, dw, ags, xstage) = refs[29:42]
    (gl, qs, gs, delta_ref, kt, acc, dq, stage, dl) = refs[42:51]
    (mbuf, pg, qp, qstage, qland, qsum, osum, xland, oland, mstage, mland) = refs[51:62]
    cland, cstage, oseq = refs[62:65]
    (wsem, isend, irecv, ksend, krecv, psend, precv) = refs[65:72]
    (dsend, drecv, osend, orecv, jsend, jrecv, nsend, nrecv, own) = refs[72:81]
    (msem, asend, arecv, bsend, brecv, xsend, xrecv, csend, crecv, tsend, trecv) = refs[81:92]
    (usend, urecv, fsend, frecv) = refs[92:]
    seq = lax.axis_index("seq")
    me = lax.axis_index("shard")
    ring = seq // 2
    far = lax.rem(seq, 2)

    def weights(e, s):
        return (
            pltpu.make_async_copy(
                w_ref.at[e, s, :128], gu.at[e, 128 * s : 128 * s + 128], wsem.at[e, s, 0]
            ),
            pltpu.make_async_copy(
                w_ref.at[e, s, 128:], dn.at[e, 64 * s : 64 * s + 64], wsem.at[e, s, 1]
            ),
        )

    def flat(block, low, high):
        return pl.ds(pl.multiple_of(block * 80 + low, 16), high - low)

    back_pieces = ((0, 32), (32, 80))

    def to_source(part, k, block, source, peer):
        low, high = back_pieces[part]
        return transfer(
            rows.at[flat(block, low, high)],
            returned.at[flat(source, low, high)],
            isend.at[part, k - 1],
            irecv.at[part, k - 1],
            "shard",
            peer,
        )

    def to_token_expert(k):
        peer = lax.rem(me + k, N_SHARD)
        return transfer(
            land.at[peer], came_ref.at[me], jsend.at[k - 1], jrecv.at[k - 1], "shard", peer
        )

    def to_ring(e, k):
        peer = lax.rem(seq + 2 * k, N_SEQ)
        return transfer(
            dw.at[e, k], kz_ref.at[e, k - 1], ksend.at[e, k - 1], krecv.at[e, k - 1], "seq", peer
        )

    def out_to_shard(k, block, source, peer):
        return transfer(
            rows.at[flat(block, 0, 64)], oland.at[source], psend.at[k - 1], precv.at[k - 1], "shard", peer
        )

    def to_head(p):
        return transfer(
            ags.at[p], gl.at[seq], osend.at[p], orecv.at[seq], "seq", p
        )

    def from_head(source):
        return transfer(gl.at[source], gl.at[source], osend.at[0], orecv.at[source], "seq", source)

    core = lax.rem(me, 2)
    chip = me // 2

    def to_core(t):
        return transfer(
            stage.at[lax.rem(t, 4), :, 1 - core],
            cland.at[lax.rem(t, 4)],
            tsend.at[t],
            trecv.at[t],
            "shard",
            me + 1 - 2 * core,
        )

    def to_owner(t, k, block, source, peer):
        return transfer(
            cstage.at[lax.rem(t, 4), block],
            dl.at[t, source],
            dsend.at[t, k - 1],
            drecv.at[t, k - 1],
            "shard",
            peer * 2 + core,
        )

    def to_token(t, source):
        return transfer(pg.at[t], tok_ref.at[source], nsend.at[t], nrecv.at[source], "seq", t)

    def out_to_seq(p):
        return transfer(
            osum.at[p], oseq.at[seq], usend.at[p], urecv.at[seq], "seq", p
        )

    def out_from_seq(source):
        return transfer(
            oseq.at[source], oseq.at[source], usend.at[0], urecv.at[source], "seq", source
        )

    def slab_to_ring(n, k, block, peer):
        source = slab_ref if n == 0 else qall_ref.at[block]
        return transfer(
            source, qall_ref.at[block], fsend.at[n, k], frecv.at[n, k], "seq", peer
        )

    def fetch(t):
        slot = lax.rem(t, 2)
        return pltpu.make_async_copy(mem_ref.at[t], mbuf.at[slot], msem.at[slot])

    def qkv_to_shard(k, block, source, peer):
        return transfer(
            qstage.at[block], qland.at[source], asend.at[k - 1], arecv.at[k - 1], "shard", peer
        )

    def qkv_to_seq(k, block, source, peer):
        return transfer(
            qsum.at[block], qkv_ref.at[source], bsend.at[k - 1], brecv.at[k - 1], "seq", peer
        )

    def gain_to_shard(k, block, source, peer):
        return transfer(
            mstage.at[block], mland.at[source], csend.at[k - 1], crecv.at[k - 1], "shard", peer
        )

    partner = seq + 1 - 2 * far
    to_pair = transfer(xstage, xland, xsend, xrecv, "seq", partner)

    greet(everyone(seq, me))
    for e in range(LOCAL_EXPERTS):
        for s in range(N_SEQ):
            for copy in weights(e, s):
                copy.start()
    slab_to_ring(0, 0, seq, partner).start()
    for k in (1, 2, 3):
        slab_to_ring(0, k, seq, lax.rem(seq + 2 * k, N_SEQ)).start()
    slab_own = pltpu.make_async_copy(slab_ref, qall_ref.at[seq], own.at[3])
    slab_own.start()

    land_copy = pltpu.make_async_copy(land_ref, land, own.at[4])
    land_copy.start()

    def split(block, e):
        return (
            block.astype(f32)
            .reshape(N_SHARD, LOCAL_EXPERTS, 8, WIDTH)[:, e]
            .reshape(128, WIDTH)
            .astype(bf16)
        )

    def join(first, second):
        halves = [half.astype(f32).reshape(N_SHARD, 1, 8, WIDTH) for half in (first, second)]
        return jnp.concatenate(halves, axis=1).reshape(N_SHARD, 16, WIDTH).astype(bf16)

    def expert(e, x, g, here):
        pre = dot(x, gu[e], NN)
        gate, up = pre[:, :FF], pre[:, FF:]
        sigmoid = jax.nn.sigmoid(gate)
        act = gate * sigmoid
        hidden = (act * up).astype(bf16)
        units = dot(g, dn[e], NT)
        gate_grad = (units * up * sigmoid * (1.0 + gate * (1.0 - sigmoid))).astype(bf16)
        up_grad = (units * act).astype(bf16)
        both = jnp.concatenate([gate_grad, up_grad], axis=1)
        hg[e, here, :] = both
        xt[e, :, here] = x.T
        ht[e, :, here] = hidden.T
        return dot(hidden, dn[e], NN).astype(bf16), dot(both, gu[e], NT).astype(bf16)

    def run_expert(e, low):
        def aligned(n, carry):
            group = pl.ds(n * 8, 8)
            here = pl.ds(pl.multiple_of(n * 256, 256), 256)
            x = land[group, low : low + 32].reshape(256, WIDTH)
            g = gr_ref[group, low : low + 32].reshape(256, WIDTH)
            out, back = expert(e, x, g, here)
            land[group, low : low + 32] = out.reshape(8, 32, WIDTH)
            for m in range(8):
                rows[flat(n * 8 + m, low, low + 32), :] = back[32 * m : 32 * m + 32]
            return carry

        lax.fori_loop(0, 2, aligned, 0)
        g = split(gr_ref[:, 32:48], e)
        gm[e] = g
        out, back = expert(e, split(land[:, 32:48], e), g, slice(512, 640))
        mixed[0, e] = out
        mixed[1, e] = back

    def expert_grads(e):
        low = 48 * e

        def block(h, carry):
            features = pl.ds(pl.multiple_of(h * 512, 512), 512)
            units = pl.ds(pl.multiple_of(h * 256, 256), 256)
            grad = dot(xt[e, features, :], hg[e], NN).astype(bf16)
            part = dot(ht[e, units, :512], gr_ref[:, low : low + 32].reshape(512, WIDTH), NN)
            part = (part + dot(ht[e, units, 512:], gm[e], NN)).astype(bf16)
            for m in range(4):
                k = lax.rem(2 * h + m // 2 + 4 - ring, 4)
                n = lax.rem(m + far, 2)
                dw[e, k, n, :128, :] = grad[128 * m : 128 * m + 128]
                dw[e, k, n, 128:, :] = part[64 * m : 64 * m + 64]
            return carry

        lax.fori_loop(0, 2, block, 0)

    for e in range(LOCAL_EXPERTS):
        for s in range(N_SEQ):
            for copy in weights(e, s):
                copy.wait()
    land_copy.wait()
    run_expert(0, 0)
    for k in range(1, N_SHARD):
        peer = lax.rem(me + k, N_SHARD)
        to_source(0, k, peer, me, peer).start()
    slab_to_ring(0, 0, partner, partner).wait_recv()
    for k in (1, 2, 3):
        slab_to_ring(1, k, partner, lax.rem(seq + 2 * k, N_SEQ)).start()
    run_expert(1, 48)
    land[:, 32:48] = join(mixed[0, 0], mixed[0, 1])
    joined = join(mixed[1, 0], mixed[1, 1])
    for n in range(N_SHARD):
        rows[80 * n + 32 : 80 * n + 48, :] = joined[n]
    for k in range(1, N_SHARD):
        peer = lax.rem(me + k, N_SHARD)
        to_source(1, k, peer, me, peer).start()
    returned[flat(me, 0, 80), :] = rows[flat(me, 0, 80), :]
    normed_copy = pltpu.make_async_copy(normed_ref, gu.at[0], own.at[4])
    normed_copy.start()
    ow_copy = pltpu.make_async_copy(ow_ref, gu.at[1], own.at[0])
    ow_copy.start()
    expert_grads(0)
    for k in (1, 3):
        to_ring(0, k).start()
    expert_grads(1)

    for part in range(2):
        for k in range(1, N_SHARD):
            source = lax.rem(me + N_SHARD - k, N_SHARD)
            to_source(part, k, source, source, source).wait_recv()
    moe_in_grad = dot(pick_ref[...], returned[...], NN)
    residual = res_ref[...]
    inverse = lax.rsqrt(jnp.mean(residual * residual, axis=1, keepdims=True) + epsilon)
    scaled = moe_in_grad * gain_ref[...]
    moe_part = inverse * scaled - residual * (inverse * inverse * inverse) * jnp.mean(
        residual * scaled, axis=1, keepdims=True
    )
    residual_grad = cot_ref[...].astype(f32) + moe_part
    resg_ref[...] = residual_grad
    branch = residual_grad.astype(bf16)
    ow_copy.wait()
    attended_grad = dot(branch, gu[1], NT).astype(bf16)
    for p in range(N_SEQ):
        ags[p] = attended_grad[:, 128 * p : 128 * p + 128]

        @pl.when(seq != p)
        def _(p=p):
            to_head(p).start()

    gl[seq] = ags[seq]
    for part in range(2):
        for k in range(1, N_SHARD):
            peer = lax.rem(me + k, N_SHARD)
            to_source(part, k, peer, me, peer).wait_send()
    for k in range(4):
        block = dot(attp[:, 256 * k : 256 * k + 256].T, branch, NN).reshape(2, N_SHARD, 8, WIDTH)
        for j in range(N_SHARD):
            rows[80 * j + 16 * k : 80 * j + 16 * k + 16, :] = jnp.concatenate(
                [block[0, j], block[1, j]], axis=0
            ).astype(bf16)
    for k in range(1, N_SEQ):
        from_head(lax.rem(seq + k, N_SEQ)).wait_recv()
    for k in (1, 3, 2):
        to_ring(1, k).start()
    to_ring(0, 2).start()
    for k in range(1, N_SHARD):
        peer = lax.rem(me + k, N_SHARD)
        out_to_shard(k, peer, me, peer).start()
    oland[me] = rows[flat(me, 0, 64), :]
    came_own = pltpu.make_async_copy(land.at[me], came_ref.at[me], own.at[0])
    came_own.start()
    fetch(0).start()
    normed_copy.wait()
    qp[...] = jnp.zeros((WIDTH, COLS), f32)

    def begin(i, carry):
        qs[i] = spread(q_ref[i], False)
        gs[i] = spread(gl[i], True)
        product = wide_ref[i] * gl[i].astype(f32).T
        delta_ref[i] = jnp.concatenate(
            [
                jnp.sum(product[:HEAD], axis=0, keepdims=True),
                jnp.sum(product[HEAD:], axis=0, keepdims=True),
            ],
            axis=1,
        )
        dq[i] = jnp.zeros((HEAD, 2 * TOK_DEV), f32)
        return carry

    lax.fori_loop(0, N_SEQ, begin, 0)

    def tile(t, i, n, masked):
        here = slice(n * BWD_TILE, (n + 1) * BWD_TILE)
        memory = mbuf[lax.rem(t, 2), 8 * n : 8 * n + 8].reshape(BWD_TILE, 2 * HEAD)
        scores = dot(memory, qs[i], NT)
        weight = jnp.exp(scores - lse_ref[i])
        if masked:
            weight = jnp.where(admitted(scores.shape, me, n * BWD_TILE), weight, 0.0)
        weight_grad = dot(memory, gs[i], NT)
        score_grad = (weight * (weight_grad - delta_ref[i])).astype(bf16)
        here_grad = dot(weight.astype(bf16), gs[i], NN) + dot(score_grad, qs[i], NN)
        if masked:
            acc[here, :] = here_grad
        else:
            acc[here, :] += here_grad
        dq[i] += dot(kt[:, here], score_grad, NN)

    def turned(grad, n, t):
        cosine, sine = cos_ref[t], sin_ref[t]
        if n:
            key = lax.broadcasted_iota(jnp.int32, cosine.shape, 1) < HEAD
            cosine = jnp.where(key, cosine, 1.0)
            sine = jnp.where(key, sine, 0.0)
        other = dot(grad, turn_ref[n], NT)
        return (grad.astype(f32) * cosine + other * sine).astype(bf16)

    def chip_sum(t):
        slot = lax.rem(t, 4)

        @pl.when(t >= 4)
        def _():
            for k in range(1, N_SHARD // 2):
                peer = lax.rem(chip + k, N_SHARD // 2)
                to_owner(t - 4, k, peer, chip, peer).wait_send()

        to_core(t).wait_recv()
        total = stage[slot, :, core].astype(f32) + cland[slot].astype(f32)
        cstage[slot] = total.astype(bf16)
        dl[t, chip] = cstage[slot, chip]
        for k in range(1, N_SHARD // 2):
            peer = lax.rem(chip + k, N_SHARD // 2)
            to_owner(t, k, peer, chip, peer).start()

    def token_gradient(t):
        for k in range(1, N_SHARD // 2):
            source = lax.rem(chip + N_SHARD // 2 - k, N_SHARD // 2)
            to_owner(t, k, source, source, source).wait_recv()
        grad = jnp.sum(dl[t].astype(f32), axis=0).astype(bf16)
        pg[t, :, 2 * HEAD :] = turned(grad, 1, t)
        grad = pg[t]

        @pl.when(t != seq)
        def _():
            to_token(t, seq).start()

        tokens = pl.ds(pl.multiple_of(t * 128, 128), 128)
        qp[...] += dot(gu[0, tokens, :].T, grad, NN)

    def sum_weights():
        for k in range(1, N_SHARD):
            peer = lax.rem(me + k, N_SHARD)
            out_to_shard(k, peer, me, peer).wait_send()
        for e in range(LOCAL_EXPERTS):
            for k in (1, 2, 3):
                to_ring(e, k).wait()
        back = []
        for e, buffer in enumerate((rows, returned)):
            for k in range(3):
                for n in range(2):
                    index = 2 * k + n
                    back.append(
                        pltpu.make_async_copy(
                            kz_ref.at[e, k, n],
                            buffer.at[192 * index : 192 * index + 192],
                            wsem.at[e, index, 0],
                        )
                    )
                    back[-1].start()
        for copy in back:
            copy.wait()
        for e, buffer in enumerate((rows, returned)):
            for n in range(2):
                total = dw[e, 0, n].astype(f32)
                for k in range(3):
                    index = 2 * k + n
                    total += buffer[192 * index : 192 * index + 192, :].astype(f32)
                if n == 0:
                    sums_ref[e] = total
                else:
                    xstage[e] = total.astype(bf16)
        to_pair.start()
        for k in range(1, N_SHARD):
            source = lax.rem(me + N_SHARD - k, N_SHARD)
            out_to_shard(k, source, source, source).wait_recv()
        osum[...] = jnp.sum(oland[...].astype(f32), axis=0).reshape(N_SEQ, 8, WIDTH)
        for p in range(N_SEQ):

            @pl.when(seq != p)
            def _(p=p):
                out_to_seq(p).start()

        oseq[seq] = osum[seq]

    def step(t, carry):
        fetch(t).wait()

        @pl.when(t + 1 < N_SEQ)
        def _():
            fetch(t + 1).start()

        @pl.when(t >= 1)
        def _():
            chip_sum(t - 1)

        @pl.when(t >= 3)
        def _():
            token_gradient(t - 3)

        for n in range(5):

            @pl.when(t == n + 1)
            def _(n=n):
                for k in range(1, 4):
                    to_token_expert(3 * n + k).start()

        @pl.when(t == N_SEQ - 2)
        def _():
            sum_weights()

        for n in range(4):
            block = mbuf[lax.rem(t, 2), 4 * n : 4 * n + 4].reshape(512, 2 * HEAD)
            kt[:, 512 * n : 512 * n + 512] = block.T[:HEAD]
        tile(t, t, 0, True)
        tile(t, t, 1, True)
        grad = dq[t] * (1.0 / math.sqrt(HEAD))
        grad = jnp.concatenate([grad[:, :TOK_DEV], grad[:, TOK_DEV:]], axis=0).T.astype(bf16)
        pg[t, :, : 2 * HEAD] = turned(grad, 0, t)

        def rest(i, inner):
            tile(t, i, 0, False)
            tile(t, i, 1, False)
            return inner

        lax.fori_loop(t + 1, N_SEQ, rest, 0)

        @pl.when(t >= 4)
        def _():
            to_core(t - 4).wait_send()

        slot = lax.rem(t, 4)
        for n in range(4):
            block = acc[512 * n : 512 * n + 512, :].astype(bf16)
            stage[slot, 2 * n : 2 * n + 2] = block.reshape(2, 2, TOK_DEV, 2 * HEAD)
        to_core(t).start()
        return carry

    lax.fori_loop(0, N_SEQ, step, 0)

    chip_sum(N_SEQ - 1)
    for t in (3, 2, 1):
        token_gradient(N_SEQ - t)
    own_token = pltpu.make_async_copy(pg.at[seq], tok_ref.at[seq], own.at[1])
    own_token.start()
    split_rows = qp[...].reshape(N_SEQ, N_SHARD, 8, COLS)
    for j in range(N_SHARD):
        qstage[j] = split_rows[:, j].reshape(64, COLS).astype(bf16)
    for k in range(1, N_SHARD):
        peer = lax.rem(me + k, N_SHARD)
        qkv_to_shard(k, peer, me, peer).start()
    qland[me] = qstage[me]
    for k in range(1, N_SHARD):
        source = lax.rem(me + N_SHARD - k, N_SHARD)
        qkv_to_shard(k, source, source, source).wait_recv()
    qsum[...] = jnp.sum(qland[...].astype(f32), axis=0).reshape(N_SEQ, 8, COLS)
    for k in range(1, N_SEQ):
        peer = lax.rem(seq + k, N_SEQ)
        qkv_to_seq(k, peer, seq, peer).start()
    own_qkv = pltpu.make_async_copy(qsum.at[seq], qkv_ref.at[seq], own.at[2])
    own_qkv.start()

    to_pair.wait()
    gain = jnp.zeros((128, 128), f32)
    for e in range(LOCAL_EXPERTS):
        sums_ref[e] += xland[e].astype(f32)
        product = pack_ref[e, :128].astype(f32) * sums_ref[e, :128]
        for c in range(8):
            gain += product[:, 128 * c : 128 * c + 128]
    gain = jnp.sum(gain, axis=1, keepdims=True) / gcol_ref[...]
    mstage[...] = gain.reshape(N_SHARD, 8, 128)
    for k in range(1, N_SHARD):
        peer = lax.rem(me + k, N_SHARD)
        gain_to_shard(k, peer, me, peer).start()
    mland[me] = mstage[me]
    for k in range(1, N_SEQ):
        out_from_seq(lax.rem(seq + k, N_SEQ)).wait_recv()
    wout_ref[...] = jnp.sum(oseq[...], axis=0)
    for k in range(1, N_SHARD):
        source = lax.rem(me + N_SHARD - k, N_SHARD)
        gain_to_shard(k, source, source, source).wait_recv()
    mgain_ref[...] = jnp.sum(mland[...], axis=0)

    for p in range(N_SEQ):

        @pl.when(seq != p)
        def _(p=p):
            to_head(p).wait_send()
            out_to_seq(p).wait_send()

    for k in range(1, N_SHARD):
        to_token_expert(k).wait()
        peer = lax.rem(me + k, N_SHARD)
        qkv_to_shard(k, peer, me, peer).wait_send()
        gain_to_shard(k, peer, me, peer).wait_send()

    def end(t, carry):
        for k in range(1, N_SHARD // 2):
            peer = lax.rem(chip + k, N_SHARD // 2)
            to_owner(t, k, peer, chip, peer).wait_send()
        to_core(t).wait_send()
        return carry

    lax.fori_loop(4, N_SEQ, end, 0)
    for k in range(1, N_SEQ):
        peer = lax.rem(seq + k, N_SEQ)
        to_token(peer, seq).wait_send()
        to_token(peer, peer).wait_recv()
        qkv_to_seq(k, peer, seq, peer).wait_send()
        source = lax.rem(seq + N_SEQ - k, N_SEQ)
        qkv_to_seq(k, source, source, source).wait_recv()
    slab_to_ring(0, 0, seq, partner).wait_send()
    for k in (1, 2, 3):
        for n, block in enumerate((seq, partner)):
            slab_to_ring(n, k, block, lax.rem(seq + 2 * k, N_SEQ)).wait_send()
            source = lax.rem(block + N_SEQ - 2 * k, N_SEQ)
            slab_to_ring(n, k, source, lax.rem(seq + N_SEQ - 2 * k, N_SEQ)).wait_recv()
    for copy in (own_token, own_qkv, came_own, slab_own):
        copy.wait()


def late(operands, ident):
    dma = pltpu.SemaphoreType.DMA
    vmem = pl.BlockSpec(memory_space=pltpu.VMEM)
    wide = jax.ShapeDtypeStruct((TOK_DEV, WIDTH), f32)
    routed = (N_SHARD, 80, WIDTH)
    grads = (LOCAL_EXPERTS, 2, 192, WIDTH)
    shapes = [
        ((LOCAL_EXPERTS, WIDTH, 2 * FF), bf16),
        ((LOCAL_EXPERTS, FF, WIDTH), bf16),
        (routed, bf16),
        ((N_SHARD * 80, WIDTH), bf16),
        ((N_SHARD * 80, WIDTH), bf16),
        ((LOCAL_EXPERTS, WIDTH, EXPERT_ROWS), bf16),
        ((LOCAL_EXPERTS, FF, EXPERT_ROWS), bf16),
        ((LOCAL_EXPERTS, EXPERT_ROWS, 2 * FF), bf16),
        ((LOCAL_EXPERTS, 128, WIDTH), bf16),
        ((2, LOCAL_EXPERTS, 128, WIDTH), bf16),
        ((LOCAL_EXPERTS, 4, 2, 192, WIDTH), bf16),
        ((N_SEQ, TOK_DEV, 128), bf16),
        ((LOCAL_EXPERTS, 192, WIDTH), bf16),
        ((N_SEQ, TOK_DEV, 2 * HEAD), bf16),
        ((N_SEQ, 2 * TOK_DEV, 2 * HEAD), bf16),
        ((N_SEQ, 2 * TOK_DEV, 2 * HEAD), bf16),
        ((N_SEQ, 1, 2 * TOK_DEV), f32),
        ((HEAD, SUPER), bf16),
        ((SUPER, 2 * HEAD), f32),
        ((N_SEQ, HEAD, 2 * TOK_DEV), f32),
        ((4, N_SHARD // 2, 2, TOK_DEV, 2 * HEAD), bf16),
        ((N_SEQ, N_SHARD // 2, TOK_DEV, 2 * HEAD), bf16),
        ((2, N_SHARD, TOK_DEV, 2 * HEAD), bf16),
        ((N_SEQ, TOK_DEV, COLS), bf16),
        ((WIDTH, COLS), f32),
        ((N_SHARD, 64, COLS), bf16),
        ((N_SHARD, 64, COLS), bf16),
        ((N_SEQ, 8, COLS), f32),
        ((N_SEQ, 8, WIDTH), f32),
        ((LOCAL_EXPERTS, 192, WIDTH), bf16),
        ((N_SHARD, 64, WIDTH), bf16),
        ((N_SHARD, 8, 128), f32),
        ((N_SHARD, 8, 128), f32),
        ((4, N_SHARD // 2, TOK_DEV, 2 * HEAD), bf16),
        ((4, N_SHARD // 2, TOK_DEV, 2 * HEAD), bf16),
        ((N_SEQ, 8, WIDTH), f32),
    ]
    shards = (N_SHARD - 1,)
    counts = [(LOCAL_EXPERTS, N_SEQ, 2)]
    counts += [(2,) + shards] * 2
    counts += [(LOCAL_EXPERTS, 3)] * 2 + [shards] * 2
    counts += [(N_SEQ, N_SHARD // 2 - 1)] * 2 + [(N_SEQ,)] * 2 + [shards] * 2 + [(N_SEQ,)] * 2
    counts += [(5,), (2,)] + [shards] * 2 + [(N_SEQ - 1,)] * 2
    semaphores = [dma(count) for count in counts] + [dma, dma]
    semaphores += [dma(shards)] * 2 + [dma((N_SEQ,))] * 4 + [dma((2, 4))] * 2
    return pl.pallas_call(
        late_kernel,
        in_specs=[vmem, ANY] + [vmem] * 4 + [ANY, vmem, ANY] + [vmem] * 3 + [ANY] + [vmem] * 3 + [ANY] * 2 + [vmem] * 2,
        out_specs=[vmem, ANY, ANY, vmem, ANY, vmem, vmem, ANY, ANY],
        out_shape=[
            wide,
            jax.ShapeDtypeStruct((N_SEQ, TOK_DEV, COLS), bf16),
            jax.ShapeDtypeStruct(routed, bf16),
            jax.ShapeDtypeStruct((LOCAL_EXPERTS, 192, WIDTH), f32),
            jax.ShapeDtypeStruct((N_SEQ, 8, COLS), f32),
            jax.ShapeDtypeStruct((8, WIDTH), f32),
            jax.ShapeDtypeStruct((8, 128), f32),
            jax.ShapeDtypeStruct((LOCAL_EXPERTS, 3, 2, 192, WIDTH), bf16),
            jax.ShapeDtypeStruct((N_SEQ, 128, 2 * WIDTH), bf16),
        ],
        scratch_shapes=[pltpu.VMEM(*shape) for shape in shapes] + semaphores,
        compiler_params=pltpu.CompilerParams(
            collective_id=ident, has_side_effects=True, vmem_limit_bytes=LIMIT << 20
        ),
        name="experts_attention_backward",
    )(*operands)


def group_columns(rows):
    lead = rows.shape[:-1]
    queries = rows[..., : HEADS * HEAD].reshape(lead + (N_SEQ, 2 * HEAD))
    keys = rows[..., HEADS * HEAD : (HEADS + KV) * HEAD].reshape(lead + (N_SEQ, HEAD))
    values = rows[..., (HEADS + KV) * HEAD :].reshape(lead + (N_SEQ, HEAD))
    return jnp.concatenate([queries, keys, values], axis=-1)


def ungroup_columns(groups):
    rows = groups.shape[0]
    return jnp.concatenate(
        [
            groups[:, :, : 2 * HEAD].reshape(rows, HEADS * HEAD),
            groups[:, :, 2 * HEAD : 3 * HEAD].reshape(rows, KV * HEAD),
            groups[:, :, 3 * HEAD :].reshape(rows, KV * HEAD),
        ],
        axis=1,
    )


def rope_pair(shard):
    half = HEAD // 2
    frequency = jnp.exp(
        jnp.arange(half, dtype=f32) * jnp.float32(-2.0 * math.log(rope_base) / HEAD)
    )
    chunk = jnp.arange(N_SEQ, dtype=jnp.int32)[:, None] * N_SHARD + shard
    position = chunk * TOK_DEV + jnp.arange(TOK_DEV, dtype=jnp.int32)[None, :]
    angles = position[:, :, None].astype(f32) * frequency[None, None, :]
    cosine, sine = lax.optimization_barrier((jnp.cos(angles), jnp.sin(angles)))
    return jnp.tile(cosine, (1, 1, 4)), jnp.tile(sine, (1, 1, 4))


def turn_matrix():
    row = jnp.arange(COLS, dtype=jnp.int32)[:, None]
    col = jnp.arange(COLS, dtype=jnp.int32)[None, :]
    half = HEAD // 2
    low = col % HEAD < half
    minus = low & (row == col + half) & (col < 3 * HEAD)
    plus = (~low) & (row == col - half) & (col < 3 * HEAD)
    return (plus.astype(f32) - minus.astype(f32)).astype(bf16)


def routing(routes, route_weights):
    ids = jnp.arange(EXPERTS, dtype=jnp.int32)
    hit = routes[:, :, None] == ids[None, None, :]
    mask = jnp.sum(hit.astype(f32), axis=1)
    weight = jnp.sum(jnp.where(hit, route_weights[:, :, None], 0.0), axis=1)
    token = jnp.arange(TOK_DEV, dtype=jnp.int32)
    earlier = (token[:, None] > token[None, :]).astype(bf16)
    before = dot(earlier, mask.astype(bf16), NN)
    code = jnp.where(mask > 0.0, before, -1.0).astype(bf16)
    place = jnp.arange(N_SHARD * 80, dtype=jnp.int32)
    row = place % 80
    slot = jnp.where(row < 40, row, jnp.where(row < 48, row - 8, row - 48))
    owner = place // 80 * LOCAL_EXPERTS + (row >= 40).astype(jnp.int32)
    widen = (owner[None, :] == ids[:, None]).astype(bf16)
    pick = dot(code, widen, NN) == slot.astype(f32)[None, :]
    high = weight.astype(bf16)
    low = (weight - high.astype(f32)).astype(bf16)
    high = jnp.where(pick, dot(high, widen, NN), 0.0)
    low = jnp.where(pick, dot(low, widen, NN), 0.0)
    return pick.astype(bf16), high.astype(bf16), low.astype(bf16), jnp.sum(high + low, axis=0)


def on_device(
    layer_input,
    attn_gain,
    moe_gain,
    w_qkv,
    w_out,
    w_gate,
    w_up,
    w_down,
    routes,
    route_weights,
    cotangent,
):
    seq = lax.axis_index("seq")
    shard = lax.axis_index("shard")

    pick, scale_high, scale_low, slot_scale = routing(routes, route_weights)
    pick_turned = pick.T
    grad_send = (slot_scale[:, None] * dot(pick_turned, cotangent, NN)).astype(bf16)

    grouped = group_columns(w_qkv)
    pieces = grouped.reshape(8, N_SEQ, 2, 128).transpose(1, 2, 0, 3)
    gains = jnp.concatenate([attn_gain, moe_gain, jnp.zeros((112,), bf16)])
    gains = jnp.broadcast_to(gains[None, None, :], (N_SEQ, 16, 128))
    pieces = jnp.concatenate([pieces.reshape(N_SEQ, 16, 128), gains], axis=1)
    tokens, columns, out_slabs = first_gather(
        layer_input.reshape(8, TOK_DEV // 8, WIDTH), pieces, w_out, 1
    )
    expert_pack = jnp.concatenate(
        [jnp.concatenate([w_gate, w_up], axis=2), w_down], axis=1
    )
    expert_weights = lax.all_gather(
        lax.optimization_barrier((expert_pack, tokens))[0], "seq", axis=1
    )
    gain_rows = columns[:, N_SEQ, :8, :16].transpose(1, 0, 2)
    gain_attn = gain_rows[:, :, :8].reshape(WIDTH).astype(f32)
    gain_moe = gain_rows[:, :, 8:].reshape(WIDTH).astype(f32)
    cosine, sine = rope_pair(shard)
    turn = turn_matrix()
    (
        queries,
        attended_wide,
        lse,
        attended,
        residual,
        normed,
        memory,
        qkv_slab,
        out_weight,
        expert_rows,
        grad_rows,
    ) = attention(
        (
            tokens.reshape(HEAD_ROWS, WIDTH),
            columns[:, :N_SEQ],
            gain_attn[None, :],
            cosine,
            sine,
            turn,
            out_slabs.reshape(128, WIDTH),
            grouped.reshape(8, 2 * WIDTH),
            layer_input,
            gain_moe[None, :],
            pick_turned,
            grad_send.reshape(N_SHARD, 80, WIDTH),
        ),
        2,
    )
    left = jnp.arange(2 * HEAD, dtype=jnp.int32) < HEAD
    turns = turn[:128, :128]
    turns = jnp.stack([turns, jnp.where(left[:, None] & left[None, :], turns, 0)])
    gain_here = lax.dynamic_slice_in_dim(gain_moe, seq * 128, 128)
    (
        residual_grad,
        token_grad,
        came_back,
        expert_sums,
        qkv_groups,
        out_weight_grad,
        moe_gain_grad,
        _,
        qkv_all,
    ) = late(
        (
            attended,
            out_weight.reshape(WIDTH, WIDTH),
            residual,
            cotangent,
            gain_moe[None, :],
            pick,
            expert_rows,
            grad_rows,
            expert_weights,
            queries,
            attended_wide,
            lse,
            memory,
            cosine,
            sine,
            turns,
            normed,
            qkv_slab.reshape(128, 2 * WIDTH),
            expert_pack,
            jnp.broadcast_to(gain_here[:, None], (128, 128)),
        ),
        3,
    )
    came_back = came_back.reshape(N_SHARD * 80, WIDTH)
    x_wide = layer_input.astype(f32)
    moe_sum = dot(scale_high, came_back, NN) + dot(scale_low, came_back, NN)
    block_out = (residual + moe_sum).astype(bf16)

    qkv_groups = qkv_groups.transpose(1, 0, 2)
    attn_gain_grad = jnp.sum(grouped.astype(f32) * qkv_groups, axis=(1, 2)) / attn_gain.astype(f32)
    qkv_weight_grad = ungroup_columns(qkv_groups)

    token_grad = token_grad.transpose(1, 0, 2).reshape(TOK_DEV, 2 * WIDTH)
    normed_grad = dot(token_grad, qkv_all.reshape(WIDTH, 2 * WIDTH), NT)
    inverse_one = lax.rsqrt(jnp.mean(x_wide * x_wide, axis=1, keepdims=True) + epsilon)
    scaled = normed_grad * gain_attn
    attn_part = inverse_one * scaled - x_wide * inverse_one**3 * jnp.mean(
        x_wide * scaled, axis=1, keepdims=True
    )
    input_grad = (residual_grad + attn_part).astype(bf16)
    return (
        block_out,
        input_grad,
        attn_gain_grad,
        moe_gain_grad[:, 0],
        qkv_weight_grad,
        out_weight_grad,
        expert_sums[:, :128, :FF],
        expert_sums[:, :128, FF:],
        expert_sums[:, 128:],
    )


def solution(mesh):
    token = P(("seq", "shard"), None)
    vector = P(("seq", "shard"))
    expert = P("shard", "seq", None)
    return jax.shard_map(
        on_device,
        mesh=mesh,
        in_specs=(
            token,
            vector,
            vector,
            token,
            token,
            expert,
            expert,
            expert,
            token,
            token,
            token,
        ),
        out_specs=(token, token, vector, vector, token, token, expert, expert, expert),
        check_vma=False,
    )
```

```python
import functools
import math

import jax
import jax.numpy as jnp
from jax import lax
from jax.experimental import pallas as pl
from jax.experimental.pallas import tpu as pltpu
from jax.sharding import PartitionSpec as P

HEADS = 16
KV = 8
HEAD = 64
EXPERTS = 32
TOPK = 8
TOK_DEV = 128
CAP = 40
WIDTH = 1024
FF = 512
N_SEQ = 8
N_SHARD = 16
HEAD_ROWS = TOK_DEV * N_SEQ
TOKENS = TOK_DEV * N_SEQ * N_SHARD
LOCAL_EXPERTS = EXPERTS // N_SHARD
EXPERT_ROWS = N_SHARD * CAP
COLS = 256
SUPER = TOK_DEV * N_SHARD
BWD_TILE = 1024
LIMIT = 63
STAGE = 3

epsilon = 1e-06
rope_base = 10000.0

f32 = jnp.float32
bf16 = jnp.bfloat16
MESH = pl.DeviceIdType.MESH
ANY = pl.BlockSpec(memory_space=pl.ANY)
NT = (((1,), (1,)), ((), ()))
NN = (((1,), (0,)), ((), ()))
TN = (((0,), (0,)), ((), ()))


def dot(left, right, dims):
    return lax.dot_general(left, right, dims, preferred_element_type=f32)


def greet(peers):
    barrier = pltpu.get_barrier_semaphore()
    for axis, peer in peers:
        pl.semaphore_signal(barrier, inc=1, device_id={axis: peer}, device_id_type=MESH)
    pl.semaphore_wait(barrier, len(peers))


def remote(source, target, send, recv, axis, peer):
    copy = pltpu.make_async_remote_copy(
        src_ref=source,
        dst_ref=target,
        send_sem=send,
        recv_sem=recv,
        device_id={axis: peer},
        device_id_type=MESH,
    )
    copy.start()
    return copy


def staged(axis, units, share, x_ref, place, sem_send, sem_recv, own):
    me = lax.axis_index(axis)
    cores = 2 if axis == "shard" else 1
    core = lax.rem(me, cores)
    pair = lax.rem(me // cores, 2)
    ring = me // (2 * cores)

    def at(r, p, c):
        return (r * 2 + p) * cores + c

    ring_peer = [at(lax.rem(ring + k, 4), pair, core) for k in (1, 2, 3)]
    ring_from = [lax.rem(ring + 4 - k, 4) for k in (1, 2, 3)]
    pair_peer = at(ring, 1 - pair, core)
    core_peer = at(ring, pair, 1 - core)
    mine = pltpu.make_async_copy(x_ref, place(me, 0, units), own)
    mine.start()
    sends = []

    def go(source, index, low, high, peer):
        n = len(sends)
        sends.append(
            remote(source, place(index, low, high), sem_send.at[n], sem_recv.at[n], axis, peer)
        )
        return sends[-1]

    to_pair = go(x_ref, me, 0, units, pair_peer)
    to_ring = [go(x_ref, me, 0, units, peer) for peer in ring_peer]
    landed = []
    if cores == 2:
        landed.append(go(x_ref, me, 0, units, core_peer))

    def pass_core(index, low, high):
        if cores == 2:
            landed.append(go(place(index, low, high), index, low, high, core_peer))

    to_pair.wait_recv()
    fwd_ring = [
        go(place(pair_peer, 0, share), pair_peer, 0, share, peer) for peer in ring_peer
    ]
    pass_core(pair_peer, 0, units)
    fwd_pair = []
    for k in (0, 2, 1):
        to_ring[k].wait_recv()
        source = at(ring_from[k], pair, core)
        if share < units:
            fwd_pair.append((k, go(place(source, share, units), source, share, units, pair_peer)))
        pass_core(source, 0, units)
    for k in (0, 2, 1):
        fwd_ring[k].wait_recv()
        pass_core(at(ring_from[k], 1 - pair, core), 0, share)
    for k, copy in fwd_pair:
        copy.wait_recv()
        pass_core(at(ring_from[k], 1 - pair, core), share, units)
    for copy in landed:
        copy.wait_recv()
    mine.wait()
    for copy in sends:
        copy.wait_send()


def first_kernel(
    x_ref, w_ref, v_ref, xo_ref, wo_ref, vo_ref, w_mid, w_pack, send, recv, own, wsend, wrecv, wown, vown
):
    seq = lax.axis_index("seq")
    shard = lax.axis_index("shard")
    greet(
        [("seq", lax.rem(seq + k, N_SEQ)) for k in range(1, N_SEQ)]
        + [("shard", lax.rem(shard + k, N_SHARD)) for k in range(1, N_SHARD)]
    )
    mine = pltpu.make_async_copy(w_ref.at[seq], w_mid.at[seq], wown)
    mine.start()
    slab = pltpu.make_async_copy(v_ref, vo_ref.at[shard], vown)
    slab.start()
    pieces = []
    for k in range(1, N_SEQ):
        peer = lax.rem(seq + k, N_SEQ)
        pieces.append(
            remote(w_ref.at[peer], w_mid.at[seq], wsend.at[k - 1], wrecv.at[k - 1], "seq", peer)
        )
    rows = []
    for k in range(1, N_SHARD):
        peer = lax.rem(shard + k, N_SHARD)
        n = 21 + k
        rows.append(
            remote(v_ref, vo_ref.at[shard], wsend.at[n], wrecv.at[n], "shard", peer)
        )
    mine.wait()
    for piece in pieces:
        piece.wait()
    packed = jnp.zeros((16, 128), f32)
    row = lax.broadcasted_iota(jnp.int32, (16, 128), 0)
    for s in range(N_SEQ):
        packed = jnp.where(row == s, w_mid[s, 16:].astype(f32), packed)
        w_pack[s] = w_mid[s, :16]
    w_pack[N_SEQ] = packed.astype(bf16)
    mine = pltpu.make_async_copy(w_pack, wo_ref.at[shard], wown)
    mine.start()
    pieces = []
    for k in range(1, N_SHARD):
        peer = lax.rem(shard + k, N_SHARD)
        n = 6 + k
        pieces.append(
            remote(w_pack, wo_ref.at[shard], wsend.at[n], wrecv.at[n], "shard", peer)
        )
    staged("seq", 8, 4, x_ref, lambda s, low, high: xo_ref.at[s, low:high], send, recv, own)
    slab.wait()
    for row in rows:
        row.wait()
    mine.wait()
    for piece in pieces:
        piece.wait()


def first_gather(x, pieces, rows, ident):
    return pl.pallas_call(
        first_kernel,
        out_shape=[
            jax.ShapeDtypeStruct((N_SEQ, 8, TOK_DEV // 8, WIDTH), bf16),
            jax.ShapeDtypeStruct((N_SHARD, N_SEQ + 1, 16, 128), bf16),
            jax.ShapeDtypeStruct((N_SHARD,) + rows.shape, bf16),
        ],
        in_specs=[ANY, ANY, ANY],
        out_specs=[ANY, ANY, ANY],
        scratch_shapes=[
            pltpu.VMEM(pieces.shape, bf16),
            pltpu.VMEM((N_SEQ + 1, 16, 128), bf16),
            pltpu.SemaphoreType.DMA((12,)),
            pltpu.SemaphoreType.DMA((12,)),
            pltpu.SemaphoreType.DMA,
            pltpu.SemaphoreType.DMA((38,)),
            pltpu.SemaphoreType.DMA((38,)),
            pltpu.SemaphoreType.DMA,
            pltpu.SemaphoreType.DMA,
        ],
        compiler_params=pltpu.CompilerParams(collective_id=ident, has_side_effects=True),
        name="gather_tokens",
    )(x, pieces, rows)


def spread(rows, right):
    zeros = jnp.zeros((TOK_DEV, HEAD), rows.dtype)
    parts = [rows[:, :HEAD], rows[:, HEAD:]]
    if right:
        parts = [jnp.concatenate([zeros, part], axis=1) for part in parts]
    else:
        parts = [jnp.concatenate([part, zeros], axis=1) for part in parts]
    return jnp.concatenate(parts, axis=0)


def admitted(shape, j, first_key):
    key_pos = first_key + lax.broadcasted_iota(jnp.int32, shape, 0)
    query_pos = j * TOK_DEV + (lax.broadcasted_iota(jnp.int32, shape, 1) & (TOK_DEV - 1))
    return query_pos >= key_pos


def transfer(source, target, send, recv, axis, peer):
    return pltpu.make_async_remote_copy(
        src_ref=source,
        dst_ref=target,
        send_sem=send,
        recv_sem=recv,
        device_id={axis: peer},
        device_id_type=MESH,
    )


def everyone(seq, shard):
    return [("seq", lax.rem(seq + k, N_SEQ)) for k in range(1, N_SEQ)] + [
        ("shard", lax.rem(shard + k, N_SHARD)) for k in range(1, N_SHARD)
    ]


def attention_kernel(*refs):
    (x_ref, cols_ref, gain_ref, cos_ref, sin_ref, turn_ref, slab_ref, rows_ref) = refs[:8]
    (own_ref, gain2_ref, pickt_ref, cot_ref, pack_ref) = refs[8:13]
    (q_ref, wide_ref, lse_ref, attp_ref, res_ref) = refs[13:18]
    (norm_ref, mem_ref, rows_out, ow_ref, land_ref, cot_out, pack_out) = refs[18:25]
    (land, vt, heads, peak_ref, total_ref, acc_ref, att, ow, weights_ref, norm, rows) = refs[25:36]
    (ksend, krecv, gsend, grecv, esend, erecv, fsend, frecv, hsend, hrecv, own, msem) = refs[36:48]
    dsend, drecv, psend, precv = refs[48:]
    seq = lax.axis_index("seq")
    me = lax.axis_index("shard")
    core = lax.rem(me, 2)
    pair = lax.rem(me // 2, 2)
    ring = me // 4
    far = lax.rem(seq, 2)
    partner = seq + 1 - 2 * far

    def at(k, other_pair, other_core):
        p = 1 - pair if other_pair else pair
        c = 1 - core if other_core else core
        return (lax.rem(ring + 4 + k, 4) * 2 + p) * 2 + c

    def message(t, m, block, peer):
        return transfer(
            land.at[t, block], land.at[t, block], ksend.at[t, m], krecv.at[t, m], "shard", peer
        )

    def first(t):
        for k in (1, 2, 3):
            message(t, k - 1, me, at(k, 0, 0)).start()
        message(t, 3, me, at(0, 1, 0)).start()
        message(t, 4, me, at(0, 0, 1)).start()

    def second(t):
        block = at(0, 1, 0)
        message(t, 3, block, block).wait_recv()
        for k in (1, 2, 3):
            message(t, 4 + k, block, at(k, 0, 0)).start()
        message(t, 8, block, at(0, 0, 1)).start()
        for k in (1, 2, 3):
            block = at(-k, 0, 0)
            message(t, k - 1, block, block).wait_recv()
            message(t, 8 + k, block, at(0, 0, 1)).start()

    def third(t):
        for k in (1, 2, 3):
            block = at(-k, 1, 0)
            message(t, 4 + k, block, at(-k, 0, 0)).wait_recv()
            message(t, 11 + k, block, at(0, 0, 1)).start()

    def fourth(t):
        peer = at(0, 0, 1)
        message(t, 4, peer, peer).wait_recv()
        message(t, 8, at(0, 1, 1), peer).wait_recv()
        for k in (1, 2, 3):
            message(t, 8 + k, at(-k, 0, 1), peer).wait_recv()
            message(t, 11 + k, at(-k, 1, 1), peer).wait_recv()

    def to_shard(k):
        peer = lax.rem(me + k, N_SHARD)
        return transfer(
            rows_ref, rows_out.at[me], esend.at[k - 1], erecv.at[k - 1], "shard", peer
        )

    def slab_to_ring(n, k, block, peer):
        source = slab_ref if n == 0 else ow.at[block]
        return transfer(source, ow.at[block], fsend.at[n, k], frecv.at[n, k], "seq", peer)

    def pack_to_ring(n, k, block, peer):
        target = pack_out.at[block] if n == 0 else pack_out.at[block, n - 1]
        source = pack_ref if n == 0 else target
        return transfer(source, target, psend.at[n, k], precv.at[n, k], "seq", peer)

    def grads_to_expert(k):
        peer = lax.rem(me + k, N_SHARD)
        return transfer(
            cot_ref.at[peer], cot_out.at[me], dsend.at[k - 1], drecv.at[k - 1], "shard", peer
        )

    def to_expert(k):
        peer = lax.rem(me + k, N_SHARD)
        here = pl.ds(pl.multiple_of(peer * 80, 16), 80)
        return transfer(
            rows.at[here], land_ref.at[me], hsend.at[k - 1], hrecv.at[k - 1], "shard", peer
        )

    def to_token(t, source):
        return transfer(
            heads.at[t], att.at[source], gsend.at[t], grecv.at[source], "seq", t
        )

    greet(everyone(seq, me))

    for half in range(2):
        block = cols_ref[:, :N_SEQ].astype(f32).reshape(N_SHARD, N_SEQ, 2, 8, 128)[:, :, half]
        block = jnp.swapaxes(block, 0, 1).reshape(WIDTH, 128).astype(bf16)
        weights_ref[:, 128 * half : 128 * half + 128] = block
    weights_ref[:, COLS:] = dot(weights_ref[:, :COLS], turn_ref[...], NN).astype(bf16)
    key = lax.broadcasted_iota(jnp.int32, (TOK_DEV, 2 * HEAD), 1) < HEAD

    def project(n, carry):
        here = pl.ds(pl.multiple_of(n * 512, 512), 512)
        x = x_ref[here, :].astype(f32)
        inverse = lax.rsqrt(jnp.mean(x * x, axis=1, keepdims=True) + epsilon)
        normed = (x * inverse * gain_ref[...]).astype(bf16)
        norm[here, :] = normed
        wide = dot(normed, weights_ref[...], NN).reshape(4, TOK_DEV, 2 * COLS)
        for m in range(4):
            t = 4 * n + m
            cosine, sine = cos_ref[t], sin_ref[t]
            query = wide[m, :, :128] * cosine + wide[m, :, 256:384] * sine
            q_ref[t] = query.astype(bf16) * jnp.bfloat16(1.0 / math.sqrt(HEAD))
            cosine, sine = jnp.where(key, cosine, 1.0), jnp.where(key, sine, 0.0)
            memory = wide[m, :, 128:256] * cosine + wide[m, :, 384:] * sine
            land[t, me] = memory.astype(bf16)
        return carry

    lax.fori_loop(0, 2, project, 0)
    norm_own = pltpu.make_async_copy(norm, norm_ref, own.at[3])
    norm_own.start()
    cot_own = pltpu.make_async_copy(cot_ref.at[me], cot_out.at[me], own.at[4])
    cot_own.start()

    def begin(t, carry):
        first(t)
        peak_ref[t] = jnp.full((1, 2 * TOK_DEV), -1e30, f32)
        total_ref[t] = jnp.zeros((1, 2 * TOK_DEV), f32)
        acc_ref[t] = jnp.zeros((HEAD, 2 * TOK_DEV), f32)
        return carry

    lax.fori_loop(0, N_SEQ, begin, 0)
    second(0)
    third(0)
    second(1)
    fourth(0)
    for k in range(1, N_SHARD):
        to_shard(k).start()
    slab_to_ring(0, 0, seq, partner).start()
    for k in (1, 2, 3):
        slab_to_ring(0, k, seq, lax.rem(seq + 2 * k, N_SEQ)).start()
    pack_to_ring(0, 0, seq, partner).start()
    for k in (1, 2, 3):
        pack_to_ring(0, k, seq, lax.rem(seq + 2 * k, N_SEQ)).start()
    pack_own = pltpu.make_async_copy(pack_ref, pack_out.at[seq], own.at[5])
    pack_own.start()
    rows_own = pltpu.make_async_copy(rows_ref, rows_out.at[me], own.at[0])
    rows_own.start()
    slab_own = pltpu.make_async_copy(slab_ref, ow.at[seq], own.at[1])
    slab_own.start()

    def tile(t, i, masked):
        queries = spread(q_ref[i], False)
        scores = dot(land[t].reshape(SUPER, 2 * HEAD), queries, NT)
        if masked:
            scores = jnp.where(admitted(scores.shape, me, 0), scores, -1e30)
        peak = peak_ref[i]
        newest = jnp.maximum(peak, jnp.max(scores, axis=0, keepdims=True))
        weights = jnp.exp(scores - newest)
        shrink = jnp.exp(peak - newest)
        total = total_ref[i] * shrink + jnp.sum(weights, axis=0, keepdims=True)
        acc = acc_ref[i] * shrink + dot(vt[...], weights.astype(bf16), NN)
        return newest, total, acc

    def step(t, carry):
        pltpu.make_async_copy(land.at[t], mem_ref.at[t], msem.at[t]).start()

        for n in range(5):

            @pl.when(t == n)
            def _(n=n):
                for k in range(1, 4):
                    grads_to_expert(3 * n + k).start()

        @pl.when(t == 2)
        def _():
            slab_to_ring(0, 0, partner, partner).wait_recv()
            for k in (1, 2, 3):
                slab_to_ring(1, k, partner, lax.rem(seq + 2 * k, N_SEQ)).start()

        @pl.when(t == STAGE)
        def _():
            pack_to_ring(0, 0, partner, partner).wait_recv()
            for k in (1, 2, 3):
                pack_to_ring(1, k, partner, lax.rem(seq + 2 * k, N_SEQ)).start()

        @pl.when(t + 1 < N_SEQ)
        def _():
            third(t + 1)

        @pl.when(t + 2 < N_SEQ)
        def _():
            second(t + 2)

        for n in range(4):
            rows = land[t, 4 * n : 4 * n + 4].reshape(512, 2 * HEAD)
            vt[:, 512 * n : 512 * n + 512] = rows.T[HEAD:]
        newest, total, acc = tile(t, t, True)
        acc = acc / total
        stacked = jnp.concatenate([acc[:, :TOK_DEV], acc[:, TOK_DEV:]], axis=0)
        wide_ref[t] = stacked
        heads[t] = stacked.T.astype(bf16)
        lse_ref[t] = newest + jnp.log(total)

        @pl.when(t != seq)
        def _():
            to_token(t, seq).start()

        def rest(n, inner):
            i = t + 1 + 2 * n
            first, other = tile(t, i, False), tile(t, i + 1, False)
            peak_ref[i], total_ref[i], acc_ref[i] = first
            peak_ref[i + 1], total_ref[i + 1], acc_ref[i + 1] = other
            return inner

        lax.fori_loop(0, (N_SEQ - 1 - t) // 2, rest, 0)

        @pl.when(lax.rem(t, 2) == 0)
        def _():
            last = N_SEQ - 1
            peak_ref[last], total_ref[last], acc_ref[last] = tile(t, last, False)

        @pl.when(t + 1 < N_SEQ)
        def _():
            fourth(t + 1)

        return carry

    lax.fori_loop(0, N_SEQ, step, 0)
    for k in (1, 2, 3):
        pack_to_ring(2, k, partner, lax.rem(seq + 2 * k, N_SEQ)).start()
    slab_own.wait()
    for k in (1, 2, 3):
        for n, block in enumerate((seq, partner)):
            slab_to_ring(n, k, block, lax.rem(seq + 2 * k, N_SEQ)).wait_send()
            source = lax.rem(block + N_SEQ - 2 * k, N_SEQ)
            slab_to_ring(n, k, source, lax.rem(seq + N_SEQ - 2 * k, N_SEQ)).wait_recv()
    slab_to_ring(0, 0, seq, partner).wait_send()
    ow_own = pltpu.make_async_copy(ow, ow_ref, own.at[1])
    ow_own.start()
    att[seq] = heads[seq]
    for k in range(1, N_SEQ):
        source = lax.rem(seq + k, N_SEQ)
        to_token(source, source).wait_recv()

    for s in range(N_SEQ):
        attp_ref[:, 128 * s : 128 * s + 128] = att[s]
    residual = own_ref[...].astype(f32) + dot(
        attp_ref[...], ow[...].reshape(WIDTH, WIDTH), NN
    )
    res_ref[...] = residual
    inverse = lax.rsqrt(jnp.mean(residual * residual, axis=1, keepdims=True) + epsilon)
    normed = (residual * inverse * gain2_ref[...]).astype(bf16)
    for k in range(N_SHARD):
        peer = lax.rem(me + k, N_SHARD)
        here = pl.ds(pl.multiple_of(peer * 80, 16), 80)
        rows[here, :] = dot(pickt_ref[here, :], normed, NN).astype(bf16)
        if k:
            to_expert(k).start()
    here = pl.ds(pl.multiple_of(me * 80, 16), 80)
    mine = pltpu.make_async_copy(rows.at[here], land_ref.at[me], own.at[2])
    mine.start()
    for k in range(1, N_SEQ):
        to_token(lax.rem(seq + k, N_SEQ), seq).wait_send()
    rows_own.wait()
    norm_own.wait()
    ow_own.wait()
    for k in range(1, N_SHARD):
        to_shard(k).wait()
    for k in range(1, N_SHARD):
        grads_to_expert(k).wait()
        to_expert(k).wait()
    mine.wait()
    cot_own.wait()
    pack_own.wait()
    pack_to_ring(0, 0, seq, partner).wait_send()
    for k in (1, 2, 3):
        for n, block in enumerate((seq, partner, partner)):
            pack_to_ring(n, k, block, lax.rem(seq + 2 * k, N_SEQ)).wait_send()
            source = lax.rem(block + N_SEQ - 2 * k, N_SEQ)
            pack_to_ring(n, k, source, lax.rem(seq + N_SEQ - 2 * k, N_SEQ)).wait_recv()

    def end(t, carry):
        for m in range(15):
            message(t, m, me, me).wait_send()
        pltpu.make_async_copy(land.at[t], mem_ref.at[t], msem.at[t]).wait()
        return carry

    lax.fori_loop(0, N_SEQ, end, 0)


def attention(operands, ident):
    dma = pltpu.SemaphoreType.DMA
    vmem = pl.BlockSpec(memory_space=pltpu.VMEM)
    shards = (N_SHARD - 1,)
    return pl.pallas_call(
        attention_kernel,
        in_specs=[vmem] * 6 + [ANY] * 2 + [vmem] * 3 + [ANY] * 2,
        out_specs=[vmem] * 5 + [ANY] * 7,
        out_shape=[
            jax.ShapeDtypeStruct((N_SEQ, TOK_DEV, 2 * HEAD), bf16),
            jax.ShapeDtypeStruct((N_SEQ, 2 * HEAD, TOK_DEV), f32),
            jax.ShapeDtypeStruct((N_SEQ, 1, 2 * TOK_DEV), f32),
            jax.ShapeDtypeStruct((TOK_DEV, WIDTH), bf16),
            jax.ShapeDtypeStruct((TOK_DEV, WIDTH), f32),
            jax.ShapeDtypeStruct((HEAD_ROWS, WIDTH), bf16),
            jax.ShapeDtypeStruct((N_SEQ, N_SHARD, TOK_DEV, 2 * HEAD), bf16),
            jax.ShapeDtypeStruct((N_SHARD, 8, 2 * WIDTH), bf16),
            jax.ShapeDtypeStruct((N_SEQ, 128, WIDTH), bf16),
            jax.ShapeDtypeStruct((N_SHARD, 80, WIDTH), bf16),
            jax.ShapeDtypeStruct((N_SHARD, 80, WIDTH), bf16),
            jax.ShapeDtypeStruct((N_SEQ, LOCAL_EXPERTS, 192, WIDTH), bf16),
        ],
        scratch_shapes=[
            pltpu.VMEM((N_SEQ, N_SHARD, TOK_DEV, 2 * HEAD), bf16),
            pltpu.VMEM((HEAD, SUPER), bf16),
            pltpu.VMEM((N_SEQ, TOK_DEV, 2 * HEAD), bf16),
            pltpu.VMEM((N_SEQ, 1, 2 * TOK_DEV), f32),
            pltpu.VMEM((N_SEQ, 1, 2 * TOK_DEV), f32),
            pltpu.VMEM((N_SEQ, HEAD, 2 * TOK_DEV), f32),
            pltpu.VMEM((N_SEQ, TOK_DEV, 128), bf16),
            pltpu.VMEM((N_SEQ, 128, WIDTH), bf16),
            pltpu.VMEM((WIDTH, 2 * COLS), bf16),
            pltpu.VMEM((HEAD_ROWS, WIDTH), bf16),
            pltpu.VMEM((N_SHARD * 80, WIDTH), bf16),
            dma((N_SEQ, 15)),
            dma((N_SEQ, 15)),
            dma((N_SEQ,)),
            dma((N_SEQ,)),
            dma(shards),
            dma(shards),
            dma((2, 4)),
            dma((2, 4)),
            dma(shards),
            dma(shards),
            dma((6,)),
            dma((N_SEQ,)),
            dma(shards),
            dma(shards),
            dma((3, 4)),
            dma((3, 4)),
        ],
        compiler_params=pltpu.CompilerParams(
            collective_id=ident, has_side_effects=True, vmem_limit_bytes=56 << 20
        ),
        name="attention_forward",
    )(*operands)


def late_kernel(*refs):
    (attp, ow_ref, res_ref, cot_ref, gain_ref, pick_ref, land_ref, gr_ref, w_ref) = refs[:9]
    (q_ref, wide_ref, lse_ref, mem_ref, cos_ref, sin_ref, turn_ref) = refs[9:16]
    (normed_ref, slab_ref, pack_ref, gcol_ref) = refs[16:20]
    (resg_ref, tok_ref, came_ref, sums_ref, qkv_ref, wout_ref, mgain_ref, kz_ref) = refs[20:28]
    qall_ref = refs[28]
    (gu, dn, land, rows, returned, xt, ht, hg, gm, mixed, dw, ags, xstage) = refs[29:42]
    (gl, qs, gs, delta_ref, kt, acc, dq, stage, dl) = refs[42:51]
    (mbuf, pg, qp, qstage, qland, qsum, osum, xland, oland, mstage, mland) = refs[51:62]
    cland, cstage, oseq, hid = refs[62:66]
    (wsem, isend, irecv, ksend, krecv, psend, precv) = refs[66:73]
    (dsend, drecv, osend, orecv, jsend, jrecv, nsend, nrecv, own) = refs[73:82]
    (msem, asend, arecv, bsend, brecv, xsend, xrecv, csend, crecv, tsend, trecv) = refs[82:93]
    (usend, urecv, fsend, frecv) = refs[93:]
    seq = lax.axis_index("seq")
    me = lax.axis_index("shard")
    ring = seq // 2
    far = lax.rem(seq, 2)

    def weights(e, s):
        return (
            pltpu.make_async_copy(
                w_ref.at[s, e, :128], gu.at[e, 128 * s : 128 * s + 128], wsem.at[e, s, 0]
            ),
            pltpu.make_async_copy(
                w_ref.at[s, e, 128:], dn.at[e, 64 * s : 64 * s + 64], wsem.at[e, s, 1]
            ),
        )

    def flat(block, low, high):
        return pl.ds(pl.multiple_of(block * 80 + low, 16), high - low)

    back_pieces = ((0, 32), (32, 80))

    def to_source(part, k, block, source, peer):
        low, high = back_pieces[part]
        return transfer(
            rows.at[flat(block, low, high)],
            returned.at[flat(source, low, high)],
            isend.at[part, k - 1],
            irecv.at[part, k - 1],
            "shard",
            peer,
        )

    def to_token_expert(n):
        m = (n + 1) % 8
        pair = lax.rem(me // 2 % 2 + (n + 1) // 8, 2)
        peer = lax.rem(me // 4 + m // 2, 4) * 4 + pair * 2 + lax.rem(me + m, 2)
        return transfer(
            land.at[peer], came_ref.at[me], jsend.at[n], jrecv.at[n], "shard", peer
        )

    def to_ring(e, k):
        peer = lax.rem(seq + 2 * k, N_SEQ)
        return transfer(
            dw.at[e, k], kz_ref.at[e, k - 1], ksend.at[e, k - 1], krecv.at[e, k - 1], "seq", peer
        )

    def out_to_core(q):
        return transfer(
            rows.at[flat(2 * q + 1 - me % 2, 0, 64)],
            oland.at[q],
            psend.at[q],
            precv.at[q],
            "shard",
            me + 1 - 2 * (me % 2),
        )

    def out_to_chip(k, block, source, peer):
        return transfer(
            rows.at[flat(2 * block + me % 2, 0, 64)],
            oland.at[8 + source],
            psend.at[7 + k],
            precv.at[7 + k],
            "shard",
            2 * peer + me % 2,
        )

    def to_head(p):
        return transfer(
            ags.at[p], gl.at[seq], osend.at[p], orecv.at[seq], "seq", p
        )

    def from_head(source):
        return transfer(gl.at[source], gl.at[source], osend.at[0], orecv.at[source], "seq", source)

    core = lax.rem(me, 2)
    chip = me // 2

    def to_core(t):
        return transfer(
            stage.at[lax.rem(t, 4), :, 1 - core],
            cland.at[lax.rem(t, 4)],
            tsend.at[t],
            trecv.at[t],
            "shard",
            me + 1 - 2 * core,
        )

    def to_owner(t, k, block, source, peer):
        return transfer(
            cstage.at[lax.rem(t, 4), block],
            dl.at[t, source],
            dsend.at[t, k - 1],
            drecv.at[t, k - 1],
            "shard",
            peer * 2 + core,
        )

    def to_token(t, source):
        return transfer(pg.at[t], tok_ref.at[source], nsend.at[t], nrecv.at[source], "seq", t)

    def out_to_seq(p):
        return transfer(
            osum.at[p], oseq.at[seq], usend.at[p], urecv.at[seq], "seq", p
        )

    def out_from_seq(source):
        return transfer(
            oseq.at[source], oseq.at[source], usend.at[0], urecv.at[source], "seq", source
        )

    def slab_to_ring(n, k, block, peer):
        source = slab_ref if n == 0 else qall_ref.at[block]
        return transfer(
            source, qall_ref.at[block], fsend.at[n, k], frecv.at[n, k], "seq", peer
        )

    def fetch(t):
        slot = lax.rem(t, 2)
        return pltpu.make_async_copy(mem_ref.at[t], mbuf.at[slot], msem.at[slot])

    def qkv_to_shard(k, block, source, peer):
        return transfer(
            qstage.at[block], qland.at[source], asend.at[k - 1], arecv.at[k - 1], "shard", peer
        )

    def qkv_to_seq(k, block, source, peer):
        return transfer(
            qsum.at[block], qkv_ref.at[source], bsend.at[k - 1], brecv.at[k - 1], "seq", peer
        )

    def gain_to_shard(k, block, source, peer):
        return transfer(
            mstage.at[block], mland.at[source], csend.at[k - 1], crecv.at[k - 1], "shard", peer
        )

    partner = seq + 1 - 2 * far
    to_pair = transfer(xstage, xland, xsend, xrecv, "seq", partner)

    greet(everyone(seq, me))
    for e in range(LOCAL_EXPERTS):
        for s in range(N_SEQ):
            for copy in weights(e, s):
                copy.start()
    slab_to_ring(0, 0, seq, partner).start()
    for k in (1, 2, 3):
        slab_to_ring(0, k, seq, lax.rem(seq + 2 * k, N_SEQ)).start()
    slab_own = pltpu.make_async_copy(slab_ref, qall_ref.at[seq], own.at[3])
    slab_own.start()

    land_copy = pltpu.make_async_copy(land_ref, land, own.at[4])
    land_copy.start()

    def split(block, e):
        return (
            block.astype(f32)
            .reshape(N_SHARD, LOCAL_EXPERTS, 8, WIDTH)[:, e]
            .reshape(128, WIDTH)
            .astype(bf16)
        )

    def join(first, second):
        halves = [half.astype(f32).reshape(N_SHARD, 1, 8, WIDTH) for half in (first, second)]
        return jnp.concatenate(halves, axis=1).reshape(N_SHARD, 16, WIDTH).astype(bf16)

    def expert(e, x, g, here):
        pre = dot(x, gu[e], NN)
        gate, up = pre[:, :FF], pre[:, FF:]
        sigmoid = jax.nn.sigmoid(gate)
        act = gate * sigmoid
        hidden = (act * up).astype(bf16)
        units = dot(g, dn[e], NT)
        gate_grad = (units * up * sigmoid * (1.0 + gate * (1.0 - sigmoid))).astype(bf16)
        up_grad = (units * act).astype(bf16)
        both = jnp.concatenate([gate_grad, up_grad], axis=1)
        hg[e, here, :] = both
        hid[e, here, :] = hidden
        return dot(both, gu[e], NT).astype(bf16)

    def run_expert(e, low):
        def aligned(n, carry):
            group = pl.ds(n * 8, 8)
            here = pl.ds(pl.multiple_of(n * 256, 256), 256)
            x = land[group, low : low + 32].reshape(256, WIDTH)
            g = gr_ref[group, low : low + 32].reshape(256, WIDTH)
            back = expert(e, x, g, here)
            for m in range(8):
                rows[flat(n * 8 + m, low, low + 32), :] = back[32 * m : 32 * m + 32]
            return carry

        lax.fori_loop(0, 2, aligned, 0)
        g = split(gr_ref[:, 32:48], e)
        gm[e] = g
        mixed[1, e] = expert(e, split(land[:, 32:48], e), g, slice(512, 640))

    def finish_expert(e, low):
        def aligned(n, carry):
            group = pl.ds(n * 8, 8)
            here = pl.ds(pl.multiple_of(n * 256, 256), 256)
            hidden = hid[e, here, :]
            xt[:, here] = land[group, low : low + 32].reshape(256, WIDTH).T
            ht[:, here] = hidden.T
            out = dot(hidden, dn[e], NN).astype(bf16)
            land[group, low : low + 32] = out.reshape(8, 32, WIDTH)
            return carry

        lax.fori_loop(0, 2, aligned, 0)
        hidden = hid[e, 512:, :]
        xt[:, 512:] = split(land[:, 32:48], e).T
        ht[:, 512:] = hidden.T
        mixed[0, e] = dot(hidden, dn[e], NN).astype(bf16)

    def expert_grads(e):
        low = 48 * e

        def block(h, carry):
            features = pl.ds(pl.multiple_of(h * 512, 512), 512)
            units = pl.ds(pl.multiple_of(h * 256, 256), 256)
            grad = dot(xt[features, :], hg[e], NN).astype(bf16)
            part = dot(ht[units, :512], gr_ref[:, low : low + 32].reshape(512, WIDTH), NN)
            part = (part + dot(ht[units, 512:], gm[e], NN)).astype(bf16)
            for m in range(4):
                k = lax.rem(2 * h + m // 2 + 4 - ring, 4)
                n = lax.rem(m + far, 2)
                dw[e, k, n, :128, :] = grad[128 * m : 128 * m + 128]
                dw[e, k, n, 128:, :] = part[64 * m : 64 * m + 64]
            return carry

        lax.fori_loop(0, 2, block, 0)

    for e in range(LOCAL_EXPERTS):
        for s in range(N_SEQ):
            for copy in weights(e, s):
                copy.wait()
    land_copy.wait()
    run_expert(0, 0)
    for k in range(1, N_SHARD):
        peer = lax.rem(me + k, N_SHARD)
        to_source(0, k, peer, me, peer).start()
    slab_to_ring(0, 0, partner, partner).wait_recv()
    for k in (1, 2, 3):
        slab_to_ring(1, k, partner, lax.rem(seq + 2 * k, N_SEQ)).start()
    run_expert(1, 48)
    joined = join(mixed[1, 0], mixed[1, 1])
    for n in range(N_SHARD):
        rows[80 * n + 32 : 80 * n + 48, :] = joined[n]
    for k in range(1, N_SHARD):
        peer = lax.rem(me + k, N_SHARD)
        to_source(1, k, peer, me, peer).start()
    returned[flat(me, 0, 80), :] = rows[flat(me, 0, 80), :]
    normed_copy = pltpu.make_async_copy(normed_ref, gu.at[0], own.at[4])
    normed_copy.start()
    ow_copy = pltpu.make_async_copy(ow_ref, gu.at[1], own.at[0])
    ow_copy.start()
    finish_expert(0, 0)
    expert_grads(0)
    for k in (1, 3):
        to_ring(0, k).start()
    finish_expert(1, 48)
    land[:, 32:48] = join(mixed[0, 0], mixed[0, 1])
    expert_grads(1)

    for part in range(2):
        for k in range(1, N_SHARD):
            source = lax.rem(me + N_SHARD - k, N_SHARD)
            to_source(part, k, source, source, source).wait_recv()
    for n in range(7):
        to_token_expert(n).start()
    moe_in_grad = dot(pick_ref[...], returned[...], NN)
    residual = res_ref[...]
    inverse = lax.rsqrt(jnp.mean(residual * residual, axis=1, keepdims=True) + epsilon)
    scaled = moe_in_grad * gain_ref[...]
    moe_part = inverse * scaled - residual * (inverse * inverse * inverse) * jnp.mean(
        residual * scaled, axis=1, keepdims=True
    )
    residual_grad = cot_ref[...].astype(f32) + moe_part
    resg_ref[...] = residual_grad
    branch = residual_grad.astype(bf16)
    ow_copy.wait()
    attended_grad = dot(branch, gu[1], NT).astype(bf16)
    for p in range(N_SEQ):
        ags[p] = attended_grad[:, 128 * p : 128 * p + 128]

        @pl.when(seq != p)
        def _(p=p):
            to_head(p).start()

    gl[seq] = ags[seq]
    for part in range(2):
        for k in range(1, N_SHARD):
            peer = lax.rem(me + k, N_SHARD)
            to_source(part, k, peer, me, peer).wait_send()
    for k in range(4):
        block = dot(attp[:, 256 * k : 256 * k + 256].T, branch, NN).reshape(2, N_SHARD, 8, WIDTH)
        for j in range(N_SHARD):
            rows[80 * j + 16 * k : 80 * j + 16 * k + 16, :] = jnp.concatenate(
                [block[0, j], block[1, j]], axis=0
            ).astype(bf16)
    for k in range(1, N_SEQ):
        from_head(lax.rem(seq + k, N_SEQ)).wait_recv()
    for k in (1, 3, 2):
        to_ring(1, k).start()
    to_ring(0, 2).start()
    for q in range(N_SHARD // 2):
        out_to_core(q).start()
    came_own = pltpu.make_async_copy(land.at[me], came_ref.at[me], own.at[0])
    came_own.start()
    fetch(0).start()
    normed_copy.wait()
    qp[...] = jnp.zeros((WIDTH, COLS), f32)

    def begin(i, carry):
        qs[i] = spread(q_ref[i], False)
        gs[i] = spread(gl[i], True)
        product = wide_ref[i] * gl[i].astype(f32).T
        delta_ref[i] = jnp.concatenate(
            [
                jnp.sum(product[:HEAD], axis=0, keepdims=True),
                jnp.sum(product[HEAD:], axis=0, keepdims=True),
            ],
            axis=1,
        )
        dq[i] = jnp.zeros((HEAD, 2 * TOK_DEV), f32)
        return carry

    lax.fori_loop(0, N_SEQ, begin, 0)

    def tile(t, i, n, masked):
        here = slice(n * BWD_TILE, (n + 1) * BWD_TILE)
        memory = mbuf[lax.rem(t, 2), 8 * n : 8 * n + 8].reshape(BWD_TILE, 2 * HEAD)
        scores = dot(memory, qs[i], NT)
        weight = jnp.exp(scores - lse_ref[i])
        if masked:
            weight = jnp.where(admitted(scores.shape, me, n * BWD_TILE), weight, 0.0)
        weight_grad = dot(memory, gs[i], NT)
        score_grad = (weight * (weight_grad - delta_ref[i])).astype(bf16)
        here_grad = dot(weight.astype(bf16), gs[i], NN) + dot(score_grad, qs[i], NN)
        if masked:
            acc[here, :] = here_grad
        else:
            acc[here, :] += here_grad
        dq[i] += dot(kt[:, here], score_grad, NN)

    def turned(grad, n, t):
        cosine, sine = cos_ref[t], sin_ref[t]
        if n:
            key = lax.broadcasted_iota(jnp.int32, cosine.shape, 1) < HEAD
            cosine = jnp.where(key, cosine, 1.0)
            sine = jnp.where(key, sine, 0.0)
        other = dot(grad, turn_ref[n], NT)
        return (grad.astype(f32) * cosine + other * sine).astype(bf16)

    def chip_sum(t):
        slot = lax.rem(t, 4)

        @pl.when(t >= 4)
        def _():
            for k in range(1, N_SHARD // 2):
                peer = lax.rem(chip + k, N_SHARD // 2)
                to_owner(t - 4, k, peer, chip, peer).wait_send()

        to_core(t).wait_recv()
        total = stage[slot, :, core].astype(f32) + cland[slot].astype(f32)
        cstage[slot] = total.astype(bf16)
        dl[t, chip] = cstage[slot, chip]
        for k in range(1, N_SHARD // 2):
            peer = lax.rem(chip + k, N_SHARD // 2)
            to_owner(t, k, peer, chip, peer).start()

    def token_gradient(t):
        for k in range(1, N_SHARD // 2):
            source = lax.rem(chip + N_SHARD // 2 - k, N_SHARD // 2)
            to_owner(t, k, source, source, source).wait_recv()
        grad = jnp.sum(dl[t].astype(f32), axis=0).astype(bf16)
        pg[t, :, 2 * HEAD :] = turned(grad, 1, t)
        grad = pg[t]

        @pl.when(t != seq)
        def _():
            to_token(t, seq).start()

        tokens = pl.ds(pl.multiple_of(t * 128, 128), 128)
        qp[...] += dot(gu[0, tokens, :].T, grad, NN)

    def out_chips():
        for q in range(N_SHARD // 2):
            out_to_core(q).wait_recv()
            here = flat(2 * q + core, 0, 64)
            total = rows[here, :].astype(f32) + oland[q].astype(f32)
            rows[here, :] = total.astype(bf16)
        oland[8 + chip] = rows[flat(me, 0, 64), :]
        for k in range(1, N_SHARD // 2):
            peer = lax.rem(chip + k, N_SHARD // 2)
            out_to_chip(k, peer, chip, peer).start()

    def sum_weights():
        for q in range(N_SHARD // 2):
            out_to_core(q).wait_send()
        for k in range(1, N_SHARD // 2):
            peer = lax.rem(chip + k, N_SHARD // 2)
            out_to_chip(k, peer, chip, peer).wait_send()
        for e in range(LOCAL_EXPERTS):
            for k in (1, 2, 3):
                to_ring(e, k).wait()
        back = []
        for e, buffer in enumerate((rows, returned)):
            for k in range(3):
                for n in range(2):
                    index = 2 * k + n
                    back.append(
                        pltpu.make_async_copy(
                            kz_ref.at[e, k, n],
                            buffer.at[192 * index : 192 * index + 192],
                            wsem.at[e, index, 0],
                        )
                    )
                    back[-1].start()
        for copy in back:
            copy.wait()
        for e, buffer in enumerate((rows, returned)):
            for n in range(2):
                total = dw[e, 0, n].astype(f32)
                for k in range(3):
                    index = 2 * k + n
                    total += buffer[192 * index : 192 * index + 192, :].astype(f32)
                if n == 0:
                    sums_ref[e] = total
                else:
                    xstage[e] = total.astype(bf16)
        to_pair.start()
        for k in range(1, N_SHARD // 2):
            source = lax.rem(chip + N_SHARD // 2 - k, N_SHARD // 2)
            out_to_chip(k, source, source, source).wait_recv()
        osum[...] = jnp.sum(oland[8:].astype(f32), axis=0).reshape(N_SEQ, 8, WIDTH)
        for p in range(N_SEQ):

            @pl.when(seq != p)
            def _(p=p):
                out_to_seq(p).start()

        oseq[seq] = osum[seq]

    def step(t, carry):
        fetch(t).wait()

        @pl.when(t + 1 < N_SEQ)
        def _():
            fetch(t + 1).start()

        @pl.when(t >= 1)
        def _():
            chip_sum(t - 1)

        @pl.when(t >= 3)
        def _():
            token_gradient(t - 3)

        for n in range(5):

            @pl.when(t == n + 1)
            def _(n=n):
                if n < 4:
                    to_token_expert(7 + 2 * n).start()
                    to_token_expert(8 + 2 * n).start()
                if n == 0:
                    out_chips()

        @pl.when(t == N_SEQ - 2)
        def _():
            sum_weights()

        for n in range(4):
            block = mbuf[lax.rem(t, 2), 4 * n : 4 * n + 4].reshape(512, 2 * HEAD)
            kt[:, 512 * n : 512 * n + 512] = block.T[:HEAD]
        tile(t, t, 0, True)
        tile(t, t, 1, True)
        grad = dq[t] * (1.0 / math.sqrt(HEAD))
        grad = jnp.concatenate([grad[:, :TOK_DEV], grad[:, TOK_DEV:]], axis=0).T.astype(bf16)
        pg[t, :, : 2 * HEAD] = turned(grad, 0, t)

        def rest(i, inner):
            tile(t, i, 0, False)
            tile(t, i, 1, False)
            return inner

        lax.fori_loop(t + 1, N_SEQ, rest, 0)

        @pl.when(t >= 4)
        def _():
            to_core(t - 4).wait_send()

        slot = lax.rem(t, 4)
        for n in range(4):
            block = acc[512 * n : 512 * n + 512, :].astype(bf16)
            stage[slot, 2 * n : 2 * n + 2] = block.reshape(2, 2, TOK_DEV, 2 * HEAD)
        to_core(t).start()
        return carry

    lax.fori_loop(0, N_SEQ, step, 0)

    chip_sum(N_SEQ - 1)
    for t in (3, 2, 1):
        token_gradient(N_SEQ - t)
    own_token = pltpu.make_async_copy(pg.at[seq], tok_ref.at[seq], own.at[1])
    own_token.start()
    split_rows = qp[...].reshape(N_SEQ, N_SHARD, 8, COLS)
    for j in range(N_SHARD):
        qstage[j] = split_rows[:, j].reshape(64, COLS).astype(bf16)
    for k in range(1, N_SHARD):
        peer = lax.rem(me + k, N_SHARD)
        qkv_to_shard(k, peer, me, peer).start()
    qland[me] = qstage[me]
    for k in range(1, N_SHARD):
        source = lax.rem(me + N_SHARD - k, N_SHARD)
        qkv_to_shard(k, source, source, source).wait_recv()
    qsum[...] = jnp.sum(qland[...].astype(f32), axis=0).reshape(N_SEQ, 8, COLS)
    for k in range(1, N_SEQ):
        peer = lax.rem(seq + k, N_SEQ)
        qkv_to_seq(k, peer, seq, peer).start()
    own_qkv = pltpu.make_async_copy(qsum.at[seq], qkv_ref.at[seq], own.at[2])
    own_qkv.start()

    to_pair.wait()
    gain = jnp.zeros((128, 128), f32)
    for e in range(LOCAL_EXPERTS):
        sums_ref[e] += xland[e].astype(f32)
        product = pack_ref[e, :128].astype(f32) * sums_ref[e, :128]
        for c in range(8):
            gain += product[:, 128 * c : 128 * c + 128]
    gain = jnp.sum(gain, axis=1, keepdims=True) / gcol_ref[...]
    mstage[...] = gain.reshape(N_SHARD, 8, 128)
    for k in range(1, N_SHARD):
        peer = lax.rem(me + k, N_SHARD)
        gain_to_shard(k, peer, me, peer).start()
    mland[me] = mstage[me]
    for k in range(1, N_SEQ):
        out_from_seq(lax.rem(seq + k, N_SEQ)).wait_recv()
    wout_ref[...] = jnp.sum(oseq[...], axis=0)
    for k in range(1, N_SHARD):
        source = lax.rem(me + N_SHARD - k, N_SHARD)
        gain_to_shard(k, source, source, source).wait_recv()
    mgain_ref[...] = jnp.sum(mland[...], axis=0)

    for p in range(N_SEQ):

        @pl.when(seq != p)
        def _(p=p):
            to_head(p).wait_send()
            out_to_seq(p).wait_send()

    for k in range(1, N_SHARD):
        to_token_expert(k - 1).wait()
        peer = lax.rem(me + k, N_SHARD)
        qkv_to_shard(k, peer, me, peer).wait_send()
        gain_to_shard(k, peer, me, peer).wait_send()

    def end(t, carry):
        for k in range(1, N_SHARD // 2):
            peer = lax.rem(chip + k, N_SHARD // 2)
            to_owner(t, k, peer, chip, peer).wait_send()
        to_core(t).wait_send()
        return carry

    lax.fori_loop(4, N_SEQ, end, 0)
    for k in range(1, N_SEQ):
        peer = lax.rem(seq + k, N_SEQ)
        to_token(peer, seq).wait_send()
        to_token(peer, peer).wait_recv()
        qkv_to_seq(k, peer, seq, peer).wait_send()
        source = lax.rem(seq + N_SEQ - k, N_SEQ)
        qkv_to_seq(k, source, source, source).wait_recv()
    slab_to_ring(0, 0, seq, partner).wait_send()
    for k in (1, 2, 3):
        for n, block in enumerate((seq, partner)):
            slab_to_ring(n, k, block, lax.rem(seq + 2 * k, N_SEQ)).wait_send()
            source = lax.rem(block + N_SEQ - 2 * k, N_SEQ)
            slab_to_ring(n, k, source, lax.rem(seq + N_SEQ - 2 * k, N_SEQ)).wait_recv()
    for copy in (own_token, own_qkv, came_own, slab_own):
        copy.wait()


def late(operands, ident):
    dma = pltpu.SemaphoreType.DMA
    vmem = pl.BlockSpec(memory_space=pltpu.VMEM)
    wide = jax.ShapeDtypeStruct((TOK_DEV, WIDTH), f32)
    routed = (N_SHARD, 80, WIDTH)
    grads = (LOCAL_EXPERTS, 2, 192, WIDTH)
    shapes = [
        ((LOCAL_EXPERTS, WIDTH, 2 * FF), bf16),
        ((LOCAL_EXPERTS, FF, WIDTH), bf16),
        (routed, bf16),
        ((N_SHARD * 80, WIDTH), bf16),
        ((N_SHARD * 80, WIDTH), bf16),
        ((WIDTH, EXPERT_ROWS), bf16),
        ((FF, EXPERT_ROWS), bf16),
        ((LOCAL_EXPERTS, EXPERT_ROWS, 2 * FF), bf16),
        ((LOCAL_EXPERTS, 128, WIDTH), bf16),
        ((2, LOCAL_EXPERTS, 128, WIDTH), bf16),
        ((LOCAL_EXPERTS, 4, 2, 192, WIDTH), bf16),
        ((N_SEQ, TOK_DEV, 128), bf16),
        ((LOCAL_EXPERTS, 192, WIDTH), bf16),
        ((N_SEQ, TOK_DEV, 2 * HEAD), bf16),
        ((N_SEQ, 2 * TOK_DEV, 2 * HEAD), bf16),
        ((N_SEQ, 2 * TOK_DEV, 2 * HEAD), bf16),
        ((N_SEQ, 1, 2 * TOK_DEV), f32),
        ((HEAD, SUPER), bf16),
        ((SUPER, 2 * HEAD), f32),
        ((N_SEQ, HEAD, 2 * TOK_DEV), f32),
        ((4, N_SHARD // 2, 2, TOK_DEV, 2 * HEAD), bf16),
        ((N_SEQ, N_SHARD // 2, TOK_DEV, 2 * HEAD), bf16),
        ((2, N_SHARD, TOK_DEV, 2 * HEAD), bf16),
        ((N_SEQ, TOK_DEV, COLS), bf16),
        ((WIDTH, COLS), f32),
        ((N_SHARD, 64, COLS), bf16),
        ((N_SHARD, 64, COLS), bf16),
        ((N_SEQ, 8, COLS), f32),
        ((N_SEQ, 8, WIDTH), f32),
        ((LOCAL_EXPERTS, 192, WIDTH), bf16),
        ((N_SHARD, 64, WIDTH), bf16),
        ((N_SHARD, 8, 128), f32),
        ((N_SHARD, 8, 128), f32),
        ((4, N_SHARD // 2, TOK_DEV, 2 * HEAD), bf16),
        ((4, N_SHARD // 2, TOK_DEV, 2 * HEAD), bf16),
        ((N_SEQ, 8, WIDTH), f32),
        ((LOCAL_EXPERTS, EXPERT_ROWS, FF), bf16),
    ]
    shards = (N_SHARD - 1,)
    counts = [(LOCAL_EXPERTS, N_SEQ, 2)]
    counts += [(2,) + shards] * 2
    counts += [(LOCAL_EXPERTS, 3)] * 2 + [shards] * 2
    counts += [(N_SEQ, N_SHARD // 2 - 1)] * 2 + [(N_SEQ,)] * 2 + [shards] * 2 + [(N_SEQ,)] * 2
    counts += [(5,), (2,)] + [shards] * 2 + [(N_SEQ - 1,)] * 2
    semaphores = [dma(count) for count in counts] + [dma, dma]
    semaphores += [dma(shards)] * 2 + [dma((N_SEQ,))] * 4 + [dma((2, 4))] * 2
    return pl.pallas_call(
        late_kernel,
        in_specs=[vmem, ANY] + [vmem] * 4 + [ANY, vmem, ANY] + [vmem] * 3 + [ANY] + [vmem] * 3 + [ANY] * 2 + [vmem] * 2,
        out_specs=[vmem, ANY, ANY, vmem, ANY, vmem, vmem, ANY, ANY],
        out_shape=[
            wide,
            jax.ShapeDtypeStruct((N_SEQ, TOK_DEV, COLS), bf16),
            jax.ShapeDtypeStruct(routed, bf16),
            jax.ShapeDtypeStruct((LOCAL_EXPERTS, 192, WIDTH), f32),
            jax.ShapeDtypeStruct((N_SEQ, 8, COLS), f32),
            jax.ShapeDtypeStruct((8, WIDTH), f32),
            jax.ShapeDtypeStruct((8, 128), f32),
            jax.ShapeDtypeStruct((LOCAL_EXPERTS, 3, 2, 192, WIDTH), bf16),
            jax.ShapeDtypeStruct((N_SEQ, 128, 2 * WIDTH), bf16),
        ],
        scratch_shapes=[pltpu.VMEM(*shape) for shape in shapes] + semaphores,
        compiler_params=pltpu.CompilerParams(
            collective_id=ident, has_side_effects=True, vmem_limit_bytes=LIMIT << 20
        ),
        name="experts_attention_backward",
    )(*operands)


def group_columns(rows):
    lead = rows.shape[:-1]
    queries = rows[..., : HEADS * HEAD].reshape(lead + (N_SEQ, 2 * HEAD))
    keys = rows[..., HEADS * HEAD : (HEADS + KV) * HEAD].reshape(lead + (N_SEQ, HEAD))
    values = rows[..., (HEADS + KV) * HEAD :].reshape(lead + (N_SEQ, HEAD))
    return jnp.concatenate([queries, keys, values], axis=-1)


def ungroup_columns(groups):
    rows = groups.shape[0]
    return jnp.concatenate(
        [
            groups[:, :, : 2 * HEAD].reshape(rows, HEADS * HEAD),
            groups[:, :, 2 * HEAD : 3 * HEAD].reshape(rows, KV * HEAD),
            groups[:, :, 3 * HEAD :].reshape(rows, KV * HEAD),
        ],
        axis=1,
    )


def rope_pair(shard):
    half = HEAD // 2
    frequency = jnp.exp(
        jnp.arange(half, dtype=f32) * jnp.float32(-2.0 * math.log(rope_base) / HEAD)
    )
    chunk = jnp.arange(N_SEQ, dtype=jnp.int32)[:, None] * N_SHARD + shard
    position = chunk * TOK_DEV + jnp.arange(TOK_DEV, dtype=jnp.int32)[None, :]
    angles = position[:, :, None].astype(f32) * frequency[None, None, :]
    cosine, sine = lax.optimization_barrier((jnp.cos(angles), jnp.sin(angles)))
    return jnp.tile(cosine, (1, 1, 4)), jnp.tile(sine, (1, 1, 4))


def turn_matrix():
    row = jnp.arange(COLS, dtype=jnp.int32)[:, None]
    col = jnp.arange(COLS, dtype=jnp.int32)[None, :]
    half = HEAD // 2
    low = col % HEAD < half
    minus = low & (row == col + half) & (col < 3 * HEAD)
    plus = (~low) & (row == col - half) & (col < 3 * HEAD)
    return (plus.astype(f32) - minus.astype(f32)).astype(bf16)


def routing(routes, route_weights):
    ids = jnp.arange(EXPERTS, dtype=jnp.int32)
    hit = routes[:, :, None] == ids[None, None, :]
    mask = jnp.sum(hit.astype(f32), axis=1)
    weight = jnp.sum(jnp.where(hit, route_weights[:, :, None], 0.0), axis=1)
    token = jnp.arange(TOK_DEV, dtype=jnp.int32)
    earlier = (token[:, None] > token[None, :]).astype(bf16)
    before = dot(earlier, mask.astype(bf16), NN)
    code = jnp.where(mask > 0.0, before, -1.0).astype(bf16)
    place = jnp.arange(N_SHARD * 80, dtype=jnp.int32)
    row = place % 80
    slot = jnp.where(row < 40, row, jnp.where(row < 48, row - 8, row - 48))
    owner = place // 80 * LOCAL_EXPERTS + (row >= 40).astype(jnp.int32)
    widen = (owner[None, :] == ids[:, None]).astype(bf16)
    pick = dot(code, widen, NN) == slot.astype(f32)[None, :]
    high = weight.astype(bf16)
    low = (weight - high.astype(f32)).astype(bf16)
    high = jnp.where(pick, dot(high, widen, NN), 0.0)
    low = jnp.where(pick, dot(low, widen, NN), 0.0)
    return pick.astype(bf16), high.astype(bf16), low.astype(bf16), jnp.sum(high + low, axis=0)


def on_device(
    layer_input,
    attn_gain,
    moe_gain,
    w_qkv,
    w_out,
    w_gate,
    w_up,
    w_down,
    routes,
    route_weights,
    cotangent,
):
    seq = lax.axis_index("seq")
    shard = lax.axis_index("shard")

    pick, scale_high, scale_low, slot_scale = routing(routes, route_weights)
    pick_turned = pick.T
    grad_send = (slot_scale[:, None] * dot(pick_turned, cotangent, NN)).astype(bf16)

    grouped = group_columns(w_qkv)
    pieces = grouped.reshape(8, N_SEQ, 2, 128).transpose(1, 2, 0, 3)
    gains = jnp.concatenate([attn_gain, moe_gain, jnp.zeros((112,), bf16)])
    gains = jnp.broadcast_to(gains[None, None, :], (N_SEQ, 16, 128))
    pieces = jnp.concatenate([pieces.reshape(N_SEQ, 16, 128), gains], axis=1)
    tokens, columns, out_slabs = first_gather(
        layer_input.reshape(8, TOK_DEV // 8, WIDTH), pieces, w_out, 1
    )
    expert_pack = jnp.concatenate(
        [jnp.concatenate([w_gate, w_up], axis=2), w_down], axis=1
    )
    gain_rows = columns[:, N_SEQ, :8, :16].transpose(1, 0, 2)
    gain_attn = gain_rows[:, :, :8].reshape(WIDTH).astype(f32)
    gain_moe = gain_rows[:, :, 8:].reshape(WIDTH).astype(f32)
    cosine, sine = rope_pair(shard)
    turn = turn_matrix()
    (
        queries,
        attended_wide,
        lse,
        attended,
        residual,
        normed,
        memory,
        qkv_slab,
        out_weight,
        expert_rows,
        grad_rows,
        expert_weights,
    ) = attention(
        (
            tokens.reshape(HEAD_ROWS, WIDTH),
            columns,
            gain_attn[None, :],
            cosine,
            sine,
            turn,
            out_slabs.reshape(128, WIDTH),
            grouped.reshape(8, 2 * WIDTH),
            layer_input,
            gain_moe[None, :],
            pick_turned,
            grad_send.reshape(N_SHARD, 80, WIDTH),
            expert_pack,
        ),
        2,
    )
    left = jnp.arange(2 * HEAD, dtype=jnp.int32) < HEAD
    turns = turn[:128, :128]
    turns = jnp.stack([turns, jnp.where(left[:, None] & left[None, :], turns, 0)])
    gain_here = lax.dynamic_slice_in_dim(gain_moe, seq * 128, 128)
    (
        residual_grad,
        token_grad,
        came_back,
        expert_sums,
        qkv_groups,
        out_weight_grad,
        moe_gain_grad,
        _,
        qkv_all,
    ) = late(
        (
            attended,
            out_weight.reshape(WIDTH, WIDTH),
            residual,
            cotangent,
            gain_moe[None, :],
            pick,
            expert_rows,
            grad_rows,
            expert_weights,
            queries,
            attended_wide,
            lse,
            memory,
            cosine,
            sine,
            turns,
            normed,
            qkv_slab.reshape(128, 2 * WIDTH),
            expert_pack,
            jnp.broadcast_to(gain_here[:, None], (128, 128)),
        ),
        3,
    )
    came_back = came_back.reshape(N_SHARD * 80, WIDTH)
    x_wide = layer_input.astype(f32)
    moe_sum = dot(scale_high, came_back, NN) + dot(scale_low, came_back, NN)
    block_out = (residual + moe_sum).astype(bf16)

    qkv_groups = qkv_groups.transpose(1, 0, 2)
    attn_gain_grad = jnp.sum(grouped.astype(f32) * qkv_groups, axis=(1, 2)) / attn_gain.astype(f32)
    qkv_weight_grad = ungroup_columns(qkv_groups)

    token_grad = token_grad.transpose(1, 0, 2).reshape(TOK_DEV, 2 * WIDTH)
    normed_grad = dot(token_grad, qkv_all.reshape(WIDTH, 2 * WIDTH), NT)
    inverse_one = lax.rsqrt(jnp.mean(x_wide * x_wide, axis=1, keepdims=True) + epsilon)
    scaled = normed_grad * gain_attn
    attn_part = inverse_one * scaled - x_wide * inverse_one**3 * jnp.mean(
        x_wide * scaled, axis=1, keepdims=True
    )
    input_grad = (residual_grad + attn_part).astype(bf16)
    return (
        block_out,
        input_grad,
        attn_gain_grad,
        moe_gain_grad[:, 0],
        qkv_weight_grad,
        out_weight_grad,
        expert_sums[:, :128, :FF],
        expert_sums[:, :128, FF:],
        expert_sums[:, 128:],
    )


def solution(mesh):
    token = P(("seq", "shard"), None)
    vector = P(("seq", "shard"))
    expert = P("shard", "seq", None)
    return jax.shard_map(
        on_device,
        mesh=mesh,
        in_specs=(
            token,
            vector,
            vector,
            token,
            token,
            expert,
            expert,
            expert,
            token,
            token,
            token,
        ),
        out_specs=(token, token, vector, vector, token, token, expert, expert, expert),
        check_vma=False,
    )
```
